32 devices in a mesh: replica: 2 (over x), shard: 16 (over z, y, core).
Axes of the slice: x: 2, y: 2, z: 4, core: 2. Of those that a mesh axis runs over, the one named last changes fastest.
Arguments:
- tokens: bfloat16 [4096, 2048], P(('replica', 'shard')), may hold values from -6 to 6
- segments: int32 [32, 128], P(('replica', 'shard')), may hold values from 0 to 7, never falling along the last dimension, each value on 1 to 64 neighbouring positions
- ln_gain: bfloat16 [2048], P('shard'), may hold values from 0.5 to 1.5
- ln_bias: bfloat16 [2048], P('shard'), may hold values from -3 to 3
- w_qkv: bfloat16 [2048, 6144], P('shard'), may hold values from -0.125 to 0.125
- b_qkv: bfloat16 [6144], P('shard'), may hold values from -3 to 3
- w_out: bfloat16 [2048, 2048], P('shard'), may hold values from -0.5 to 0.5
- w_gateup: bfloat16 [2048, 11264], P('shard'), may hold values from -0.125 to 0.125
- w_down: bfloat16 [5632, 2048], P('shard'), may hold values from -0.078125 to 0.078125
- cotangent: bfloat16 [4096, 2048], P(('replica', 'shard')), may hold values from -6 to 6
Outputs:
- block_output: bfloat16 [4096, 2048], P(('replica', 'shard'))
- tokens_grad: bfloat16 [4096, 2048], P(('replica', 'shard'))
- gain_grad: float32 [2048], P('shard')
- bias_grad: float32 [2048], P('shard')
- qkv_grad: float32 [2048, 6144], P('shard')
- qkv_bias_grad: float32 [6144], P('shard')
- out_grad: float32 [2048, 2048], P('shard')
- gateup_grad: float32 [2048, 11264], P('shard')
- down_grad: float32 [5632, 2048], P('shard')
The draws below stay inside these ranges and needn't reach their ends.
Inputs may be any that keep to these rules, and one draw needn't show every extreme that they name: `segments`: within each sequence of 128 tokens the numbers start at 0 and never fall; each of the 8 documents holds 1 to 64 tokens, and one holds exactly 64.
All inputs are finite; a program needn't handle non-finite values.
Results may differ from the reference program's by a relative error of at most 0.0085.
Values may be sent and summed in bfloat16 or wider, within the bound.
No kernel may reach another device: no remote copies, remote signals or barrier semaphores. Data moves between devices by JAX's collectives and lax.ppermute only.
A program may use at most 512 MiB of HBM per device.

```python
import math
import jax
import jax.numpy as jnp
import numpy as np
from jax import lax

D = 2048
HEADS = 32
HEAD_DIM = 64
ROT = 16
FF = 5632
TOK_DEV = 128
DOCS = 8
SEQS = 32
TOKENS = 4096


def level_of(own_key, shape, split, least, largest):
    factor_of, own = 1.0, jax.random.fold_in(own_key, 6)
    for axis_at, shards_of in split:
        draws = jnp.exp(jax.random.uniform(jax.random.fold_in(own, axis_at), (shards_of,), jnp.float32, least / len(split), largest / len(split)))
        factor_of = factor_of * jnp.repeat(draws, shape[axis_at] // shards_of).reshape([-1 if axis == axis_at else 1 for axis in range(len(shape))])
    return factor_of


def split_up(number_of, total, most, skew):
    loads = [(1 << 20) // math.isqrt(grade ** skew) + 1 for grade in range(2, number_of + 1)]
    spare, holding = total - most - (number_of - 1), [1] * (number_of - 1)
    while spare > 0:
        candidates = [i for i in range(number_of - 1) if holding[i] < most]
        mass, budget = sum([loads[i] for i in candidates]), spare
        for i in candidates:
            more = min(most - holding[i], max(1, budget * loads[i] // mass), spare)
            holding[i] = holding[i] + more
            spare = spare - more
    return np.array([most] + holding)


def uneven(rng, count, total, reach, lean):
    if count == 2:
        one = jax.random.randint(rng, (), max(1, total - reach), min(reach, total - 1) + 1)
        return jnp.stack([one, total - one])
    sizes = jnp.asarray(split_up(count, total, reach, lean), jnp.int32)
    couples = (count - 1) // 2
    source_of, taker = sizes[1:1 + 2 * couples:2], sizes[2:2 + 2 * couples:2]
    margin = jnp.minimum(source_of - 1, reach - taker)
    passed = jax.random.randint(jax.random.fold_in(rng, 1), (couples,), 0, 1 << 20) % (margin + 1)
    sizes = sizes.at[1:1 + 2 * couples:2].set(source_of - passed).at[2:2 + 2 * couples:2].set(taker + passed)
    return sizes[jax.random.permutation(jax.random.fold_in(rng, 2), count)]


def gaussian(stream_key, dims, width, bound, pieces=(), kind=jnp.bfloat16):
    entries = width * jax.random.normal(stream_key, dims, jnp.float32)
    if pieces:
        entries = entries * level_of(stream_key, dims, pieces, -0.22, 0.18)
    return jnp.clip(entries, -bound, bound).astype(kind)


def setup_inputs(seed: int = 0) -> dict:
    seeds = jax.random.split(jax.random.key(seed), 11)
    tokens = gaussian(seeds[0], (TOKENS, D), 1.0, 6.0, ((0, 32),))
    segments = jax.vmap(lambda own: jnp.searchsorted(jnp.cumsum(uneven(own, DOCS, TOK_DEV, TOK_DEV // 2, 2)), jnp.arange(TOK_DEV), side="right"))(jax.random.split(seeds[1], SEQS)).reshape((SEQS, TOK_DEV)).astype(jnp.int32)
    ln_gain = jnp.clip(1.0 + 0.1 * jax.random.normal(seeds[2], (D,), jnp.float32), 0.5, 1.5).astype(jnp.bfloat16)
    ln_bias = gaussian(seeds[3], (D,), 0.3, 3.0, ((0, 16),))
    w_qkv = gaussian(seeds[4], (D, 3 * D), D ** -0.5, 0.125, ((0, 16),))
    b_qkv = gaussian(seeds[5], (3 * D,), 0.3, 3.0, ((0, 16),))
    w_out = gaussian(seeds[6], (D, D), (D // 16) ** -0.5, 0.5, ((0, 16),))
    w_gateup = gaussian(seeds[7], (D, 2 * FF), D ** -0.5, 0.125, ((0, 16),))
    w_down = gaussian(seeds[8], (FF, D), FF ** -0.5, 0.078125, ((0, 16),))
    cotangent = gaussian(seeds[9], (TOKENS, D), 1.0, 6.0, ((0, 32),))
    return dict(tokens=tokens, segments=segments, ln_gain=ln_gain, ln_bias=ln_bias, w_qkv=w_qkv, b_qkv=b_qkv, w_out=w_out, w_gateup=w_gateup, w_down=w_down, cotangent=cotangent)


epsilon = 1e-05
rope_base = 10000.0
highest = lax.Precision.HIGHEST

@jax.custom_vjp
def low(v):
    return lax.optimization_barrier(v.astype(jnp.bfloat16)).astype(jnp.float32)

@jax.custom_vjp
def low_back(v):
    return v

def low_keep(v):
    return (low(v), None)

def low_pass(kept, grad):
    return (grad,)

def back_keep(v):
    return (v, None)

def back_low(kept, grad):
    return (low(grad),)
low.defvjp(low_keep, low_pass)
low_back.defvjp(back_keep, back_low)

def rotary_tables(segment_row):
    length = segment_row.shape[0]
    indices = jnp.arange(length, dtype=jnp.int32)
    same_doc = segment_row[:, None] == segment_row[None, :]
    doc_start = lax.optimization_barrier(jnp.min(jnp.where(same_doc, indices[None, :], length), axis=1)).astype(jnp.int32)
    in_doc = (indices - doc_start).astype(jnp.float32)
    half_rot = ROT // 2
    inverse = rope_base ** (-(jnp.arange(half_rot, dtype=jnp.float32) * (2.0 / ROT)))
    angles = in_doc[:, None] * inverse[None, :]
    return (jnp.cos(angles)[:, None, :], jnp.sin(angles)[:, None, :])

def rotate(tensor, cos_table, sin_table):
    half_rot = cos_table.shape[-1]
    leading = tensor[..., :half_rot]
    trailing = tensor[..., half_rot:2 * half_rot]
    return jnp.concatenate([leading * cos_table - trailing * sin_table, trailing * cos_table + leading * sin_table, tensor[..., 2 * half_rot:]], axis=-1)

def sequence_group(params, group_tokens, group_segments):
    gain, bias, w_qkv, b_qkv, w_out, w_gateup, w_down = params
    group_count, length, model_width = group_tokens.shape
    centered = group_tokens - lax.optimization_barrier(jnp.mean(group_tokens, axis=-1, keepdims=True))
    inv_std = lax.rsqrt(lax.optimization_barrier(jnp.mean(centered * centered, axis=-1, keepdims=True)) + epsilon)
    normed = low(centered * inv_std * gain + bias)
    joined = low_back(jnp.einsum('gsd,de->gse', normed, w_qkv, precision=highest) + b_qkv)
    head_shape = (group_count, length, HEADS, HEAD_DIM)
    cos_table, sin_table = jax.vmap(rotary_tables)(group_segments)
    queries = low(rotate(joined[..., :model_width].reshape(head_shape), cos_table, sin_table))
    keys_rot = low(rotate(joined[..., model_width:2 * model_width].reshape(head_shape), cos_table, sin_table))
    values = low(joined[..., 2 * model_width:].reshape(head_shape))
    score_scale = 1.0 / math.sqrt(HEAD_DIM)
    scores = low_back(jnp.einsum('gqhd,gkhd->ghqk', queries, keys_rot, precision=highest) * score_scale)
    indices = jnp.arange(length, dtype=jnp.int32)
    allowed = (group_segments[:, :, None] == group_segments[:, None, :]) & (indices[:, None] >= indices[None, :])[None]
    scores = jnp.where(allowed[:, None], scores, -1e+30)
    row_max = lax.optimization_barrier(jnp.max(scores, axis=-1, keepdims=True))
    exp_scores = jnp.exp(scores - row_max)
    probs = low(exp_scores / lax.optimization_barrier(jnp.sum(exp_scores, axis=-1, keepdims=True)))
    context = jnp.einsum('ghqk,gkhd->gqhd', probs, values, precision=highest).reshape(group_count, length, model_width)
    context = low(low_back(context))
    attn_branch = jnp.einsum('gsd,de->gse', context, w_out, precision=highest)
    gateup = low_back(jnp.einsum('gsd,df->gsf', normed, w_gateup, precision=highest))
    gate_part = gateup[..., :FF]
    hidden = low(gate_part * jax.nn.sigmoid(gate_part) * gateup[..., FF:])
    ffn_branch = jnp.einsum('gsf,fd->gsd', hidden, w_down, precision=highest)
    return group_tokens + attn_branch + ffn_branch

def reference(tokens, segments, ln_gain, ln_bias, w_qkv, b_qkv, w_out, w_gateup, w_down, cotangent):
    per_group = math.gcd(SEQS, max(1, 4096 // TOK_DEV))
    groups = SEQS // per_group
    params = (ln_gain.astype(jnp.float32), ln_bias.astype(jnp.float32), w_qkv.astype(jnp.float32), b_qkv.astype(jnp.float32), w_out.astype(jnp.float32), w_gateup.astype(jnp.float32), w_down.astype(jnp.float32))
    stacked = tokens.astype(jnp.float32).reshape(groups, per_group, TOK_DEV, D)
    seg_groups = segments.reshape(groups, per_group, TOK_DEV)
    step_function = jax.checkpoint(sequence_group)

    def forward(inputs, weights):

        def apply_group(bundle):
            return step_function(weights, bundle[0], bundle[1])
        return lax.map(apply_group, (inputs, seg_groups))
    outputs, pullback = jax.vjp(forward, stacked, params)
    grad_tokens, grad_params = pullback(cotangent.astype(jnp.float32).reshape(stacked.shape))
    return (outputs.reshape(TOKENS, D).astype(jnp.bfloat16), grad_tokens.reshape(TOKENS, D).astype(jnp.bfloat16), grad_params[0], grad_params[1], grad_params[2], grad_params[3], grad_params[4], grad_params[5], grad_params[6])
```

```python
import functools
import math

import jax
import jax.numpy as jnp
from jax import lax
from jax.experimental import pallas as pl
from jax.experimental.pallas import tpu as pltpu
from jax.sharding import Mesh, PartitionSpec as P

HEADS = 32
HEAD_DIM = 64
ROT = 16
PAIR = 2 * HEAD_DIM
LANES = 128

epsilon = 1e-05
rope_base = 10000.0
score_scale = 1.0 / math.sqrt(HEAD_DIM)

bf16 = jnp.bfloat16
f32 = jnp.float32


def up_to(size, step):
    return -(-size // step) * step


def mm(a, b, dims):
    return lax.dot_general(a, b, (dims, ((), ())), preferred_element_type=f32)


def rotary_tables(segments):
    count, length = segments.shape
    indices = jnp.arange(length, dtype=jnp.int32)
    same_doc = segments[:, :, None] == segments[:, None, :]
    doc_start = jnp.min(jnp.where(same_doc, indices[None, None, :], length), axis=2)
    in_doc = (indices[None, :] - doc_start).astype(f32).reshape(count * length, 1)
    allowed = same_doc & (indices[:, None] >= indices[None, :])[None]
    half_rot = ROT // 2
    lane = jnp.arange(PAIR, dtype=jnp.int32) % HEAD_DIM
    inverse = rope_base ** (-((lane % half_rot).astype(f32) * (2.0 / ROT)))
    angles = in_doc * inverse[None, :]
    cos, sin = jnp.cos(angles), jnp.sin(angles)
    turned = (lane < ROT)[None, :]
    low = (lane < half_rot)[None, :]
    own = jnp.where(turned, cos, 1.0)
    after = jnp.where(low, -sin, 0.0)
    before = jnp.where(turned & ~low, sin, 0.0)
    return own, after, before, jnp.where(allowed, 0.0, -1e30).astype(f32)


def turn(x, own, after, before):
    half = ROT // 2
    width = x.shape[-1]
    return x * own + pltpu.roll(x, width - half, 1) * after + pltpu.roll(x, half, 1) * before


def head_mask(rows):
    return lax.broadcasted_iota(jnp.int32, (rows, PAIR), 1) < HEAD_DIM


def both_heads(x, first):
    zero = jnp.zeros_like(x)
    return jnp.concatenate([jnp.where(first, x, zero), jnp.where(first, zero, x)], axis=0)


def attend_kernel(joined_ref, bias_ref, own_ref, after_ref, before_ref, mask_ref, fused_ref, context_ref, probs_ref):
    length = joined_ref.shape[0]
    first = head_mask(length)
    own, after, before = own_ref[...], after_ref[...], before_ref[...]
    joined = joined_ref[...] + bias_ref[...]
    q = turn(joined[:, :PAIR], own, after, before).astype(bf16)
    k = turn(joined[:, PAIR : 2 * PAIR], own, after, before).astype(bf16)
    v = joined[:, 2 * PAIR :].astype(bf16)
    mask = mask_ref[0]
    scores = mm(both_heads(q, first), k, ((1,), (1,))) * score_scale
    scores = scores + jnp.concatenate([mask, mask], axis=0)
    top = jnp.max(scores, axis=1, keepdims=True)
    exps = jnp.exp(scores - top)
    probs = exps / jnp.sum(exps, axis=1, keepdims=True)
    low = probs.astype(bf16)
    side = jnp.concatenate([low[:length], low[length:]], axis=1)
    context = mm(side, both_heads(v, first), ((1,), (0,)))
    fused_ref[:, :PAIR] = q
    fused_ref[:, PAIR : 2 * PAIR] = k
    fused_ref[:, 2 * PAIR :] = v
    context_ref[...] = context.astype(bf16)
    probs_ref[0] = probs


def attend_back_kernel(fused_ref, probs_ref, dcontext_ref, own_ref, after_ref, before_ref, dfused_ref, sums_ref):
    length = fused_ref.shape[0]
    first = head_mask(length)
    own, after, before = own_ref[...], after_ref[...], before_ref[...]
    q = fused_ref[:, :PAIR]
    k = fused_ref[:, PAIR : 2 * PAIR]
    v = fused_ref[:, 2 * PAIR :]
    probs = probs_ref[0]
    dc = both_heads(dcontext_ref[...], first)
    dprobs = mm(dc, v, ((1,), (1,)))
    dscores = (probs * (dprobs - jnp.sum(dprobs * probs, axis=1, keepdims=True))).astype(bf16)
    dv = mm(probs.astype(bf16), dc, ((0,), (0,)))
    side = jnp.concatenate([dscores[:length], dscores[length:]], axis=1)
    dq = mm(side, both_heads(k, first), ((1,), (0,))) * score_scale
    dk = mm(dscores, both_heads(q, first), ((0,), (0,))) * score_scale
    out = jnp.concatenate(
        [turn(dq, own, -after, -before).astype(bf16), turn(dk, own, -after, -before).astype(bf16), dv.astype(bf16)],
        axis=1,
    )
    dfused_ref[...] = out

    @pl.when(pl.program_id(0) == 0)
    def _():
        sums_ref[...] = jnp.zeros_like(sums_ref)

    sums_ref[...] += jnp.sum(out.astype(f32), axis=0, keepdims=True)


def attend(joined, bias, tables, count):
    own, after, before, mask = tables
    tokens, width = joined.shape
    length = tokens // count
    row = lambda w: pl.BlockSpec((length, w), lambda i: (i, 0))
    return pl.pallas_call(
        attend_kernel,
        grid=(count,),
        in_specs=[
            row(width),
            pl.BlockSpec((1, width), lambda i: (0, 0)),
            row(PAIR),
            row(PAIR),
            row(PAIR),
            pl.BlockSpec((1, length, length), lambda i: (i, 0, 0)),
        ],
        out_specs=[row(width), row(PAIR), pl.BlockSpec((1, 2 * length, length), lambda i: (i, 0, 0))],
        out_shape=[
            jax.ShapeDtypeStruct((tokens, width), bf16),
            jax.ShapeDtypeStruct((tokens, PAIR), bf16),
            jax.ShapeDtypeStruct((count, 2 * length, length), f32),
        ],
        compiler_params=pltpu.CompilerParams(vmem_limit_bytes=32 << 20),
        cost_estimate=pl.CostEstimate(flops=tokens * length * PAIR * 8, bytes_accessed=tokens * 6000, transcendentals=tokens * length * 2),
    )(joined, bias, own, after, before, mask)


def attend_back(fused, probs, dcontext, tables, count):
    own, after, before, _ = tables
    tokens, width = fused.shape
    length = tokens // count
    row = lambda w: pl.BlockSpec((length, w), lambda i: (i, 0))
    return pl.pallas_call(
        attend_back_kernel,
        grid=(count,),
        in_specs=[
            row(width),
            pl.BlockSpec((1, 2 * length, length), lambda i: (i, 0, 0)),
            row(PAIR),
            row(PAIR),
            row(PAIR),
            row(PAIR),
        ],
        out_specs=[row(width), pl.BlockSpec((1, width), lambda i: (0, 0))],
        out_shape=[jax.ShapeDtypeStruct((tokens, width), bf16), jax.ShapeDtypeStruct((1, width), f32)],
        compiler_params=pltpu.CompilerParams(vmem_limit_bytes=32 << 20),
        cost_estimate=pl.CostEstimate(flops=tokens * length * PAIR * 16, bytes_accessed=tokens * 6000, transcendentals=0),
    )(fused, probs, dcontext, own, after, before)


def per_device(
    groups, tp, outer, tokens, segments, ln_gain, ln_bias, w_qkv, b_qkv, w_out, w_gateup, w_down, cotangent
):
    length, width = tokens.shape
    shards = tp * outer
    rows = w_qkv.shape[0]
    ffn = w_gateup.shape[1] // 2
    own_ffn = ffn // tp
    wide = up_to(own_ffn, LANES)
    own_qkv = 3 * PAIR

    small = jnp.concatenate([ln_gain, ln_bias, b_qkv, segments[0].astype(bf16)])
    small_rows = up_to(-(-small.shape[0] // width), 16)
    small_rows_of = jnp.pad(small, (0, small_rows * width - small.shape[0])).reshape(small_rows, width)
    packed = jnp.concatenate([tokens, small_rows_of], axis=0)
    gathered = lax.all_gather(packed, "tp", axis=0, tiled=False)
    vectors = gathered[:, length:, :].reshape(tp, -1)[:, : small.shape[0]]
    seg_all = vectors[:, small.shape[0] - length :].astype(jnp.int32)
    vectors = vectors[:, : small.shape[0] - length]
    if outer > 1:
        vectors = lax.all_gather(vectors, "outer", axis=1, tiled=False)
    vectors = vectors.reshape(shards, -1)
    gain_all = vectors[:, :rows].reshape(width).astype(f32)
    bias_all = vectors[:, rows : 2 * rows].reshape(width).astype(f32)
    qkv_bias = vectors[:, 2 * rows :].reshape(3, tp, PAIR).astype(f32)
    me = lax.axis_index("tp")
    my_bias = lax.dynamic_index_in_dim(qkv_bias, me, 1, keepdims=False).reshape(1, own_qkv)
    tokens_all = gathered[:, :length, :].reshape(tp * length, width)
    cotangent_all = lax.all_gather(cotangent, "tp", axis=0, tiled=True)

    qkv_cols = w_qkv.reshape(rows, 3, tp, PAIR).transpose(2, 0, 1, 3).reshape(tp, rows, own_qkv)
    ffn_cols = jnp.pad(
        w_gateup.reshape(rows, 2, tp, own_ffn).transpose(2, 0, 1, 3), ((0, 0), (0, 0), (0, 0), (0, wide - own_ffn))
    ).reshape(tp, rows, 2 * wide)
    columns = lax.all_to_all(jnp.concatenate([qkv_cols, ffn_cols], axis=2), "tp", 0, 0, tiled=True)
    if outer > 1:
        columns = lax.all_gather(columns, "outer", axis=1, tiled=False)
        w_out = lax.all_gather(w_out, "outer", axis=0, tiled=True)
        w_down = lax.all_gather(w_down, "outer", axis=0, tiled=True)
    columns = columns.reshape(width, own_qkv + 2 * wide)
    w_rows = jnp.concatenate([w_out, w_down, jnp.zeros((wide - own_ffn, width), bf16)], axis=0)

    tokens32 = tokens_all.astype(f32)
    centered = tokens32 - jnp.mean(tokens32, axis=1, keepdims=True)
    inv_std = lax.rsqrt(jnp.mean(centered * centered, axis=1, keepdims=True) + epsilon)
    normal_part = centered * inv_std
    normed = (normal_part * gain_all + bias_all).astype(bf16)
    tables = rotary_tables(seg_all)
    joined = mm(normed, columns[:, :own_qkv], ((1,), (0,)))
    fused, context, probs = attend(joined, my_bias, tables, tp)
    gateup = mm(normed, columns[:, own_qkv:], ((1,), (0,)))
    gate, up = gateup[:, :wide], gateup[:, wide:]
    s = jax.nn.sigmoid(gate)
    hidden = (gate * s * up).astype(bf16)
    inner = jnp.concatenate([context, hidden], axis=1)
    branch = mm(inner, w_rows, ((1,), (0,))).astype(bf16)
    branch = lax.psum_scatter(branch, "tp", scatter_dimension=0, tiled=True)
    block_output = (tokens.astype(f32) + branch.astype(f32)).astype(bf16)

    dinner = mm(cotangent_all, w_rows, ((1,), (1,)))
    dcontext = dinner[:, :PAIR].astype(bf16)
    dhidden = dinner[:, PAIR:]
    dgate = (dhidden * up * s * (1.0 + gate * (1.0 - s))).astype(bf16)
    dup = (dhidden * gate * s).astype(bf16)
    dfused, bias_sums = attend_back(fused, probs, dcontext, tables, tp)
    dcolumns = jnp.concatenate([dfused, dgate, dup], axis=1)
    dnormed = mm(dcolumns, columns, ((1,), (1,)))
    rows_grad = mm(inner, cotangent_all, ((0,), (0,)))[: PAIR + own_ffn]
    columns_grad = mm(normed, dcolumns, ((0,), (0,)))
    gain_sum = jnp.sum(dnormed * normal_part, axis=0)
    bias_sum = jnp.sum(dnormed, axis=0)
    dnormed_own = lax.psum_scatter(dnormed.astype(bf16), "tp", scatter_dimension=0, tiled=True).astype(f32)
    t32 = tokens.astype(f32)
    c = t32 - jnp.mean(t32, axis=1, keepdims=True)
    inv = lax.rsqrt(jnp.mean(c * c, axis=1, keepdims=True) + epsilon)
    xhat = c * inv
    e = dnormed_own * gain_all
    tokens_back = inv * (e - jnp.mean(e, axis=1, keepdims=True) - xhat * jnp.mean(e * xhat, axis=1, keepdims=True))
    tokens_grad = (cotangent.astype(f32) + tokens_back).astype(bf16)

    extra = jnp.concatenate(
        [gain_sum[:, None], bias_sum[:, None], jnp.zeros((width, LANES - 2), f32)], axis=1
    )
    grads = jnp.concatenate([columns_grad, extra], axis=1)
    if outer > 1:
        grads = grads.reshape(tp, outer, rows, -1)
        grads = lax.psum_scatter(grads, "outer", scatter_dimension=1, tiled=True)
        rows_out = lax.psum_scatter(rows_grad[:PAIR], "outer", scatter_dimension=0, tiled=True)
        rows_down = lax.psum_scatter(rows_grad[PAIR:], "outer", scatter_dimension=0, tiled=True)
        bias_sums = lax.psum(bias_sums, "outer")
    else:
        rows_out, rows_down = rows_grad[:PAIR], rows_grad[PAIR:]
    grads = grads.reshape(tp, rows, -1).astype(bf16)
    grads = lax.all_to_all(grads, "tp", 0, 0, tiled=True)
    rows_out = lax.psum(rows_out.astype(bf16), "replica").astype(f32)
    rows_down = lax.psum(rows_down.astype(bf16), "replica").astype(f32)
    grads = lax.psum(grads, "replica").astype(f32)
    qkv_grad = grads[:, :, :own_qkv].reshape(tp, rows, 3, PAIR).transpose(1, 2, 0, 3).reshape(rows, -1)
    gateup_grad = (
        grads[:, :, own_qkv : own_qkv + 2 * wide]
        .reshape(tp, rows, 2, wide)[..., :own_ffn]
        .transpose(1, 2, 0, 3)
        .reshape(rows, -1)
    )
    own_sums = jnp.sum(grads[:, :, own_qkv + 2 * wide :], axis=0)
    bias_all_sums = lax.all_gather(bias_sums.reshape(3, PAIR), "tp", axis=1, tiled=False)
    bias_all_sums = lax.psum(bias_all_sums, "replica").reshape(-1)
    place = me * outer + lax.axis_index("outer")
    qkv_bias_grad = lax.dynamic_slice_in_dim(bias_all_sums, place * (3 * rows), 3 * rows, 0)
    return (
        block_output,
        tokens_grad,
        own_sums[:, 0],
        own_sums[:, 1],
        qkv_grad,
        qkv_bias_grad,
        rows_out,
        gateup_grad,
        rows_down,
    )


def solution(mesh):
    groups, shards = mesh.shape["replica"], mesh.shape["shard"]
    tp = math.gcd(shards, HEADS // 2)
    outer = shards // tp
    inner_mesh = Mesh(mesh.devices.reshape(groups, tp, outer), ("replica", "tp", "outer"))
    everywhere = P(("replica", "tp", "outer"), None)
    vector = P(("tp", "outer"))
    matrix = P(("tp", "outer"), None)
    return jax.shard_map(
        functools.partial(per_device, groups, tp, outer),
        mesh=inner_mesh,
        in_specs=(everywhere, everywhere, vector, vector, matrix, vector, matrix, matrix, matrix, everywhere),
        out_specs=(everywhere, everywhere, vector, vector, matrix, vector, matrix, matrix, matrix),
        check_vma=False,
    )
```

```python
import functools
import math

import jax
import jax.numpy as jnp
from jax import lax
from jax.experimental import pallas as pl
from jax.experimental.pallas import tpu as pltpu
from jax.sharding import Mesh, PartitionSpec as P

HEADS = 32
HEAD_DIM = 64
ROT = 16
PAIR = 2 * HEAD_DIM
TP = ("z", "y", "c")
LANES = 128
SEQUENCES = 8
CHUNK = 512

epsilon = 1e-05
rope_base = 10000.0
score_scale = 1.0 / math.sqrt(HEAD_DIM)

bf16 = jnp.bfloat16
f32 = jnp.float32


def up_to(size, step):
    return -(-size // step) * step


def mm(a, b, dims):
    return lax.dot_general(a, b, (dims, ((), ())), preferred_element_type=f32)


def rotary_tables(segments):
    count, length = segments.shape
    indices = jnp.arange(length, dtype=jnp.int32)
    same_doc = segments[:, :, None] == segments[:, None, :]
    doc_start = jnp.min(jnp.where(same_doc, indices[None, None, :], length), axis=2)
    in_doc = (indices[None, :] - doc_start).astype(f32).reshape(count * length, 1)
    allowed = same_doc & (indices[:, None] >= indices[None, :])[None]
    half_rot = ROT // 2
    lane = jnp.arange(PAIR, dtype=jnp.int32) % HEAD_DIM
    inverse = rope_base ** (-((lane % half_rot).astype(f32) * (2.0 / ROT)))
    angles = in_doc * inverse[None, :]
    cos, sin = jnp.cos(angles), jnp.sin(angles)
    turned = (lane < ROT)[None, :]
    low = (lane < half_rot)[None, :]
    own = jnp.where(turned, cos, 1.0)
    after = jnp.where(low, -sin, 0.0)
    before = jnp.where(turned & ~low, sin, 0.0)
    return own, after, before, jnp.where(allowed, 0.0, -1e30).astype(f32)


def turn(x, own, after, before):
    half = ROT // 2
    width = x.shape[-1]
    return x * own + pltpu.roll(x, width - half, 1) * after + pltpu.roll(x, half, 1) * before


def head_mask(rows):
    return lax.broadcasted_iota(jnp.int32, (rows, PAIR), 1) < HEAD_DIM


def both_heads(x, first):
    zero = jnp.zeros_like(x)
    return jnp.concatenate([jnp.where(first, x, zero), jnp.where(first, zero, x)], axis=0)


def attend_kernel(joined_ref, bias_ref, own_ref, after_ref, before_ref, mask_ref, fused_ref, context_ref, probs_ref):
    length = mask_ref.shape[1]
    first = head_mask(length)
    for n in range(mask_ref.shape[0]):
        rows = pl.ds(n * length, length)
        own, after, before = own_ref[rows, :], after_ref[rows, :], before_ref[rows, :]
        joined = joined_ref[rows, :] + bias_ref[...]
        q = turn(joined[:, :PAIR], own, after, before).astype(bf16)
        k = turn(joined[:, PAIR : 2 * PAIR], own, after, before).astype(bf16)
        v = joined[:, 2 * PAIR :].astype(bf16)
        mask = mask_ref[n]
        scores = mm(both_heads(q, first), k, ((1,), (1,))) * score_scale
        scores = scores + jnp.concatenate([mask, mask], axis=0)
        top = jnp.max(scores, axis=1, keepdims=True)
        exps = jnp.exp(scores - top)
        probs = exps / jnp.sum(exps, axis=1, keepdims=True)
        low = probs.astype(bf16)
        side = jnp.concatenate([low[:length], low[length:]], axis=1)
        context = mm(side, both_heads(v, first), ((1,), (0,)))
        fused_ref[rows, :PAIR] = q
        fused_ref[rows, PAIR : 2 * PAIR] = k
        fused_ref[rows, 2 * PAIR :] = v
        context_ref[rows, :] = context.astype(bf16)
        probs_ref[n] = probs


def attend_back_kernel(fused_ref, probs_ref, dcontext_ref, own_ref, after_ref, before_ref, dfused_ref, sums_ref):
    length = probs_ref.shape[2]
    first = head_mask(length)
    total = jnp.zeros(sums_ref.shape, f32)
    for n in range(probs_ref.shape[0]):
        rows = pl.ds(n * length, length)
        own, after, before = own_ref[rows, :], after_ref[rows, :], before_ref[rows, :]
        q = fused_ref[rows, :PAIR]
        k = fused_ref[rows, PAIR : 2 * PAIR]
        v = fused_ref[rows, 2 * PAIR :]
        probs = probs_ref[n]
        dc = both_heads(dcontext_ref[rows, :], first)
        dprobs = mm(dc, v, ((1,), (1,)))
        dscores = (probs * (dprobs - jnp.sum(dprobs * probs, axis=1, keepdims=True))).astype(bf16)
        dv = mm(probs.astype(bf16), dc, ((0,), (0,)))
        side = jnp.concatenate([dscores[:length], dscores[length:]], axis=1)
        dq = mm(side, both_heads(k, first), ((1,), (0,))) * score_scale
        dk = mm(dscores, both_heads(q, first), ((0,), (0,))) * score_scale
        out = jnp.concatenate(
            [turn(dq, own, -after, -before).astype(bf16), turn(dk, own, -after, -before).astype(bf16), dv.astype(bf16)],
            axis=1,
        )
        dfused_ref[rows, :] = out
        total = total + jnp.sum(out.astype(f32), axis=0, keepdims=True)

    @pl.when(pl.program_id(0) == 0)
    def _():
        sums_ref[...] = jnp.zeros_like(sums_ref)

    sums_ref[...] += total


def attend(joined, bias, tables, count):
    own, after, before, mask = tables
    tokens, width = joined.shape
    length = tokens // count
    many = math.gcd(count, SEQUENCES)
    row = lambda w: pl.BlockSpec((many * length, w), lambda i: (i, 0))
    return pl.pallas_call(
        attend_kernel,
        name="attend",
        grid=(count // many,),
        in_specs=[
            row(width),
            pl.BlockSpec((1, width), lambda i: (0, 0)),
            row(PAIR),
            row(PAIR),
            row(PAIR),
            pl.BlockSpec((many, length, length), lambda i: (i, 0, 0)),
        ],
        out_specs=[row(width), row(PAIR), pl.BlockSpec((many, 2 * length, length), lambda i: (i, 0, 0))],
        out_shape=[
            jax.ShapeDtypeStruct((tokens, width), bf16),
            jax.ShapeDtypeStruct((tokens, PAIR), bf16),
            jax.ShapeDtypeStruct((count, 2 * length, length), f32),
        ],
        compiler_params=pltpu.CompilerParams(vmem_limit_bytes=32 << 20),
        cost_estimate=pl.CostEstimate(flops=tokens * length * PAIR * 8, bytes_accessed=tokens * 6000, transcendentals=tokens * length * 2),
    )(joined, bias, own, after, before, mask)


def attend_back(fused, probs, dcontext, tables, count, *others):
    own, after, before, _ = tables
    tokens, width = fused.shape
    length = tokens // count
    many = math.gcd(count, SEQUENCES)
    row = lambda w: pl.BlockSpec((many * length, w), lambda i: (i, 0))
    return pl.pallas_call(
        ignoring(attend_back_kernel, 6, len(others)),
        name="attend_back",
        grid=(count // many,),
        in_specs=[
            row(width),
            pl.BlockSpec((many, 2 * length, length), lambda i: (i, 0, 0)),
            row(PAIR),
            row(PAIR),
            row(PAIR),
            row(PAIR),
            *anywhere(others),
        ],
        out_specs=[row(width), pl.BlockSpec((1, width), lambda i: (0, 0))],
        out_shape=[jax.ShapeDtypeStruct((tokens, width), bf16), jax.ShapeDtypeStruct((1, width), f32)],
        compiler_params=pltpu.CompilerParams(vmem_limit_bytes=32 << 20),
        cost_estimate=pl.CostEstimate(flops=tokens * length * PAIR * 16, bytes_accessed=tokens * 6000, transcendentals=0),
    )(fused, probs, dcontext, own, after, before, *others)


def shifted(x, axis, size, step):
    return lax.ppermute(x, axis, [(i, (i + step) % size) for i in range(size)])


def limits(mib):
    return pltpu.CompilerParams(vmem_limit_bytes=mib << 20)


def cost(flops, moved):
    return pl.CostEstimate(flops=1, bytes_accessed=1, transcendentals=0)


def whole_block(array):
    return pl.BlockSpec(array.shape, lambda *_: (0,) * array.ndim)


def pack_kernel(part_ref, own_ref, out_ref, *, sections, tp, size, wide):
    own = own_ref[...]
    rows = own.shape[0]
    for t in range(tp):
        pieces = []
        for section in range(sections):
            at = (section * tp + t) * size
            pieces.append(own[:, at : at + size])
            if wide > size:
                pieces.append(jnp.zeros((rows, wide - size), own.dtype))
        out_ref[t] = jnp.concatenate(pieces, axis=1) if len(pieces) > 1 else pieces[0]


def pack(weight, part, groups, sections, tp, size, wide):
    rows, width = weight.shape
    half = rows // groups
    step = min(half, 16)
    return pl.pallas_call(
        functools.partial(pack_kernel, sections=sections, tp=tp, size=size, wide=wide),
        name="pack",
        grid_spec=pltpu.PrefetchScalarGridSpec(
            num_scalar_prefetch=1,
            grid=(half // step,),
            in_specs=[pl.BlockSpec((step, width), lambda i, part: (part[0] * (half // step) + i, 0))],
            out_specs=pl.BlockSpec((tp, step, sections * wide), lambda i, part: (0, i, 0)),
        ),
        out_shape=jax.ShapeDtypeStruct((tp, half, sections * wide), weight.dtype),
        compiler_params=limits(32),
        cost_estimate=cost(0, 4 * half * width),
    )(part, weight)


def nothing(*refs):
    del refs


def anywhere(arrays):
    return [pl.BlockSpec(memory_space=pl.ANY) for _ in arrays]


def after(x, *others):
    return pl.pallas_call(
        nothing,
        name="after",
        in_specs=anywhere((x, *others)),
        out_specs=pl.BlockSpec(memory_space=pl.ANY),
        out_shape=jax.ShapeDtypeStruct(x.shape, x.dtype),
        input_output_aliases={0: 0},
    )(x, *others)


def ignoring(kernel, at, count):
    return lambda *refs: kernel(*refs[:at], *refs[at + count :])


def in_three(x):
    parts = []
    for _ in range(3):
        low = lax.reduce_precision(x, 8, 7)
        parts.append(low.astype(bf16))
        x = x - low
    return parts


def as_column(row):
    n = row.shape[1]
    square = lax.broadcasted_iota(jnp.int32, (n, n), 0) == lax.broadcasted_iota(jnp.int32, (n, n), 1)
    return jnp.sum(jnp.where(square, row, 0.0), axis=1, keepdims=True)


def normal_of(a_ref, b_ref, stats_ref):
    parts = []
    for k, ref in enumerate((a_ref, b_ref)):
        mean, inv_std = as_column(stats_ref[k, 0:1, :]), as_column(stats_ref[k, 1:2, :])
        parts.append((ref[0].astype(f32) - mean) * inv_std)
    return jnp.concatenate(parts, axis=0)


def unpack_kernel(part_ref, own_ref, other_ref, out_ref, *, sections, tp, size, wide):
    got = jnp.where(pl.program_id(0) == 0, own_ref[...], other_ref[...])
    for section in range(sections):
        pieces = [got[t, :, section * wide : section * wide + size] for t in range(tp)]
        out_ref[:, section * tp * size : (section + 1) * tp * size] = jnp.concatenate(pieces, axis=1).astype(f32)


def unpack(own, other, part, sections, size, wide):
    tp, half, width = own.shape
    step = min(half, 16)
    count = half // step
    return pl.pallas_call(
        functools.partial(unpack_kernel, sections=sections, tp=tp, size=size, wide=wide),
        name="unpack",
        grid_spec=pltpu.PrefetchScalarGridSpec(
            num_scalar_prefetch=1,
            grid=(2, count),
            in_specs=[
                pl.BlockSpec((tp, step, width), lambda i, j, part: (0, jnp.where(i == 0, j, count - 1), 0)),
                pl.BlockSpec((tp, step, width), lambda i, j, part: (0, jnp.where(i == 0, 0, j), 0)),
            ],
            out_specs=pl.BlockSpec(
                (step, sections * tp * size), lambda i, j, part: (lax.rem(part[0] + i, 2) * count + j, 0)
            ),
        ),
        out_shape=jax.ShapeDtypeStruct((2 * half, sections * tp * size), f32),
        compiler_params=limits(48),
        cost_estimate=cost(0, 12 * half * width * tp),
    )(part, own, other)


def gate_kernel(
    a_ref, b_ref, stats_ref, gain_ref, bias_ref, gu_ref, qkv_ref, normed_ref, gate_ref, up_ref, hidden_ref, joined_ref
):
    normed = (normal_of(a_ref, b_ref, stats_ref) * gain_ref[...] + bias_ref[...]).astype(bf16)
    normed_ref[...] = normed
    wide = gate_ref.shape[1]
    gateup = mm(normed, gu_ref[...], ((1,), (0,)))
    gate, up = gateup[:, :wide], gateup[:, wide:]
    gate_ref[...] = gate
    up_ref[...] = up
    hidden_ref[...] = (gate * jax.nn.sigmoid(gate) * up).astype(bf16)
    joined_ref[...] = mm(normed, qkv_ref[...], ((1,), (0,)))


def gate_forward(gathered, stats, gain, bias, gu, qkv):
    count, padded, width = gathered.shape
    length, wide = LANES, gu.shape[1] // 2
    tokens = count * length
    block = lambda k: pl.BlockSpec((1, length, width), lambda i: (2 * i + k, 0, 0))
    row = lambda w: pl.BlockSpec((2 * length, w), lambda i: (i, 0))
    return pl.pallas_call(
        gate_kernel,
        name="gate_fwd",
        grid=(count // 2,),
        in_specs=[
            block(0),
            block(1),
            pl.BlockSpec((2, 8, length), lambda i: (i, 0, 0)),
            whole_block(gain),
            whole_block(bias),
            whole_block(gu),
            whole_block(qkv),
        ],
        out_specs=[row(width), row(wide), row(wide), row(wide), row(3 * PAIR)],
        out_shape=[
            jax.ShapeDtypeStruct((tokens, width), bf16),
            jax.ShapeDtypeStruct((tokens, wide), f32),
            jax.ShapeDtypeStruct((tokens, wide), f32),
            jax.ShapeDtypeStruct((tokens, wide), bf16),
            jax.ShapeDtypeStruct((tokens, 3 * PAIR), f32),
        ],
        compiler_params=limits(56),
        cost_estimate=cost(2 * tokens * width * (2 * wide + 3 * PAIR), tokens * (4 * width + 10 * wide + 12 * PAIR)),
    )(gathered, gathered, stats, gain, bias, gu, qkv)


def branch_kernel(far, order_ref, ac_ref, bc_ref, ah_ref, bh_ref, w_ref, *refs):
    context = jnp.concatenate([ac_ref[...], bc_ref[...]], axis=0)
    hidden = jnp.concatenate([ah_ref[...], bh_ref[...]], axis=0)
    total = mm(context, w_ref[:PAIR, :], ((1,), (0,))) + mm(hidden, w_ref[PAIR:, :], ((1,), (0,)))
    if far:
        refs[0][...] = total.astype(bf16)
        return
    got_ref, sent_ref, keep_ref = refs
    keep_ref[...] = total + got_ref[...].astype(f32)

    @pl.when(pl.program_id(0) < pl.num_programs(0) // 2)
    def _():
        sent_ref[...] = keep_ref[...].astype(bf16)


def branches(order, context, hidden, w, got=None):
    tokens, wide = hidden.shape
    width = w.shape[1]
    count = order.shape[0]
    step = 2 * LANES
    row = lambda x, k: pl.BlockSpec((LANES, x.shape[1]), lambda i, order: (order[2 * i + k], 0))
    plain = pl.BlockSpec((step, width), lambda i, order: (i, 0))
    if got is None:
        out_specs = [plain]
        out_shape = [jax.ShapeDtypeStruct((count * LANES, width), bf16)]
        more = []
    else:
        sent = count // 4
        out_specs = [
            pl.BlockSpec((step, width), lambda i, order: (jnp.minimum(i, sent - 1), 0)),
            pl.BlockSpec((step, width), lambda i, order: (jnp.maximum(i - sent, 0), 0)),
        ]
        out_shape = [jax.ShapeDtypeStruct((count * LANES // 2, width), kind) for kind in (bf16, f32)]
        more = [got]
    return pl.pallas_call(
        functools.partial(branch_kernel, got is None),
        name="branch_far" if got is None else "branch_near",
        grid_spec=pltpu.PrefetchScalarGridSpec(
            num_scalar_prefetch=1,
            grid=(count // 2,),
            in_specs=[
                row(context, 0),
                row(context, 1),
                row(hidden, 0),
                row(hidden, 1),
                whole_block(w),
                *[plain for _ in more],
            ],
            out_specs=out_specs,
        ),
        out_shape=out_shape,
        compiler_params=limits(48),
        cost_estimate=cost(2 * tokens * width * (PAIR + wide), 2 * tokens * (width + PAIR + wide)),
    )(order, context, context, hidden, hidden, w, *more)


def gate_back_kernel(cotangent_ref, gate_ref, up_ref, w_ref, dgateup_ref, dcontext_ref):
    dinner = mm(cotangent_ref[...], w_ref[...], ((1,), (1,)))
    dcontext_ref[...] = dinner[:, :PAIR].astype(bf16)
    dhidden = dinner[:, PAIR:]
    gate, up = gate_ref[...], up_ref[...]
    s = jax.nn.sigmoid(gate)
    wide = gate.shape[1]
    dgateup_ref[:, :wide] = (dhidden * up * s * (1.0 + gate * (1.0 - s))).astype(bf16)
    dgateup_ref[:, wide:] = (dhidden * gate * s).astype(bf16)


def gate_backward(cotangent, gate, up, w, *others):
    tokens, wide = gate.shape
    width = w.shape[1]
    row = lambda w: pl.BlockSpec((2 * LANES, w), lambda i: (i, 0))
    return pl.pallas_call(
        ignoring(gate_back_kernel, 4, len(others)),
        name="gate_back",
        grid=(tokens // (2 * LANES),),
        in_specs=[row(width), row(wide), row(wide), whole_block(w), *anywhere(others)],
        out_specs=[row(2 * wide), row(PAIR)],
        out_shape=[jax.ShapeDtypeStruct((tokens, 2 * wide), bf16), jax.ShapeDtypeStruct((tokens, PAIR), bf16)],
        compiler_params=limits(48),
        cost_estimate=cost(2 * tokens * width * (PAIR + wide), tokens * (2 * width + 12 * wide)),
    )(cotangent, gate, up, w, *others)


def grads_kernel(part_ref, normed_ref, d_ref, mine_ref, theirs_ref):
    grads = mm(normed_ref[...], d_ref[...], ((0,), (0,)))
    count, half, _ = mine_ref.shape
    first = part_ref[0] == 0
    for t in range(count):
        low = grads[2 * t * half : (2 * t + 1) * half]
        high = grads[(2 * t + 1) * half : (2 * t + 2) * half]
        mine_ref[t] = jnp.where(first, low, high)
        theirs_ref[t] = jnp.where(first, high, low).astype(bf16)


def split_grads(part, normed, d, half, *others):
    tokens, width = normed.shape
    step = 4 * LANES
    out = d.shape[1]
    blocks = step // (2 * half)
    piece = lambda: pl.BlockSpec((blocks, half, out), lambda i, part: (i, 0, 0))
    return pl.pallas_call(
        ignoring(grads_kernel, 3, len(others)),
        name="grads",
        grid_spec=pltpu.PrefetchScalarGridSpec(
            num_scalar_prefetch=1,
            grid=(width // step,),
            in_specs=[pl.BlockSpec((tokens, step), lambda i, part: (0, i)), whole_block(d)]
            + anywhere(others),
            out_specs=[piece(), piece()],
        ),
        out_shape=[
            jax.ShapeDtypeStruct((width // (2 * half), half, out), f32),
            jax.ShapeDtypeStruct((width // (2 * half), half, out), bf16),
        ],
        compiler_params=limits(56),
        cost_estimate=cost(2 * tokens * width * d.shape[1], 2 * tokens * (width + d.shape[1]) + 3 * width * out),
    )(part, normed, d, *others)


def rows_kernel(context_ref, hidden_ref, cotangent_ref, out_ref):
    cotangent = cotangent_ref[...]
    out_ref[:PAIR, :] = mm(context_ref[...], cotangent, ((0,), (0,))).astype(out_ref.dtype)
    hidden = mm(hidden_ref[...], cotangent, ((0,), (0,)))
    out_ref[PAIR:, :] = hidden[: out_ref.shape[0] - PAIR].astype(out_ref.dtype)


def rows_grads(context, hidden, cotangent, own, kind, *others):
    tokens, width = cotangent.shape
    step = 4 * LANES
    return pl.pallas_call(
        ignoring(rows_kernel, 3, len(others)),
        name="rows",
        grid=(width // step,),
        in_specs=[
            whole_block(context),
            whole_block(hidden),
            pl.BlockSpec((tokens, step), lambda i: (0, i)),
            *anywhere(others),
        ],
        out_specs=pl.BlockSpec((own, step), lambda i: (0, i)),
        out_shape=jax.ShapeDtypeStruct((own, width), kind),
        compiler_params=limits(56),
        cost_estimate=cost(2 * tokens * width * own, tokens * width * 2),
    )(context, hidden, cotangent, *others)


def dnormed_kernel(order_ref, a_ref, b_ref, as_ref, bs_ref, ag_ref, bg_ref, aq_ref, bq_ref, gu_ref, qkv_ref, *refs):
    *far_refs, out_ref, sums_ref = refs if len(refs) == 2 else (*refs[:-2], refs[-1], refs[-2])
    step = pl.program_id(0)
    gateup = jnp.concatenate([ag_ref[...], bg_ref[...]], axis=0)
    fused = jnp.concatenate([aq_ref[...], bq_ref[...]], axis=0)

    @pl.when(step == 0)
    def _():
        sums_ref[...] = jnp.zeros_like(sums_ref)

    means = [as_column(ref[0, 0:1, :]) for ref in (as_ref, bs_ref)]
    stds = [as_column(ref[0, 1:2, :]) for ref in (as_ref, bs_ref)]
    width = gu_ref.shape[0]
    for at in range(0, width, CHUNK):
        cols = pl.ds(at, CHUNK)
        dnormed = mm(gateup, gu_ref[cols, :], ((1,), (1,))) + mm(fused, qkv_ref[cols, :], ((1,), (1,)))
        out_ref[:, cols] = dnormed.astype(out_ref.dtype)
        normal = jnp.concatenate(
            [(ref[0, :, cols].astype(f32) - mean) * std for ref, mean, std in zip((a_ref, b_ref), means, stds)], axis=0
        )
        sums_ref[0:1, cols] += jnp.sum(dnormed * normal, axis=0, keepdims=True)
        sums_ref[1:2, cols] += jnp.sum(dnormed, axis=0, keepdims=True)
    for i, far_ref in enumerate(far_refs):

        @pl.when(step == i)
        def _():
            far_ref[...] = out_ref[...]


def dnormed_share(order, *others, gathered, stats, dgateup, dfused, gu, qkv, far):
    width = gathered.shape[2]
    count = order.shape[0]
    step = 2 * LANES
    block = lambda k: pl.BlockSpec((1, LANES, width), lambda i, order: (order[2 * i + k], 0, 0))
    stat = lambda k: pl.BlockSpec((1, 8, LANES), lambda i, order: (order[2 * i + k], 0, 0))
    row = lambda x, k: pl.BlockSpec((LANES, x.shape[1]), lambda i, order: (order[2 * i + k], 0))
    if far:
        outs = [pl.BlockSpec((step, width), lambda i, order: (0, 0)) for _ in range(count // 2)]
        shapes = [jax.ShapeDtypeStruct((step, width), bf16) for _ in range(count // 2)]
    else:
        outs = [pl.BlockSpec((step, width), lambda i, order: (i, 0))]
        shapes = [jax.ShapeDtypeStruct((count * LANES, width), f32)]
    return pl.pallas_call(
        ignoring(dnormed_kernel, 11, len(others)),
        name="dn_far" if far else "dn_near",
        grid_spec=pltpu.PrefetchScalarGridSpec(
            num_scalar_prefetch=1,
            grid=(count // 2,),
            in_specs=[
                block(0),
                block(1),
                stat(0),
                stat(1),
                row(dgateup, 0),
                row(dgateup, 1),
                row(dfused, 0),
                row(dfused, 1),
                whole_block(gu),
                whole_block(qkv),
                *anywhere(others),
            ],
            out_specs=[*outs, pl.BlockSpec((8, width), lambda i, order: (0, 0))],
            scratch_shapes=[pltpu.VMEM((step, width), bf16)] if far else [],
        ),
        out_shape=[*shapes, jax.ShapeDtypeStruct((8, width), f32)],
        compiler_params=limits(60),
        cost_estimate=cost(
            2 * count * LANES * width * (dgateup.shape[1] + dfused.shape[1]), count * LANES * width * 8
        ),
    )(order, gathered, gathered, stats, stats, dgateup, dgateup, dfused, dfused, gu, qkv, *others)


def combine_kernel(near_ref, *refs):
    got_refs, sent_refs, keep_ref = refs[: len(refs) - 1 - (len(refs) - 1) // 3], refs[-1 - (len(refs) - 1) // 3 : -1], refs[-1]
    for i, got_ref in enumerate(got_refs):

        @pl.when(pl.program_id(0) == i)
        def _():
            total = near_ref[...] + got_ref[...].astype(f32)
            if i < len(sent_refs):
                sent_refs[i][...] = total.astype(bf16)
            else:
                keep_ref[...] = total


def combine(near, got, *others):
    rows, width = near.shape
    step = rows // len(got)
    sent = len(got) // 2
    fixed = pl.BlockSpec((step, width), lambda i: (0, 0))
    return pl.pallas_call(
        ignoring(combine_kernel, 1 + len(got), len(others)),
        name="combine",
        grid=(len(got),),
        in_specs=[pl.BlockSpec((step, width), lambda i: (i, 0)), *[fixed for _ in got], *anywhere(others)],
        out_specs=[fixed for _ in range(sent)] + [pl.BlockSpec((step, width), lambda i: (jnp.maximum(i - sent, 0), 0))],
        out_shape=[jax.ShapeDtypeStruct((step, width), bf16) for _ in range(sent)]
        + [jax.ShapeDtypeStruct((rows // 2, width), f32)],
        compiler_params=limits(48),
        cost_estimate=cost(0, rows * width * 9),
    )(near, *got, *others)


def add_kernel(keep_ref, got_ref, out_ref):
    out_ref[...] = (keep_ref[...] + got_ref[...].astype(f32)).astype(bf16)


def add_up(keep, got, *others):
    rows, width = keep.shape
    row = pl.BlockSpec((LANES, width), lambda i: (i, 0))
    return pl.pallas_call(
        ignoring(add_kernel, 2, len(others)),
        name="add_up",
        grid=(rows // LANES,),
        in_specs=[row, row, *anywhere(others)],
        out_specs=row,
        out_shape=jax.ShapeDtypeStruct((rows, width), bf16),
        compiler_params=limits(16),
        cost_estimate=cost(0, rows * width * 8),
    )(keep, got, *others)


def per_device(
    groups, outer, zs, ys, cs, tokens, segments, ln_gain, ln_bias, w_qkv, b_qkv, w_out, w_gateup, w_down, cotangent
):
    length, width = tokens.shape
    tp = zs * ys * cs
    shards = tp * outer
    z, y, c = (lax.axis_index(axis) for axis in TP)
    me = (z * ys + y) * cs + c

    own_ffn = w_gateup.shape[1] // 2 // tp
    wide = up_to(own_ffn, LANES)
    own_qkv = 3 * PAIR
    rows = w_qkv.shape[0]
    half = rows // groups
    part = lax.axis_index("replica")
    parts = part.astype(jnp.int32).reshape(1)
    steps = sorted(range(zs), key=lambda k: -min(k, zs - k))
    order = [
        jnp.stack(
            [
                (lax.rem(z + zs - k, zs) * ys + lax.rem(y + ys - j, ys)) * cs + lax.rem(c + cs - i, cs)
                for j in reversed(range(ys))
                for k in steps
            ]
        ).astype(jnp.int32)
        for i in range(cs)
    ]

    plain_order = [
        jnp.stack(
            [(k * ys + lax.rem(y + ys - j, ys)) * cs + lax.rem(c + cs - i, cs) for j in reversed(range(ys)) for k in range(zs)]
        ).astype(jnp.int32)
        for i in range(cs)
    ]

    tokens32 = tokens.astype(f32)
    mean = jnp.mean(tokens32, axis=1)
    centered = tokens32 - mean[:, None]
    inv_std = lax.rsqrt(jnp.mean(centered * centered, axis=1) + epsilon)
    small = jnp.concatenate(
        [ln_gain, ln_bias, b_qkv, segments[0].astype(bf16), *in_three(mean), *in_three(inv_std)]
    )
    of_params = 2 * rows + b_qkv.shape[0]
    small_rows = up_to(-(-small.shape[0] // width), 16)
    small_rows_of = jnp.pad(small, (0, small_rows * width - small.shape[0])).reshape(small_rows, width)
    packed = jnp.concatenate([tokens, small_rows_of], axis=0)
    gathered = lax.all_gather(packed, TP, axis=0, tiled=False)

    cotangent_all = lax.all_gather(cotangent, TP, axis=0, tiled=True)

    def other(own):
        return shifted(own, "replica", groups, 1)

    def to_columns(own):
        own = lax.all_to_all(own, TP, 0, 0, tiled=True)
        whole = jnp.zeros((tp, groups, half, own.shape[-1]), bf16)
        whole = lax.dynamic_update_slice(whole, own[:, None], (0, part, 0, 0))
        whole = lax.dynamic_update_slice(whole, other(own)[:, None], (0, 1 - part, 0, 0))
        whole = whole.reshape(tp, rows, own.shape[-1])
        if outer > 1:
            whole = lax.all_gather(whole, "outer", axis=1, tiled=False)
        return whole.reshape(width, own.shape[-1])

    gu_cols = to_columns(pack(w_gateup, parts, groups, 2, tp, own_ffn, wide))
    qkv_cols = to_columns(pack(w_qkv, parts, groups, 3, tp, PAIR, PAIR))
    if outer > 1:
        w_out = lax.all_gather(w_out, "outer", axis=0, tiled=True)
        w_down = lax.all_gather(w_down, "outer", axis=0, tiled=True)
    w_rows = jnp.concatenate([w_out, w_down, jnp.zeros((wide - own_ffn, width), bf16)], axis=0)

    vectors = gathered[:, length:, :].reshape(tp, -1)[:, : small.shape[0]]
    of_tokens = vectors[:, of_params:].reshape(tp, 7, length)
    seg_all = of_tokens[:, 0].astype(jnp.int32)
    of_tokens = of_tokens[:, 1:].astype(f32).reshape(tp, 2, 3, length)
    stats = jnp.pad(of_tokens[:, :, 0] + of_tokens[:, :, 1] + of_tokens[:, :, 2], ((0, 0), (0, 6), (0, 0)))
    vectors = vectors[:, :of_params]
    if outer > 1:
        vectors = lax.all_gather(vectors, "outer", axis=1, tiled=False)
    vectors = vectors.reshape(shards, -1)
    gain_all = vectors[:, :rows].reshape(1, width).astype(f32)
    bias_all = vectors[:, rows : 2 * rows].reshape(1, width).astype(f32)
    qkv_bias = vectors[:, 2 * rows :].reshape(3, tp, PAIR).astype(f32)
    my_bias = lax.dynamic_index_in_dim(qkv_bias, me, 1, keepdims=False).reshape(1, own_qkv)
    tables = rotary_tables(seg_all)

    normed, gate, up, hidden, joined = gate_forward(gathered, stats, gain_all, bias_all, gu_cols, qkv_cols)
    fused, context, probs = attend(joined, my_bias, tables, tp)
    branch_far = branches(plain_order[1], context, hidden, w_rows)[0]
    branch_sent, branch_keep = branches(plain_order[0], context, hidden, w_rows, shifted(branch_far, "c", cs, 1))
    branch_got = shifted(branch_sent, "y", ys, 1)

    dgateup, dcontext = gate_backward(cotangent_all, gate, up, w_rows, branch_sent)

    def grads_of(d, *others):
        if outer == 1:
            return split_grads(parts, normed, d, half, *others)
        mine, theirs = of_replicas(mm(normed, d, ((0,), (0,))))
        return mine, theirs.astype(bf16)

    def of_replicas(grads):
        if outer > 1:
            grads = lax.psum_scatter(grads.reshape(tp, outer, rows, -1), "outer", scatter_dimension=1, tiled=True)
        grads = grads.reshape(tp, groups, half, -1)
        mine = lax.dynamic_index_in_dim(grads, part, 1, keepdims=False)
        return mine, lax.dynamic_index_in_dim(grads, 1 - part, 1, keepdims=False)

    gu_mine, gu_theirs = grads_of(dgateup)
    gu_got = other(gu_theirs)
    dfused, bias_sums = attend_back(fused, probs, dcontext, tables, tp, gu_theirs)
    share = functools.partial(dnormed_share, gathered=gathered, stats=stats, dgateup=dgateup, dfused=dfused, gu=gu_cols, qkv=qkv_cols)
    branch = add_up(branch_keep, branch_got, dfused)
    branch_own = lax.psum_scatter(branch, "z", scatter_dimension=0, tiled=True)
    block_output = (tokens32 + branch_own.astype(f32)).astype(bf16)
    *far_shares, far_sums = share(order[1], branch, far=True)
    got = [shifted(far_share, "c", cs, 1) for far_share in far_shares]
    near_share, near_sums = share(order[0], *far_shares, far=False)
    gain_sum, bias_sum = near_sums[0] + far_sums[0], near_sums[1] + far_sums[1]

    per_row = own_qkv // half
    tiled_sums = jnp.broadcast_to(bias_sums.reshape(1, half, per_row), (width // half, half, per_row)).reshape(width, per_row)
    extra = jnp.concatenate(
        [gain_sum[:, None], bias_sum[:, None], tiled_sums, jnp.zeros((width, LANES - 2 - per_row), f32)], axis=1
    )
    mine, theirs = of_replicas(extra)
    extra = jnp.concatenate([mine[..., :2], theirs[..., :2], mine[..., 2 : 2 + per_row]], axis=2)
    extra = jnp.pad(extra, ((0, 0), (0, 0), (own_ffn, 2 * wide - own_ffn - 4 - per_row)))
    gu_total = (gu_mine + after(gu_got, near_share).astype(f32) + extra).astype(bf16)
    gu_own = lax.all_to_all(gu_total, TP, 0, 0, tiled=True)
    *sent, keep = combine(near_share, got, gu_total)
    qkv_mine, qkv_theirs = grads_of(dfused, *sent)
    qkv_got = other(qkv_theirs)
    rows_part = rows_grads(context, hidden, cotangent_all, PAIR + own_ffn, bf16 if outer == 1 else f32, qkv_theirs)
    if outer > 1:
        rows_out = lax.psum_scatter(rows_part[:PAIR], "outer", scatter_dimension=0, tiled=True)
        rows_down = lax.psum_scatter(rows_part[PAIR:], "outer", scatter_dimension=0, tiled=True)
        rows_part = jnp.concatenate([rows_out, rows_down], axis=0).astype(bf16)
    rows_got = other(rows_part)
    dnormed_own = 0.0
    leaving = []
    for i, pair in enumerate(sent):
        pair = shifted(after(pair, *leaving, rows_part) if leaving else pair, "y", ys, 1)
        at = 2 * i * length
        for j, k in enumerate(steps[2 * i : 2 * i + 2]):
            rows_at = slice(j * length, (j + 1) * length)
            term = keep[at : at + 2 * length][rows_at] + pair[rows_at].astype(f32)
            if k:
                leaving.append(term.astype(bf16))
                term = shifted(leaving[-1], "z", zs, zs - k).astype(f32)
            dnormed_own = dnormed_own + term
    inv = inv_std[:, None]
    xhat = centered * inv
    e = dnormed_own * gain_all
    tokens_back = inv * (e - jnp.mean(e, axis=1, keepdims=True) - xhat * jnp.mean(e * xhat, axis=1, keepdims=True))
    tokens_grad = (cotangent.astype(f32) + tokens_back).astype(bf16)
    qkv_total = (qkv_mine + qkv_got.astype(f32)).astype(bf16)
    qkv_total = after(qkv_total, gu_own, branch_own)
    qkv_own = lax.all_to_all(qkv_total, TP, 0, 0, tiled=True)
    gu_other = other(gu_own)
    gateup_grad = unpack(gu_own, gu_other, parts, 2, own_ffn, wide)
    qkv_grad = unpack(qkv_own, other(qkv_own), parts, 3, PAIR, PAIR)
    rows_grad = rows_part.astype(f32) + rows_got.astype(f32)
    sums_of = lambda x: jnp.sum(x[:, :, own_ffn : own_ffn + 4].astype(f32), axis=0)
    mine, theirs = sums_of(gu_own), sums_of(gu_other)
    here, there = mine[:, :2] + theirs[:, 2:], theirs[:, :2] + mine[:, 2:]
    first = part == 0
    own_sums = jnp.concatenate([jnp.where(first, here, there), jnp.where(first, there, here)], axis=0)
    bias_of = lambda x: x[:, :, own_ffn + 4 : own_ffn + 4 + per_row].reshape(tp, 3, PAIR).astype(f32)
    bias_grads = bias_of(gu_own) + bias_of(gu_other)
    bias_grads = bias_grads.transpose(1, 0, 2).reshape(-1)
    place = me * outer + lax.axis_index("outer")
    qkv_bias_grad = lax.dynamic_slice_in_dim(bias_grads, place * (3 * rows), 3 * rows, 0)
    return (
        block_output,
        tokens_grad,
        own_sums[:, 0],
        own_sums[:, 1],
        qkv_grad,
        qkv_bias_grad,
        rows_grad[: PAIR // outer],
        gateup_grad,
        rows_grad[PAIR // outer :],
    )


def solution(mesh):
    groups, shards = mesh.shape["replica"], mesh.shape["shard"]
    tp = math.gcd(shards, HEADS // 2)
    outer = shards // tp
    ys = cs = 2
    zs = tp // (ys * cs)
    inner_mesh = Mesh(mesh.devices.reshape(groups, zs, ys, cs, outer), ("replica", *TP, "outer"))
    everywhere = P(("replica", *TP, "outer"), None)
    vector = P((*TP, "outer"))
    matrix = P((*TP, "outer"), None)
    return jax.shard_map(
        functools.partial(per_device, groups, outer, zs, ys, cs),
        mesh=inner_mesh,
        in_specs=(everywhere, everywhere, vector, vector, matrix, vector, matrix, matrix, matrix, everywhere),
        out_specs=(everywhere, everywhere, vector, vector, matrix, vector, matrix, matrix, matrix),
        check_vma=False,
    )
```

```python
import functools
import math

import jax
import jax.numpy as jnp
from jax import lax
from jax.experimental import pallas as pl
from jax.experimental.pallas import tpu as pltpu
from jax.sharding import Mesh, PartitionSpec as P

HEADS = 32
HEAD_DIM = 64
ROT = 16
PAIR = 2 * HEAD_DIM
TP = ("z", "y", "c")
LANES = 128
SEQUENCES = 8
CHUNK = 512

epsilon = 1e-05
rope_base = 10000.0
score_scale = 1.0 / math.sqrt(HEAD_DIM)

bf16 = jnp.bfloat16
f32 = jnp.float32


def up_to(size, step):
    return -(-size // step) * step


def mm(a, b, dims):
    return lax.dot_general(a, b, (dims, ((), ())), preferred_element_type=f32)


def rotary_tables(segments):
    count, length = segments.shape
    indices = jnp.arange(length, dtype=jnp.int32)
    same_doc = segments[:, :, None] == segments[:, None, :]
    doc_start = jnp.min(jnp.where(same_doc, indices[None, None, :], length), axis=2)
    in_doc = (indices[None, :] - doc_start).astype(f32).reshape(count * length, 1)
    allowed = same_doc & (indices[:, None] >= indices[None, :])[None]
    half_rot = ROT // 2
    lane = jnp.arange(PAIR, dtype=jnp.int32) % HEAD_DIM
    inverse = rope_base ** (-((lane % half_rot).astype(f32) * (2.0 / ROT)))
    angles = in_doc * inverse[None, :]
    cos, sin = jnp.cos(angles), jnp.sin(angles)
    turned = (lane < ROT)[None, :]
    low = (lane < half_rot)[None, :]
    own = jnp.where(turned, cos, 1.0)
    after = jnp.where(low, -sin, 0.0)
    before = jnp.where(turned & ~low, sin, 0.0)
    return own, after, before, jnp.where(allowed, 0.0, -1e30).astype(f32)


def turn(x, own, after, before):
    half = ROT // 2
    width = x.shape[-1]
    return x * own + pltpu.roll(x, width - half, 1) * after + pltpu.roll(x, half, 1) * before


def head_mask(rows):
    return lax.broadcasted_iota(jnp.int32, (rows, PAIR), 1) < HEAD_DIM


def both_heads(x, first):
    zero = jnp.zeros_like(x)
    return jnp.concatenate([jnp.where(first, x, zero), jnp.where(first, zero, x)], axis=0)


def attend_kernel(joined_ref, bias_ref, own_ref, after_ref, before_ref, mask_ref, fused_ref, context_ref, probs_ref):
    length = mask_ref.shape[1]
    first = head_mask(length)
    for n in range(mask_ref.shape[0]):
        rows = pl.ds(n * length, length)
        own, after, before = own_ref[rows, :], after_ref[rows, :], before_ref[rows, :]
        joined = joined_ref[rows, :] + bias_ref[...]
        q = turn(joined[:, :PAIR], own, after, before).astype(bf16)
        k = turn(joined[:, PAIR : 2 * PAIR], own, after, before).astype(bf16)
        v = joined[:, 2 * PAIR :].astype(bf16)
        mask = mask_ref[n]
        scores = mm(both_heads(q, first), k, ((1,), (1,))) * score_scale
        scores = scores + jnp.concatenate([mask, mask], axis=0)
        top = jnp.max(scores, axis=1, keepdims=True)
        exps = jnp.exp(scores - top)
        probs = exps / jnp.sum(exps, axis=1, keepdims=True)
        low = probs.astype(bf16)
        side = jnp.concatenate([low[:length], low[length:]], axis=1)
        context = mm(side, both_heads(v, first), ((1,), (0,)))
        fused_ref[rows, :PAIR] = q
        fused_ref[rows, PAIR : 2 * PAIR] = k
        fused_ref[rows, 2 * PAIR :] = v
        context_ref[rows, :] = context.astype(bf16)
        probs_ref[n] = probs


def attend_back_kernel(fused_ref, probs_ref, dcontext_ref, own_ref, after_ref, before_ref, dfused_ref, sums_ref):
    length = probs_ref.shape[2]
    first = head_mask(length)
    total = jnp.zeros(sums_ref.shape, f32)
    for n in range(probs_ref.shape[0]):
        rows = pl.ds(n * length, length)
        own, after, before = own_ref[rows, :], after_ref[rows, :], before_ref[rows, :]
        q = fused_ref[rows, :PAIR]
        k = fused_ref[rows, PAIR : 2 * PAIR]
        v = fused_ref[rows, 2 * PAIR :]
        probs = probs_ref[n]
        dc = both_heads(dcontext_ref[rows, :], first)
        dprobs = mm(dc, v, ((1,), (1,)))
        dscores = (probs * (dprobs - jnp.sum(dprobs * probs, axis=1, keepdims=True))).astype(bf16)
        dv = mm(probs.astype(bf16), dc, ((0,), (0,)))
        side = jnp.concatenate([dscores[:length], dscores[length:]], axis=1)
        dq = mm(side, both_heads(k, first), ((1,), (0,))) * score_scale
        dk = mm(dscores, both_heads(q, first), ((0,), (0,))) * score_scale
        out = jnp.concatenate(
            [turn(dq, own, -after, -before).astype(bf16), turn(dk, own, -after, -before).astype(bf16), dv.astype(bf16)],
            axis=1,
        )
        dfused_ref[rows, :] = out
        total = total + jnp.sum(out.astype(f32), axis=0, keepdims=True)

    @pl.when(pl.program_id(0) == 0)
    def _():
        sums_ref[...] = jnp.zeros_like(sums_ref)

    sums_ref[...] += total


def attend(joined, bias, tables, count):
    own, after, before, mask = tables
    tokens, width = joined.shape
    length = tokens // count
    many = math.gcd(count, SEQUENCES)
    row = lambda w: pl.BlockSpec((many * length, w), lambda i: (i, 0))
    return pl.pallas_call(
        attend_kernel,
        name="attend",
        grid=(count // many,),
        in_specs=[
            row(width),
            pl.BlockSpec((1, width), lambda i: (0, 0)),
            row(PAIR),
            row(PAIR),
            row(PAIR),
            pl.BlockSpec((many, length, length), lambda i: (i, 0, 0)),
        ],
        out_specs=[row(width), row(PAIR), pl.BlockSpec((many, 2 * length, length), lambda i: (i, 0, 0))],
        out_shape=[
            jax.ShapeDtypeStruct((tokens, width), bf16),
            jax.ShapeDtypeStruct((tokens, PAIR), bf16),
            jax.ShapeDtypeStruct((count, 2 * length, length), f32),
        ],
        compiler_params=pltpu.CompilerParams(vmem_limit_bytes=32 << 20),
        cost_estimate=pl.CostEstimate(flops=tokens * length * PAIR * 8, bytes_accessed=tokens * 6000, transcendentals=tokens * length * 2),
    )(joined, bias, own, after, before, mask)


def attend_back(fused, probs, dcontext, tables, count, *others):
    own, after, before, _ = tables
    tokens, width = fused.shape
    length = tokens // count
    many = math.gcd(count, SEQUENCES)
    row = lambda w: pl.BlockSpec((many * length, w), lambda i: (i, 0))
    return pl.pallas_call(
        ignoring(attend_back_kernel, 6, len(others)),
        name="attend_back",
        grid=(count // many,),
        in_specs=[
            row(width),
            pl.BlockSpec((many, 2 * length, length), lambda i: (i, 0, 0)),
            row(PAIR),
            row(PAIR),
            row(PAIR),
            row(PAIR),
            *anywhere(others),
        ],
        out_specs=[row(width), pl.BlockSpec((1, width), lambda i: (0, 0))],
        out_shape=[jax.ShapeDtypeStruct((tokens, width), bf16), jax.ShapeDtypeStruct((1, width), f32)],
        compiler_params=pltpu.CompilerParams(vmem_limit_bytes=32 << 20),
        cost_estimate=pl.CostEstimate(flops=tokens * length * PAIR * 16, bytes_accessed=tokens * 6000, transcendentals=0),
    )(fused, probs, dcontext, own, after, before, *others)


def shifted(x, axis, size, step):
    return lax.ppermute(x, axis, [(i, (i + step) % size) for i in range(size)])


def limits(mib):
    return pltpu.CompilerParams(vmem_limit_bytes=mib << 20)


def cost(flops, moved):
    return pl.CostEstimate(flops=1, bytes_accessed=1, transcendentals=0)


def whole_block(array):
    return pl.BlockSpec(array.shape, lambda *_: (0,) * array.ndim)


def pack_kernel(part_ref, own_ref, out_ref, *, sections, tp, size, wide):
    own = own_ref[...]
    rows = own.shape[0]
    for t in range(tp):
        pieces = []
        for section in range(sections):
            at = (section * tp + t) * size
            pieces.append(own[:, at : at + size])
            if wide > size:
                pieces.append(jnp.zeros((rows, wide - size), own.dtype))
        out_ref[t] = jnp.concatenate(pieces, axis=1) if len(pieces) > 1 else pieces[0]


def pack(weight, part, groups, sections, tp, size, wide):
    rows, width = weight.shape
    half = rows // groups
    step = min(half, 16)
    return pl.pallas_call(
        functools.partial(pack_kernel, sections=sections, tp=tp, size=size, wide=wide),
        name="pack",
        grid_spec=pltpu.PrefetchScalarGridSpec(
            num_scalar_prefetch=1,
            grid=(half // step,),
            in_specs=[pl.BlockSpec((step, width), lambda i, part: (part[0] * (half // step) + i, 0))],
            out_specs=pl.BlockSpec((tp, step, sections * wide), lambda i, part: (0, i, 0)),
        ),
        out_shape=jax.ShapeDtypeStruct((tp, half, sections * wide), weight.dtype),
        compiler_params=limits(32),
        cost_estimate=cost(0, 4 * half * width),
    )(part, weight)


def nothing(*refs):
    del refs


def anywhere(arrays):
    return [pl.BlockSpec(memory_space=pl.ANY) for _ in arrays]


def after(x, *others):
    return pl.pallas_call(
        nothing,
        name="after",
        in_specs=anywhere((x, *others)),
        out_specs=pl.BlockSpec(memory_space=pl.ANY),
        out_shape=jax.ShapeDtypeStruct(x.shape, x.dtype),
        input_output_aliases={0: 0},
    )(x, *others)


def ignoring(kernel, at, count):
    return lambda *refs: kernel(*refs[:at], *refs[at + count :])


def unpack_kernel(part_ref, own_ref, other_ref, out_ref, *, sections, tp, size, wide):
    got = jnp.where(pl.program_id(0) == 0, own_ref[...], other_ref[...])
    for section in range(sections):
        pieces = [got[t, :, section * wide : section * wide + size] for t in range(tp)]
        out_ref[:, section * tp * size : (section + 1) * tp * size] = jnp.concatenate(pieces, axis=1).astype(f32)


def unpack(own, other, part, sections, size, wide):
    tp, half, width = own.shape
    step = min(half, 16)
    count = half // step
    return pl.pallas_call(
        functools.partial(unpack_kernel, sections=sections, tp=tp, size=size, wide=wide),
        name="unpack",
        grid_spec=pltpu.PrefetchScalarGridSpec(
            num_scalar_prefetch=1,
            grid=(2, count),
            in_specs=[
                pl.BlockSpec((tp, step, width), lambda i, j, part: (0, jnp.where(i == 0, j, count - 1), 0)),
                pl.BlockSpec((tp, step, width), lambda i, j, part: (0, jnp.where(i == 0, 0, j), 0)),
            ],
            out_specs=pl.BlockSpec(
                (step, sections * tp * size), lambda i, j, part: (lax.rem(part[0] + i, 2) * count + j, 0)
            ),
        ),
        out_shape=jax.ShapeDtypeStruct((2 * half, sections * tp * size), f32),
        compiler_params=limits(48),
        cost_estimate=cost(0, 12 * half * width * tp),
    )(part, own, other)


def gate_kernel(
    a_ref, b_ref, gain_ref, bias_ref, gu_ref, qkv_ref, stats_ref, normed_ref, gate_ref, up_ref, hidden_ref, joined_ref
):
    x = jnp.concatenate([a_ref[0], b_ref[0]], axis=0).astype(f32)
    mean = jnp.mean(x, axis=1, keepdims=True)
    centered = x - mean
    inv_std = lax.rsqrt(jnp.mean(centered * centered, axis=1, keepdims=True) + epsilon)
    lane = lax.broadcasted_iota(jnp.int32, stats_ref.shape, 1)
    stats_ref[...] = jnp.where(lane == 0, mean, inv_std)
    normed = (centered * inv_std * gain_ref[...] + bias_ref[...]).astype(bf16)
    normed_ref[...] = normed
    wide = gate_ref.shape[1]
    gateup = mm(normed, gu_ref[...], ((1,), (0,)))
    gate, up = gateup[:, :wide], gateup[:, wide:]
    gate_ref[...] = gate
    up_ref[...] = up
    hidden_ref[...] = (gate * jax.nn.sigmoid(gate) * up).astype(bf16)
    joined_ref[...] = mm(normed, qkv_ref[...], ((1,), (0,)))


def gate_forward(gathered, gain, bias, gu, qkv):
    count, padded, width = gathered.shape
    length, wide = LANES, gu.shape[1] // 2
    tokens = count * length
    block = lambda k: pl.BlockSpec((1, length, width), lambda i: (2 * i + k, 0, 0))
    row = lambda w: pl.BlockSpec((2 * length, w), lambda i: (i, 0))
    return pl.pallas_call(
        gate_kernel,
        name="gate_fwd",
        grid=(count // 2,),
        in_specs=[
            block(0),
            block(1),
            whole_block(gain),
            whole_block(bias),
            whole_block(gu),
            whole_block(qkv),
        ],
        out_specs=[row(LANES), row(width), row(wide), row(wide), row(wide), row(3 * PAIR)],
        out_shape=[
            jax.ShapeDtypeStruct((tokens, LANES), f32),
            jax.ShapeDtypeStruct((tokens, width), bf16),
            jax.ShapeDtypeStruct((tokens, wide), f32),
            jax.ShapeDtypeStruct((tokens, wide), f32),
            jax.ShapeDtypeStruct((tokens, wide), bf16),
            jax.ShapeDtypeStruct((tokens, 3 * PAIR), f32),
        ],
        compiler_params=limits(56),
        cost_estimate=cost(2 * tokens * width * (2 * wide + 3 * PAIR), tokens * (4 * width + 10 * wide + 12 * PAIR)),
    )(gathered, gathered, gain, bias, gu, qkv)


def branch_kernel(far, order_ref, ac_ref, bc_ref, ah_ref, bh_ref, w_ref, *refs):
    context = jnp.concatenate([ac_ref[...], bc_ref[...]], axis=0)
    hidden = jnp.concatenate([ah_ref[...], bh_ref[...]], axis=0)
    total = mm(context, w_ref[:PAIR, :], ((1,), (0,))) + mm(hidden, w_ref[PAIR:, :], ((1,), (0,)))
    if far:
        refs[0][...] = total.astype(bf16)
        return
    got_ref, sent_ref, keep_ref = refs
    keep_ref[...] = total + got_ref[...].astype(f32)

    @pl.when(pl.program_id(0) < pl.num_programs(0) // 2)
    def _():
        sent_ref[...] = keep_ref[...].astype(bf16)


def branches(order, context, hidden, w, got=None):
    tokens, wide = hidden.shape
    width = w.shape[1]
    count = order.shape[0]
    step = 2 * LANES
    row = lambda x, k: pl.BlockSpec((LANES, x.shape[1]), lambda i, order: (order[2 * i + k], 0))
    plain = pl.BlockSpec((step, width), lambda i, order: (i, 0))
    if got is None:
        out_specs = [plain]
        out_shape = [jax.ShapeDtypeStruct((count * LANES, width), bf16)]
        more = []
    else:
        sent = count // 4
        out_specs = [
            pl.BlockSpec((step, width), lambda i, order: (jnp.minimum(i, sent - 1), 0)),
            pl.BlockSpec((step, width), lambda i, order: (jnp.maximum(i - sent, 0), 0)),
        ]
        out_shape = [jax.ShapeDtypeStruct((count * LANES // 2, width), kind) for kind in (bf16, f32)]
        more = [got]
    return pl.pallas_call(
        functools.partial(branch_kernel, got is None),
        name="branch_far" if got is None else "branch_near",
        grid_spec=pltpu.PrefetchScalarGridSpec(
            num_scalar_prefetch=1,
            grid=(count // 2,),
            in_specs=[
                row(context, 0),
                row(context, 1),
                row(hidden, 0),
                row(hidden, 1),
                whole_block(w),
                *[plain for _ in more],
            ],
            out_specs=out_specs,
        ),
        out_shape=out_shape,
        compiler_params=limits(48),
        cost_estimate=cost(2 * tokens * width * (PAIR + wide), 2 * tokens * (width + PAIR + wide)),
    )(order, context, context, hidden, hidden, w, *more)


def gate_back_kernel(cotangent_ref, gate_ref, up_ref, w_ref, dgateup_ref, dcontext_ref):
    dinner = mm(cotangent_ref[...], w_ref[...], ((1,), (1,)))
    dcontext_ref[...] = dinner[:, :PAIR].astype(bf16)
    dhidden = dinner[:, PAIR:]
    gate, up = gate_ref[...], up_ref[...]
    s = jax.nn.sigmoid(gate)
    wide = gate.shape[1]
    dgateup_ref[:, :wide] = (dhidden * up * s * (1.0 + gate * (1.0 - s))).astype(bf16)
    dgateup_ref[:, wide:] = (dhidden * gate * s).astype(bf16)


def gate_backward(cotangent, gate, up, w, *others):
    tokens, wide = gate.shape
    width = w.shape[1]
    row = lambda w: pl.BlockSpec((2 * LANES, w), lambda i: (i, 0))
    return pl.pallas_call(
        ignoring(gate_back_kernel, 4, len(others)),
        name="gate_back",
        grid=(tokens // (2 * LANES),),
        in_specs=[row(width), row(wide), row(wide), whole_block(w), *anywhere(others)],
        out_specs=[row(2 * wide), row(PAIR)],
        out_shape=[jax.ShapeDtypeStruct((tokens, 2 * wide), bf16), jax.ShapeDtypeStruct((tokens, PAIR), bf16)],
        compiler_params=limits(48),
        cost_estimate=cost(2 * tokens * width * (PAIR + wide), tokens * (2 * width + 12 * wide)),
    )(cotangent, gate, up, w, *others)


def grads_kernel(part_ref, normed_ref, d_ref, mine_ref, theirs_ref):
    grads = mm(normed_ref[...], d_ref[...], ((0,), (0,)))
    count, half, _ = mine_ref.shape
    first = part_ref[0] == 0
    for t in range(count):
        low = grads[2 * t * half : (2 * t + 1) * half]
        high = grads[(2 * t + 1) * half : (2 * t + 2) * half]
        mine_ref[t] = jnp.where(first, low, high)
        theirs_ref[t] = jnp.where(first, high, low).astype(bf16)


def split_grads(part, normed, d, half, *others):
    tokens, width = normed.shape
    step = 4 * LANES
    out = d.shape[1]
    blocks = step // (2 * half)
    piece = lambda: pl.BlockSpec((blocks, half, out), lambda i, part: (i, 0, 0))
    return pl.pallas_call(
        ignoring(grads_kernel, 3, len(others)),
        name="grads",
        grid_spec=pltpu.PrefetchScalarGridSpec(
            num_scalar_prefetch=1,
            grid=(width // step,),
            in_specs=[pl.BlockSpec((tokens, step), lambda i, part: (0, i)), whole_block(d)]
            + anywhere(others),
            out_specs=[piece(), piece()],
        ),
        out_shape=[
            jax.ShapeDtypeStruct((width // (2 * half), half, out), f32),
            jax.ShapeDtypeStruct((width // (2 * half), half, out), bf16),
        ],
        compiler_params=limits(56),
        cost_estimate=cost(2 * tokens * width * d.shape[1], 2 * tokens * (width + d.shape[1]) + 3 * width * out),
    )(part, normed, d, *others)


def rows_kernel(context_ref, hidden_ref, cotangent_ref, out_ref):
    cotangent = cotangent_ref[...]
    out_ref[:PAIR, :] = mm(context_ref[...], cotangent, ((0,), (0,))).astype(out_ref.dtype)
    hidden = mm(hidden_ref[...], cotangent, ((0,), (0,)))
    out_ref[PAIR:, :] = hidden[: out_ref.shape[0] - PAIR].astype(out_ref.dtype)


def rows_grads(context, hidden, cotangent, own, kind, *others):
    tokens, width = cotangent.shape
    step = 4 * LANES
    return pl.pallas_call(
        ignoring(rows_kernel, 3, len(others)),
        name="rows",
        grid=(width // step,),
        in_specs=[
            whole_block(context),
            whole_block(hidden),
            pl.BlockSpec((tokens, step), lambda i: (0, i)),
            *anywhere(others),
        ],
        out_specs=pl.BlockSpec((own, step), lambda i: (0, i)),
        out_shape=jax.ShapeDtypeStruct((own, width), kind),
        compiler_params=limits(56),
        cost_estimate=cost(2 * tokens * width * own, tokens * width * 2),
    )(context, hidden, cotangent, *others)


def dnormed_kernel(order_ref, a_ref, b_ref, as_ref, bs_ref, ag_ref, bg_ref, aq_ref, bq_ref, gu_ref, qkv_ref, *refs):
    *far_refs, out_ref, sums_ref = refs if len(refs) == 2 else (*refs[:-2], refs[-1], refs[-2])
    step = pl.program_id(0)
    gateup = jnp.concatenate([ag_ref[...], bg_ref[...]], axis=0)
    fused = jnp.concatenate([aq_ref[...], bq_ref[...]], axis=0)

    @pl.when(step == 0)
    def _():
        sums_ref[...] = jnp.zeros_like(sums_ref)

    means = [ref[:, 0:1] for ref in (as_ref, bs_ref)]
    stds = [ref[:, 1:2] for ref in (as_ref, bs_ref)]
    width = gu_ref.shape[0]
    for at in range(0, width, CHUNK):
        cols = pl.ds(at, CHUNK)
        dnormed = mm(gateup, gu_ref[cols, :], ((1,), (1,))) + mm(fused, qkv_ref[cols, :], ((1,), (1,)))
        out_ref[:, cols] = dnormed.astype(out_ref.dtype)
        normal = jnp.concatenate(
            [(ref[0, :, cols].astype(f32) - mean) * std for ref, mean, std in zip((a_ref, b_ref), means, stds)], axis=0
        )
        sums_ref[0:1, cols] += jnp.sum(dnormed * normal, axis=0, keepdims=True)
        sums_ref[1:2, cols] += jnp.sum(dnormed, axis=0, keepdims=True)
    for i, far_ref in enumerate(far_refs):

        @pl.when(step == i)
        def _():
            far_ref[...] = out_ref[...]


def dnormed_share(order, *others, gathered, stats, dgateup, dfused, gu, qkv, far):
    width = gathered.shape[2]
    count = order.shape[0]
    step = 2 * LANES
    block = lambda k: pl.BlockSpec((1, LANES, width), lambda i, order: (order[2 * i + k], 0, 0))
    row = lambda x, k: pl.BlockSpec((LANES, x.shape[1]), lambda i, order: (order[2 * i + k], 0))
    if far:
        outs = [pl.BlockSpec((step, width), lambda i, order: (0, 0)) for _ in range(count // 2)]
        shapes = [jax.ShapeDtypeStruct((step, width), bf16) for _ in range(count // 2)]
    else:
        outs = [pl.BlockSpec((step, width), lambda i, order: (i, 0))]
        shapes = [jax.ShapeDtypeStruct((count * LANES, width), f32)]
    return pl.pallas_call(
        ignoring(dnormed_kernel, 11, len(others)),
        name="dn_far" if far else "dn_near",
        grid_spec=pltpu.PrefetchScalarGridSpec(
            num_scalar_prefetch=1,
            grid=(count // 2,),
            in_specs=[
                block(0),
                block(1),
                row(stats, 0),
                row(stats, 1),
                row(dgateup, 0),
                row(dgateup, 1),
                row(dfused, 0),
                row(dfused, 1),
                whole_block(gu),
                whole_block(qkv),
                *anywhere(others),
            ],
            out_specs=[*outs, pl.BlockSpec((8, width), lambda i, order: (0, 0))],
            scratch_shapes=[pltpu.VMEM((step, width), bf16)] if far else [],
        ),
        out_shape=[*shapes, jax.ShapeDtypeStruct((8, width), f32)],
        compiler_params=limits(60),
        cost_estimate=cost(
            2 * count * LANES * width * (dgateup.shape[1] + dfused.shape[1]), count * LANES * width * 8
        ),
    )(order, gathered, gathered, stats, stats, dgateup, dgateup, dfused, dfused, gu, qkv, *others)


def combine_kernel(near_ref, *refs):
    got_refs, sent_refs, keep_ref = refs[: len(refs) - 1 - (len(refs) - 1) // 3], refs[-1 - (len(refs) - 1) // 3 : -1], refs[-1]
    for i, got_ref in enumerate(got_refs):

        @pl.when(pl.program_id(0) == i)
        def _():
            total = near_ref[...] + got_ref[...].astype(f32)
            if i < len(sent_refs):
                sent_refs[i][...] = total.astype(bf16)
            else:
                keep_ref[...] = total


def combine(near, got, *others):
    rows, width = near.shape
    step = rows // len(got)
    sent = len(got) // 2
    fixed = pl.BlockSpec((step, width), lambda i: (0, 0))
    return pl.pallas_call(
        ignoring(combine_kernel, 1 + len(got), len(others)),
        name="combine",
        grid=(len(got),),
        in_specs=[pl.BlockSpec((step, width), lambda i: (i, 0)), *[fixed for _ in got], *anywhere(others)],
        out_specs=[fixed for _ in range(sent)] + [pl.BlockSpec((step, width), lambda i: (jnp.maximum(i - sent, 0), 0))],
        out_shape=[jax.ShapeDtypeStruct((step, width), bf16) for _ in range(sent)]
        + [jax.ShapeDtypeStruct((rows // 2, width), f32)],
        compiler_params=limits(48),
        cost_estimate=cost(0, rows * width * 9),
    )(near, *got, *others)


def add_kernel(keep_ref, got_ref, out_ref):
    out_ref[...] = (keep_ref[...] + got_ref[...].astype(f32)).astype(bf16)


def add_up(keep, got, *others):
    rows, width = keep.shape
    row = pl.BlockSpec((LANES, width), lambda i: (i, 0))
    return pl.pallas_call(
        ignoring(add_kernel, 2, len(others)),
        name="add_up",
        grid=(rows // LANES,),
        in_specs=[row, row, *anywhere(others)],
        out_specs=row,
        out_shape=jax.ShapeDtypeStruct((rows, width), bf16),
        compiler_params=limits(16),
        cost_estimate=cost(0, rows * width * 8),
    )(keep, got, *others)


def per_device(
    groups, outer, zs, ys, cs, tokens, segments, ln_gain, ln_bias, w_qkv, b_qkv, w_out, w_gateup, w_down, cotangent
):
    length, width = tokens.shape
    tp = zs * ys * cs
    shards = tp * outer
    z, y, c = (lax.axis_index(axis) for axis in TP)
    me = (z * ys + y) * cs + c

    own_ffn = w_gateup.shape[1] // 2 // tp
    wide = up_to(own_ffn, LANES)
    own_qkv = 3 * PAIR
    rows = w_qkv.shape[0]
    half = rows // groups
    part = lax.axis_index("replica")
    parts = part.astype(jnp.int32).reshape(1)
    steps = sorted(range(zs), key=lambda k: -min(k, zs - k))
    order = [
        jnp.stack(
            [
                (lax.rem(z + zs - k, zs) * ys + lax.rem(y + ys - j, ys)) * cs + lax.rem(c + cs - i, cs)
                for j in reversed(range(ys))
                for k in steps
            ]
        ).astype(jnp.int32)
        for i in range(cs)
    ]

    plain_order = [
        jnp.stack(
            [(k * ys + lax.rem(y + ys - j, ys)) * cs + lax.rem(c + cs - i, cs) for j in reversed(range(ys)) for k in range(zs)]
        ).astype(jnp.int32)
        for i in range(cs)
    ]

    small = jnp.concatenate([ln_gain, ln_bias, b_qkv, segments[0].astype(bf16)])
    of_params = 2 * rows + b_qkv.shape[0]
    small_rows = up_to(-(-small.shape[0] // width), 16)
    small_rows_of = jnp.pad(small, (0, small_rows * width - small.shape[0])).reshape(small_rows, width)
    packed = jnp.concatenate([tokens, small_rows_of], axis=0)
    gathered = lax.all_gather(packed, TP, axis=0, tiled=False)

    cotangent_all = lax.all_gather(cotangent, TP, axis=0, tiled=True)

    def other(own):
        return shifted(own, "replica", groups, 1)

    def to_columns(own):
        own = lax.all_to_all(own, TP, 0, 0, tiled=True)
        whole = jnp.zeros((tp, groups, half, own.shape[-1]), bf16)
        whole = lax.dynamic_update_slice(whole, own[:, None], (0, part, 0, 0))
        whole = lax.dynamic_update_slice(whole, other(own)[:, None], (0, 1 - part, 0, 0))
        whole = whole.reshape(tp, rows, own.shape[-1])
        if outer > 1:
            whole = lax.all_gather(whole, "outer", axis=1, tiled=False)
        return whole.reshape(width, own.shape[-1])

    gu_cols = to_columns(pack(w_gateup, parts, groups, 2, tp, own_ffn, wide))
    qkv_cols = to_columns(pack(w_qkv, parts, groups, 3, tp, PAIR, PAIR))
    if outer > 1:
        w_out = lax.all_gather(w_out, "outer", axis=0, tiled=True)
        w_down = lax.all_gather(w_down, "outer", axis=0, tiled=True)
    w_rows = jnp.concatenate([w_out, w_down, jnp.zeros((wide - own_ffn, width), bf16)], axis=0)

    vectors = gathered[:, length:, :].reshape(tp, -1)[:, : small.shape[0]]
    seg_all = vectors[:, of_params:].astype(jnp.int32)
    vectors = vectors[:, :of_params]
    if outer > 1:
        vectors = lax.all_gather(vectors, "outer", axis=1, tiled=False)
    vectors = vectors.reshape(shards, -1)
    gain_all = vectors[:, :rows].reshape(1, width).astype(f32)
    bias_all = vectors[:, rows : 2 * rows].reshape(1, width).astype(f32)
    qkv_bias = vectors[:, 2 * rows :].reshape(3, tp, PAIR).astype(f32)
    my_bias = lax.dynamic_index_in_dim(qkv_bias, me, 1, keepdims=False).reshape(1, own_qkv)
    tables = rotary_tables(seg_all)

    stats, normed, gate, up, hidden, joined = gate_forward(gathered, gain_all, bias_all, gu_cols, qkv_cols)
    fused, context, probs = attend(joined, my_bias, tables, tp)
    branch_far = branches(plain_order[1], context, hidden, w_rows)[0]
    branch_sent, branch_keep = branches(plain_order[0], context, hidden, w_rows, shifted(branch_far, "c", cs, 1))
    branch_got = shifted(branch_sent, "y", ys, 1)

    dgateup, dcontext = gate_backward(cotangent_all, gate, up, w_rows, branch_sent)

    def grads_of(d, *others):
        if outer == 1:
            return split_grads(parts, normed, d, half, *others)
        mine, theirs = of_replicas(mm(normed, d, ((0,), (0,))))
        return mine, theirs.astype(bf16)

    def of_replicas(grads):
        if outer > 1:
            grads = lax.psum_scatter(grads.reshape(tp, outer, rows, -1), "outer", scatter_dimension=1, tiled=True)
        grads = grads.reshape(tp, groups, half, -1)
        mine = lax.dynamic_index_in_dim(grads, part, 1, keepdims=False)
        return mine, lax.dynamic_index_in_dim(grads, 1 - part, 1, keepdims=False)

    gu_mine, gu_theirs = grads_of(dgateup)
    gu_got = other(gu_theirs)
    dfused, bias_sums = attend_back(fused, probs, dcontext, tables, tp, gu_theirs)
    share = functools.partial(dnormed_share, gathered=gathered, stats=stats, dgateup=dgateup, dfused=dfused, gu=gu_cols, qkv=qkv_cols)
    branch = add_up(branch_keep, branch_got, dfused)
    branch_own = lax.psum_scatter(branch, "z", scatter_dimension=0, tiled=True)
    tokens32 = tokens.astype(f32)
    block_output = (tokens32 + branch_own.astype(f32)).astype(bf16)
    *far_shares, far_sums = share(order[1], branch, far=True)
    got = [shifted(far_share, "c", cs, 1) for far_share in far_shares]
    near_share, near_sums = share(order[0], *far_shares, far=False)
    gain_sum, bias_sum = near_sums[0] + far_sums[0], near_sums[1] + far_sums[1]

    per_row = own_qkv // half
    tiled_sums = jnp.broadcast_to(bias_sums.reshape(1, half, per_row), (width // half, half, per_row)).reshape(width, per_row)
    extra = jnp.concatenate(
        [gain_sum[:, None], bias_sum[:, None], tiled_sums, jnp.zeros((width, LANES - 2 - per_row), f32)], axis=1
    )
    mine, theirs = of_replicas(extra)
    extra = jnp.concatenate([mine[..., :2], theirs[..., :2], mine[..., 2 : 2 + per_row]], axis=2)
    extra = jnp.pad(extra, ((0, 0), (0, 0), (own_ffn, 2 * wide - own_ffn - 4 - per_row)))
    *sent, keep = combine(near_share, got)
    gu_total = (gu_mine + after(gu_got, *sent).astype(f32) + extra).astype(bf16)
    gu_own = lax.all_to_all(gu_total, TP, 0, 0, tiled=True)
    qkv_mine, qkv_theirs = grads_of(dfused, gu_total)
    qkv_got = other(qkv_theirs)
    rows_part = rows_grads(context, hidden, cotangent_all, PAIR + own_ffn, bf16 if outer == 1 else f32, qkv_theirs)
    if outer > 1:
        rows_out = lax.psum_scatter(rows_part[:PAIR], "outer", scatter_dimension=0, tiled=True)
        rows_down = lax.psum_scatter(rows_part[PAIR:], "outer", scatter_dimension=0, tiled=True)
        rows_part = jnp.concatenate([rows_out, rows_down], axis=0).astype(bf16)
    rows_got = other(rows_part)
    dnormed_own = 0.0
    leaving = []
    for i, pair in enumerate(sent):
        pair = shifted(after(pair, *leaving, rows_part) if leaving else pair, "y", ys, 1)
        at = 2 * i * length
        for j, k in enumerate(steps[2 * i : 2 * i + 2]):
            rows_at = slice(j * length, (j + 1) * length)
            term = keep[at : at + 2 * length][rows_at] + pair[rows_at].astype(f32)
            if k:
                leaving.append(term.astype(bf16))
                term = shifted(leaving[-1], "z", zs, zs - k).astype(f32)
            dnormed_own = dnormed_own + term
    centered = tokens32 - jnp.mean(tokens32, axis=1, keepdims=True)
    inv = lax.rsqrt(jnp.mean(centered * centered, axis=1, keepdims=True) + epsilon)
    xhat = centered * inv
    e = dnormed_own * gain_all
    tokens_back = inv * (e - jnp.mean(e, axis=1, keepdims=True) - xhat * jnp.mean(e * xhat, axis=1, keepdims=True))
    tokens_grad = (cotangent.astype(f32) + tokens_back).astype(bf16)
    qkv_total = (qkv_mine + qkv_got.astype(f32)).astype(bf16)
    qkv_total = after(qkv_total, gu_own, branch_own)
    qkv_own = lax.all_to_all(qkv_total, TP, 0, 0, tiled=True)
    gu_other = other(gu_own)
    gateup_grad = unpack(gu_own, gu_other, parts, 2, own_ffn, wide)
    qkv_grad = unpack(qkv_own, other(qkv_own), parts, 3, PAIR, PAIR)
    rows_grad = rows_part.astype(f32) + rows_got.astype(f32)
    sums_of = lambda x: jnp.sum(x[:, :, own_ffn : own_ffn + 4].astype(f32), axis=0)
    mine, theirs = sums_of(gu_own), sums_of(gu_other)
    here, there = mine[:, :2] + theirs[:, 2:], theirs[:, :2] + mine[:, 2:]
    first = part == 0
    own_sums = jnp.concatenate([jnp.where(first, here, there), jnp.where(first, there, here)], axis=0)
    bias_of = lambda x: x[:, :, own_ffn + 4 : own_ffn + 4 + per_row].reshape(tp, 3, PAIR).astype(f32)
    bias_grads = bias_of(gu_own) + bias_of(gu_other)
    bias_grads = bias_grads.transpose(1, 0, 2).reshape(-1)
    place = me * outer + lax.axis_index("outer")
    qkv_bias_grad = lax.dynamic_slice_in_dim(bias_grads, place * (3 * rows), 3 * rows, 0)
    return (
        block_output,
        tokens_grad,
        own_sums[:, 0],
        own_sums[:, 1],
        qkv_grad,
        qkv_bias_grad,
        rows_grad[: PAIR // outer],
        gateup_grad,
        rows_grad[PAIR // outer :],
    )


def solution(mesh):
    groups, shards = mesh.shape["replica"], mesh.shape["shard"]
    tp = math.gcd(shards, HEADS // 2)
    outer = shards // tp
    ys = cs = 2
    zs = tp // (ys * cs)
    inner_mesh = Mesh(mesh.devices.reshape(groups, zs, ys, cs, outer), ("replica", *TP, "outer"))
    everywhere = P(("replica", *TP, "outer"), None)
    vector = P((*TP, "outer"))
    matrix = P((*TP, "outer"), None)
    return jax.shard_map(
        functools.partial(per_device, groups, outer, zs, ys, cs),
        mesh=inner_mesh,
        in_specs=(everywhere, everywhere, vector, vector, matrix, vector, matrix, matrix, matrix, everywhere),
        out_specs=(everywhere, everywhere, vector, vector, matrix, vector, matrix, matrix, matrix),
        check_vma=False,
    )
```

```python
import functools
import math

import jax
import jax.numpy as jnp
from jax import lax
from jax.experimental import pallas as pl
from jax.experimental.pallas import tpu as pltpu
from jax.sharding import Mesh, PartitionSpec as P

HEADS = 32
HEAD_DIM = 64
ROT = 16
PAIR = 2 * HEAD_DIM
TP = ("z", "y", "c")
LANES = 128
SEQUENCES = 8
CHUNK = 512

epsilon = 1e-05
rope_base = 10000.0
score_scale = 1.0 / math.sqrt(HEAD_DIM)

bf16 = jnp.bfloat16
f32 = jnp.float32


def up_to(size, step):
    return -(-size // step) * step


def mm(a, b, dims):
    return lax.dot_general(a, b, (dims, ((), ())), preferred_element_type=f32)


def rotary_tables(segments):
    count, length = segments.shape
    indices = jnp.arange(length, dtype=jnp.int32)
    same_doc = segments[:, :, None] == segments[:, None, :]
    doc_start = jnp.min(jnp.where(same_doc, indices[None, None, :], length), axis=2)
    in_doc = (indices[None, :] - doc_start).astype(f32).reshape(count * length, 1)
    allowed = same_doc & (indices[:, None] >= indices[None, :])[None]
    half_rot = ROT // 2
    lane = jnp.arange(PAIR, dtype=jnp.int32) % HEAD_DIM
    inverse = rope_base ** (-((lane % half_rot).astype(f32) * (2.0 / ROT)))
    angles = in_doc * inverse[None, :]
    cos, sin = jnp.cos(angles), jnp.sin(angles)
    turned = (lane < ROT)[None, :]
    low = (lane < half_rot)[None, :]
    own = jnp.where(turned, cos, 1.0)
    after = jnp.where(low, -sin, 0.0)
    before = jnp.where(turned & ~low, sin, 0.0)
    return own, after, before, jnp.where(allowed, 0.0, -1e30).astype(f32)


def turn(x, own, after, before):
    half = ROT // 2
    width = x.shape[-1]
    return x * own + pltpu.roll(x, width - half, 1) * after + pltpu.roll(x, half, 1) * before


def head_mask(rows):
    return lax.broadcasted_iota(jnp.int32, (rows, PAIR), 1) < HEAD_DIM


def both_heads(x, first):
    zero = jnp.zeros_like(x)
    return jnp.concatenate([jnp.where(first, x, zero), jnp.where(first, zero, x)], axis=0)


def attend_kernel(joined_ref, bias_ref, own_ref, after_ref, before_ref, mask_ref, fused_ref, context_ref, probs_ref):
    length = mask_ref.shape[1]
    first = head_mask(length)
    for n in range(mask_ref.shape[0]):
        rows = pl.ds(n * length, length)
        own, after, before = own_ref[rows, :], after_ref[rows, :], before_ref[rows, :]
        joined = joined_ref[rows, :] + bias_ref[...]
        q = turn(joined[:, :PAIR], own, after, before).astype(bf16)
        k = turn(joined[:, PAIR : 2 * PAIR], own, after, before).astype(bf16)
        v = joined[:, 2 * PAIR :].astype(bf16)
        mask = mask_ref[n]
        scores = mm(both_heads(q, first), k, ((1,), (1,))) * score_scale
        scores = scores + jnp.concatenate([mask, mask], axis=0)
        top = jnp.max(scores, axis=1, keepdims=True)
        exps = jnp.exp(scores - top)
        probs = exps / jnp.sum(exps, axis=1, keepdims=True)
        low = probs.astype(bf16)
        side = jnp.concatenate([low[:length], low[length:]], axis=1)
        context = mm(side, both_heads(v, first), ((1,), (0,)))
        fused_ref[rows, :PAIR] = q
        fused_ref[rows, PAIR : 2 * PAIR] = k
        fused_ref[rows, 2 * PAIR :] = v
        context_ref[rows, :] = context.astype(bf16)
        probs_ref[n] = probs


def attend_back_kernel(fused_ref, probs_ref, dcontext_ref, own_ref, after_ref, before_ref, dfused_ref, sums_ref):
    length = probs_ref.shape[2]
    first = head_mask(length)
    total = jnp.zeros(sums_ref.shape, f32)
    for n in range(probs_ref.shape[0]):
        rows = pl.ds(n * length, length)
        own, after, before = own_ref[rows, :], after_ref[rows, :], before_ref[rows, :]
        q = fused_ref[rows, :PAIR]
        k = fused_ref[rows, PAIR : 2 * PAIR]
        v = fused_ref[rows, 2 * PAIR :]
        probs = probs_ref[n]
        dc = both_heads(dcontext_ref[rows, :], first)
        dprobs = mm(dc, v, ((1,), (1,)))
        dscores = (probs * (dprobs - jnp.sum(dprobs * probs, axis=1, keepdims=True))).astype(bf16)
        dv = mm(probs.astype(bf16), dc, ((0,), (0,)))
        side = jnp.concatenate([dscores[:length], dscores[length:]], axis=1)
        dq = mm(side, both_heads(k, first), ((1,), (0,))) * score_scale
        dk = mm(dscores, both_heads(q, first), ((0,), (0,))) * score_scale
        out = jnp.concatenate(
            [turn(dq, own, -after, -before).astype(bf16), turn(dk, own, -after, -before).astype(bf16), dv.astype(bf16)],
            axis=1,
        )
        dfused_ref[rows, :] = out
        total = total + jnp.sum(out.astype(f32), axis=0, keepdims=True)

    @pl.when(pl.program_id(0) == 0)
    def _():
        sums_ref[...] = jnp.zeros_like(sums_ref)

    sums_ref[...] += total


def attend(joined, bias, tables, count):
    own, after, before, mask = tables
    tokens, width = joined.shape
    length = tokens // count
    many = math.gcd(count, SEQUENCES)
    row = lambda w: pl.BlockSpec((many * length, w), lambda i: (i, 0))
    return pl.pallas_call(
        attend_kernel,
        name="attend",
        grid=(count // many,),
        in_specs=[
            row(width),
            pl.BlockSpec((1, width), lambda i: (0, 0)),
            row(PAIR),
            row(PAIR),
            row(PAIR),
            pl.BlockSpec((many, length, length), lambda i: (i, 0, 0)),
        ],
        out_specs=[row(width), row(PAIR), pl.BlockSpec((many, 2 * length, length), lambda i: (i, 0, 0))],
        out_shape=[
            jax.ShapeDtypeStruct((tokens, width), bf16),
            jax.ShapeDtypeStruct((tokens, PAIR), bf16),
            jax.ShapeDtypeStruct((count, 2 * length, length), f32),
        ],
        compiler_params=pltpu.CompilerParams(vmem_limit_bytes=32 << 20),
        cost_estimate=pl.CostEstimate(flops=tokens * length * PAIR * 8, bytes_accessed=tokens * 6000, transcendentals=tokens * length * 2),
    )(joined, bias, own, after, before, mask)


def attend_back(fused, probs, dcontext, tables, count, *others):
    own, after, before, _ = tables
    tokens, width = fused.shape
    length = tokens // count
    many = math.gcd(count, SEQUENCES)
    row = lambda w: pl.BlockSpec((many * length, w), lambda i: (i, 0))
    return pl.pallas_call(
        ignoring(attend_back_kernel, 6, len(others)),
        name="attend_back",
        grid=(count // many,),
        in_specs=[
            row(width),
            pl.BlockSpec((many, 2 * length, length), lambda i: (i, 0, 0)),
            row(PAIR),
            row(PAIR),
            row(PAIR),
            row(PAIR),
            *anywhere(others),
        ],
        out_specs=[row(width), pl.BlockSpec((1, width), lambda i: (0, 0))],
        out_shape=[jax.ShapeDtypeStruct((tokens, width), bf16), jax.ShapeDtypeStruct((1, width), f32)],
        compiler_params=pltpu.CompilerParams(vmem_limit_bytes=32 << 20),
        cost_estimate=pl.CostEstimate(flops=tokens * length * PAIR * 16, bytes_accessed=tokens * 6000, transcendentals=0),
    )(fused, probs, dcontext, own, after, before, *others)


def shifted(x, axis, size, step):
    return lax.ppermute(x, axis, [(i, (i + step) % size) for i in range(size)])


def limits(mib):
    return pltpu.CompilerParams(vmem_limit_bytes=mib << 20)


def cost(flops, moved):
    return pl.CostEstimate(flops=1, bytes_accessed=1, transcendentals=0)


def whole_block(array):
    return pl.BlockSpec(array.shape, lambda *_: (0,) * array.ndim)


def pack_kernel(part_ref, own_ref, out_ref, *, sections, tp, size, wide):
    own = own_ref[...]
    rows = own.shape[0]
    for t in range(tp):
        pieces = []
        for section in range(sections):
            at = (section * tp + t) * size
            pieces.append(own[:, at : at + size])
            if wide > size:
                pieces.append(jnp.zeros((rows, wide - size), own.dtype))
        out_ref[t] = jnp.concatenate(pieces, axis=1) if len(pieces) > 1 else pieces[0]


def pack(weight, part, groups, sections, tp, size, wide):
    rows, width = weight.shape
    half = rows // groups
    step = min(half, 16)
    return pl.pallas_call(
        functools.partial(pack_kernel, sections=sections, tp=tp, size=size, wide=wide),
        name="pack",
        grid_spec=pltpu.PrefetchScalarGridSpec(
            num_scalar_prefetch=1,
            grid=(half // step,),
            in_specs=[pl.BlockSpec((step, width), lambda i, part: (part[0] * (half // step) + i, 0))],
            out_specs=pl.BlockSpec((tp, step, sections * wide), lambda i, part: (0, i, 0)),
        ),
        out_shape=jax.ShapeDtypeStruct((tp, half, sections * wide), weight.dtype),
        compiler_params=limits(32),
        cost_estimate=cost(0, 4 * half * width),
    )(part, weight)


def nothing(*refs):
    del refs


def anywhere(arrays):
    return [pl.BlockSpec(memory_space=pl.ANY) for _ in arrays]


def after(x, *others):
    return pl.pallas_call(
        nothing,
        name="after",
        in_specs=anywhere((x, *others)),
        out_specs=pl.BlockSpec(memory_space=pl.ANY),
        out_shape=jax.ShapeDtypeStruct(x.shape, x.dtype),
        input_output_aliases={0: 0},
    )(x, *others)


def ignoring(kernel, at, count):
    return lambda *refs: kernel(*refs[:at], *refs[at + count :])


def unpack_kernel(part_ref, own_ref, other_ref, out_ref, *, sections, tp, size, wide):
    got = jnp.where(pl.program_id(0) == 0, own_ref[...], other_ref[...])
    for section in range(sections):
        pieces = [got[t, :, section * wide : section * wide + size] for t in range(tp)]
        out_ref[:, section * tp * size : (section + 1) * tp * size] = jnp.concatenate(pieces, axis=1).astype(f32)


def unpack(own, other, part, sections, size, wide):
    tp, half, width = own.shape
    step = min(half, 16)
    count = half // step
    return pl.pallas_call(
        functools.partial(unpack_kernel, sections=sections, tp=tp, size=size, wide=wide),
        name="unpack",
        grid_spec=pltpu.PrefetchScalarGridSpec(
            num_scalar_prefetch=1,
            grid=(2, count),
            in_specs=[
                pl.BlockSpec((tp, step, width), lambda i, j, part: (0, jnp.where(i == 0, j, count - 1), 0)),
                pl.BlockSpec((tp, step, width), lambda i, j, part: (0, jnp.where(i == 0, 0, j), 0)),
            ],
            out_specs=pl.BlockSpec(
                (step, sections * tp * size), lambda i, j, part: (lax.rem(part[0] + i, 2) * count + j, 0)
            ),
        ),
        out_shape=jax.ShapeDtypeStruct((2 * half, sections * tp * size), f32),
        compiler_params=limits(48),
        cost_estimate=cost(0, 12 * half * width * tp),
    )(part, own, other)


def gate_kernel(
    a_ref, b_ref, gain_ref, bias_ref, gu_ref, qkv_ref, stats_ref, normed_ref, gate_ref, up_ref, hidden_ref, joined_ref
):
    x = jnp.concatenate([a_ref[0], b_ref[0]], axis=0).astype(f32)
    mean = jnp.mean(x, axis=1, keepdims=True)
    centered = x - mean
    inv_std = lax.rsqrt(jnp.mean(centered * centered, axis=1, keepdims=True) + epsilon)
    lane = lax.broadcasted_iota(jnp.int32, stats_ref.shape, 1)
    stats_ref[...] = jnp.where(lane == 0, mean, inv_std)
    normed = (centered * inv_std * gain_ref[...] + bias_ref[...]).astype(bf16)
    normed_ref[...] = normed
    wide = gate_ref.shape[1]
    gateup = mm(normed, gu_ref[...], ((1,), (0,)))
    gate, up = gateup[:, :wide], gateup[:, wide:]
    gate_ref[...] = gate
    up_ref[...] = up
    hidden_ref[...] = (gate * jax.nn.sigmoid(gate) * up).astype(bf16)
    joined_ref[...] = mm(normed, qkv_ref[...], ((1,), (0,)))


def gate_forward(gathered, gain, bias, gu, qkv):
    count, padded, width = gathered.shape
    length, wide = LANES, gu.shape[1] // 2
    tokens = count * length
    block = lambda k: pl.BlockSpec((1, length, width), lambda i: (2 * i + k, 0, 0))
    row = lambda w: pl.BlockSpec((2 * length, w), lambda i: (i, 0))
    return pl.pallas_call(
        gate_kernel,
        name="gate_fwd",
        grid=(count // 2,),
        in_specs=[
            block(0),
            block(1),
            whole_block(gain),
            whole_block(bias),
            whole_block(gu),
            whole_block(qkv),
        ],
        out_specs=[row(LANES), row(width), row(wide), row(wide), row(wide), row(3 * PAIR)],
        out_shape=[
            jax.ShapeDtypeStruct((tokens, LANES), f32),
            jax.ShapeDtypeStruct((tokens, width), bf16),
            jax.ShapeDtypeStruct((tokens, wide), f32),
            jax.ShapeDtypeStruct((tokens, wide), f32),
            jax.ShapeDtypeStruct((tokens, wide), bf16),
            jax.ShapeDtypeStruct((tokens, 3 * PAIR), f32),
        ],
        compiler_params=limits(56),
        cost_estimate=cost(2 * tokens * width * (2 * wide + 3 * PAIR), tokens * (4 * width + 10 * wide + 12 * PAIR)),
    )(gathered, gathered, gain, bias, gu, qkv)


def branch_kernel(far, order_ref, ac_ref, bc_ref, ah_ref, bh_ref, w_ref, *refs):
    context = jnp.concatenate([ac_ref[...], bc_ref[...]], axis=0)
    hidden = jnp.concatenate([ah_ref[...], bh_ref[...]], axis=0)
    total = mm(context, w_ref[:PAIR, :], ((1,), (0,))) + mm(hidden, w_ref[PAIR:, :], ((1,), (0,)))
    if far:
        refs[0][...] = total.astype(bf16)
        return
    got_ref, sent_ref, keep_ref = refs
    keep_ref[...] = total + got_ref[...].astype(f32)

    @pl.when(pl.program_id(0) < pl.num_programs(0) // 2)
    def _():
        sent_ref[...] = keep_ref[...].astype(bf16)


def branches(order, context, hidden, w, got=None):
    tokens, wide = hidden.shape
    width = w.shape[1]
    count = order.shape[0]
    step = 2 * LANES
    row = lambda x, k: pl.BlockSpec((LANES, x.shape[1]), lambda i, order: (order[2 * i + k], 0))
    plain = pl.BlockSpec((step, width), lambda i, order: (i, 0))
    if got is None:
        out_specs = [plain]
        out_shape = [jax.ShapeDtypeStruct((count * LANES, width), bf16)]
        more = []
    else:
        sent = count // 4
        out_specs = [
            pl.BlockSpec((step, width), lambda i, order: (jnp.minimum(i, sent - 1), 0)),
            pl.BlockSpec((step, width), lambda i, order: (jnp.maximum(i - sent, 0), 0)),
        ]
        out_shape = [jax.ShapeDtypeStruct((count * LANES // 2, width), kind) for kind in (bf16, f32)]
        more = [got]
    return pl.pallas_call(
        functools.partial(branch_kernel, got is None),
        name="branch_far" if got is None else "branch_near",
        grid_spec=pltpu.PrefetchScalarGridSpec(
            num_scalar_prefetch=1,
            grid=(count // 2,),
            in_specs=[
                row(context, 0),
                row(context, 1),
                row(hidden, 0),
                row(hidden, 1),
                whole_block(w),
                *[plain for _ in more],
            ],
            out_specs=out_specs,
        ),
        out_shape=out_shape,
        compiler_params=limits(48),
        cost_estimate=cost(2 * tokens * width * (PAIR + wide), 2 * tokens * (width + PAIR + wide)),
    )(order, context, context, hidden, hidden, w, *more)


def gate_back_kernel(cotangent_ref, gate_ref, up_ref, w_ref, dgateup_ref, dcontext_ref):
    dinner = mm(cotangent_ref[...], w_ref[...], ((1,), (1,)))
    dcontext_ref[...] = dinner[:, :PAIR].astype(bf16)
    dhidden = dinner[:, PAIR:]
    gate, up = gate_ref[...], up_ref[...]
    s = jax.nn.sigmoid(gate)
    wide = gate.shape[1]
    dgateup_ref[:, :wide] = (dhidden * up * s * (1.0 + gate * (1.0 - s))).astype(bf16)
    dgateup_ref[:, wide:] = (dhidden * gate * s).astype(bf16)


def gate_backward(cotangent, gate, up, w, *others):
    tokens, wide = gate.shape
    width = w.shape[1]
    row = lambda w: pl.BlockSpec((2 * LANES, w), lambda i: (i, 0))
    return pl.pallas_call(
        ignoring(gate_back_kernel, 4, len(others)),
        name="gate_back",
        grid=(tokens // (2 * LANES),),
        in_specs=[row(width), row(wide), row(wide), whole_block(w), *anywhere(others)],
        out_specs=[row(2 * wide), row(PAIR)],
        out_shape=[jax.ShapeDtypeStruct((tokens, 2 * wide), bf16), jax.ShapeDtypeStruct((tokens, PAIR), bf16)],
        compiler_params=limits(48),
        cost_estimate=cost(2 * tokens * width * (PAIR + wide), tokens * (2 * width + 12 * wide)),
    )(cotangent, gate, up, w, *others)


def grads_kernel(part_ref, normed_ref, d_ref, mine_ref, theirs_ref):
    grads = mm(normed_ref[...], d_ref[...], ((0,), (0,)))
    count, half, _ = mine_ref.shape
    first = part_ref[0] == 0
    for t in range(count):
        low = grads[2 * t * half : (2 * t + 1) * half]
        high = grads[(2 * t + 1) * half : (2 * t + 2) * half]
        mine_ref[t] = jnp.where(first, low, high)
        theirs_ref[t] = jnp.where(first, high, low).astype(bf16)


def split_grads(part, normed, d, half, *others):
    tokens, width = normed.shape
    step = 4 * LANES
    out = d.shape[1]
    blocks = step // (2 * half)
    piece = lambda: pl.BlockSpec((blocks, half, out), lambda i, part: (i, 0, 0))
    return pl.pallas_call(
        ignoring(grads_kernel, 3, len(others)),
        name="grads",
        grid_spec=pltpu.PrefetchScalarGridSpec(
            num_scalar_prefetch=1,
            grid=(width // step,),
            in_specs=[pl.BlockSpec((tokens, step), lambda i, part: (0, i)), whole_block(d)]
            + anywhere(others),
            out_specs=[piece(), piece()],
        ),
        out_shape=[
            jax.ShapeDtypeStruct((width // (2 * half), half, out), f32),
            jax.ShapeDtypeStruct((width // (2 * half), half, out), bf16),
        ],
        compiler_params=limits(56),
        cost_estimate=cost(2 * tokens * width * d.shape[1], 2 * tokens * (width + d.shape[1]) + 3 * width * out),
    )(part, normed, d, *others)


def rows_kernel(context_ref, hidden_ref, cotangent_ref, out_ref):
    cotangent = cotangent_ref[...]
    out_ref[:PAIR, :] = mm(context_ref[...], cotangent, ((0,), (0,))).astype(out_ref.dtype)
    hidden = mm(hidden_ref[...], cotangent, ((0,), (0,)))
    out_ref[PAIR:, :] = hidden[: out_ref.shape[0] - PAIR].astype(out_ref.dtype)


def rows_grads(context, hidden, cotangent, own, kind, *others):
    tokens, width = cotangent.shape
    step = 4 * LANES
    return pl.pallas_call(
        ignoring(rows_kernel, 3, len(others)),
        name="rows",
        grid=(width // step,),
        in_specs=[
            whole_block(context),
            whole_block(hidden),
            pl.BlockSpec((tokens, step), lambda i: (0, i)),
            *anywhere(others),
        ],
        out_specs=pl.BlockSpec((own, step), lambda i: (0, i)),
        out_shape=jax.ShapeDtypeStruct((own, width), kind),
        compiler_params=limits(56),
        cost_estimate=cost(2 * tokens * width * own, tokens * width * 2),
    )(context, hidden, cotangent, *others)


def dnormed_kernel(order_ref, a_ref, b_ref, as_ref, bs_ref, ag_ref, bg_ref, aq_ref, bq_ref, gu_ref, qkv_ref, *refs):
    if len(refs) == 2:
        far_refs, (out_ref, sums_ref) = (), refs
    else:
        keep_ref, got_ref, *far_refs, branch_ref, sums_ref, out_ref = refs
        branch_ref[...] = (keep_ref[...] + got_ref[...].astype(f32)).astype(bf16)
    step = pl.program_id(0)
    gateup = jnp.concatenate([ag_ref[...], bg_ref[...]], axis=0)
    fused = jnp.concatenate([aq_ref[...], bq_ref[...]], axis=0)

    @pl.when(step == 0)
    def _():
        sums_ref[...] = jnp.zeros_like(sums_ref)

    means = [ref[:, 0:1] for ref in (as_ref, bs_ref)]
    stds = [ref[:, 1:2] for ref in (as_ref, bs_ref)]
    width = gu_ref.shape[0]
    for at in range(0, width, CHUNK):
        cols = pl.ds(at, CHUNK)
        dnormed = mm(gateup, gu_ref[cols, :], ((1,), (1,))) + mm(fused, qkv_ref[cols, :], ((1,), (1,)))
        out_ref[:, cols] = dnormed.astype(out_ref.dtype)
        normal = jnp.concatenate(
            [(ref[0, :, cols].astype(f32) - mean) * std for ref, mean, std in zip((a_ref, b_ref), means, stds)], axis=0
        )
        sums_ref[0:1, cols] += jnp.sum(dnormed * normal, axis=0, keepdims=True)
        sums_ref[1:2, cols] += jnp.sum(dnormed, axis=0, keepdims=True)
    for i, far_ref in enumerate(far_refs):

        @pl.when(step == i)
        def _():
            far_ref[...] = out_ref[...]


def dnormed_share(order, *others, gathered, stats, dgateup, dfused, gu, qkv, far=()):
    width = gathered.shape[2]
    count = order.shape[0]
    step = 2 * LANES
    block = lambda k: pl.BlockSpec((1, LANES, width), lambda i, order: (order[2 * i + k], 0, 0))
    row = lambda x, k: pl.BlockSpec((LANES, x.shape[1]), lambda i, order: (order[2 * i + k], 0))
    if far:
        outs = [pl.BlockSpec((step, width), lambda i, order: (0, 0)) for _ in range(count // 2)]
        shapes = [jax.ShapeDtypeStruct((step, width), bf16) for _ in range(count // 2)]
        part = pl.BlockSpec((far[0].shape[0] // (count // 2), width), lambda i, order: (i, 0))
        outs.append(part)
        shapes.append(jax.ShapeDtypeStruct(far[0].shape, bf16))
    else:
        outs = [pl.BlockSpec((step, width), lambda i, order: (i, 0))]
        shapes = [jax.ShapeDtypeStruct((count * LANES, width), f32)]
    return pl.pallas_call(
        ignoring(dnormed_kernel, 11 + len(far), len(others)),
        name="dn_far" if far else "dn_near",
        grid_spec=pltpu.PrefetchScalarGridSpec(
            num_scalar_prefetch=1,
            grid=(count // 2,),
            in_specs=[
                block(0),
                block(1),
                row(stats, 0),
                row(stats, 1),
                row(dgateup, 0),
                row(dgateup, 1),
                row(dfused, 0),
                row(dfused, 1),
                whole_block(gu),
                whole_block(qkv),
                *[part for _ in far],
                *anywhere(others),
            ],
            out_specs=[*outs, pl.BlockSpec((8, width), lambda i, order: (0, 0))],
            scratch_shapes=[pltpu.VMEM((step, width), bf16)] if far else [],
        ),
        out_shape=[*shapes, jax.ShapeDtypeStruct((8, width), f32)],
        compiler_params=limits(60),
        cost_estimate=cost(
            2 * count * LANES * width * (dgateup.shape[1] + dfused.shape[1]), count * LANES * width * 8
        ),
    )(order, gathered, gathered, stats, stats, dgateup, dgateup, dfused, dfused, gu, qkv, *far, *others)


def combine_kernel(near_ref, *refs):
    got_refs, sent_refs, keep_ref = refs[: len(refs) - 1 - (len(refs) - 1) // 3], refs[-1 - (len(refs) - 1) // 3 : -1], refs[-1]
    for i, got_ref in enumerate(got_refs):

        @pl.when(pl.program_id(0) == i)
        def _():
            total = near_ref[...] + got_ref[...].astype(f32)
            if i < len(sent_refs):
                sent_refs[i][...] = total.astype(bf16)
            else:
                keep_ref[...] = total


def combine(near, got, *others):
    rows, width = near.shape
    step = rows // len(got)
    sent = len(got) // 2
    fixed = pl.BlockSpec((step, width), lambda i: (0, 0))
    return pl.pallas_call(
        ignoring(combine_kernel, 1 + len(got), len(others)),
        name="combine",
        grid=(len(got),),
        in_specs=[pl.BlockSpec((step, width), lambda i: (i, 0)), *[fixed for _ in got], *anywhere(others)],
        out_specs=[fixed for _ in range(sent)] + [pl.BlockSpec((step, width), lambda i: (jnp.maximum(i - sent, 0), 0))],
        out_shape=[jax.ShapeDtypeStruct((step, width), bf16) for _ in range(sent)]
        + [jax.ShapeDtypeStruct((rows // 2, width), f32)],
        compiler_params=limits(48),
        cost_estimate=cost(0, rows * width * 9),
    )(near, *got, *others)


def per_device(
    groups, outer, zs, ys, cs, tokens, segments, ln_gain, ln_bias, w_qkv, b_qkv, w_out, w_gateup, w_down, cotangent
):
    length, width = tokens.shape
    tp = zs * ys * cs
    shards = tp * outer
    z, y, c = (lax.axis_index(axis) for axis in TP)
    me = (z * ys + y) * cs + c

    own_ffn = w_gateup.shape[1] // 2 // tp
    wide = up_to(own_ffn, LANES)
    own_qkv = 3 * PAIR
    rows = w_qkv.shape[0]
    half = rows // groups
    part = lax.axis_index("replica")
    parts = part.astype(jnp.int32).reshape(1)
    steps = sorted(range(zs), key=lambda k: -min(k, zs - k))
    order = [
        jnp.stack(
            [
                (lax.rem(z + zs - k, zs) * ys + lax.rem(y + ys - j, ys)) * cs + lax.rem(c + cs - i, cs)
                for j in reversed(range(ys))
                for k in steps
            ]
        ).astype(jnp.int32)
        for i in range(cs)
    ]

    plain_order = [
        jnp.stack(
            [(k * ys + lax.rem(y + ys - j, ys)) * cs + lax.rem(c + cs - i, cs) for j in reversed(range(ys)) for k in range(zs)]
        ).astype(jnp.int32)
        for i in range(cs)
    ]

    small = jnp.concatenate([ln_gain, ln_bias, b_qkv, segments[0].astype(bf16)])
    of_params = 2 * rows + b_qkv.shape[0]
    small_rows = up_to(-(-small.shape[0] // width), 16)
    small_rows_of = jnp.pad(small, (0, small_rows * width - small.shape[0])).reshape(small_rows, width)
    packed = jnp.concatenate([tokens, small_rows_of], axis=0)
    gathered = lax.all_gather(packed, TP, axis=0, tiled=False)

    cotangent_all = lax.all_gather(cotangent, TP, axis=0, tiled=True)

    def other(own):
        return shifted(own, "replica", groups, 1)

    def to_columns(own):
        own = lax.all_to_all(own, TP, 0, 0, tiled=True)
        whole = jnp.zeros((tp, groups, half, own.shape[-1]), bf16)
        whole = lax.dynamic_update_slice(whole, own[:, None], (0, part, 0, 0))
        whole = lax.dynamic_update_slice(whole, other(own)[:, None], (0, 1 - part, 0, 0))
        whole = whole.reshape(tp, rows, own.shape[-1])
        if outer > 1:
            whole = lax.all_gather(whole, "outer", axis=1, tiled=False)
        return whole.reshape(width, own.shape[-1])

    gu_cols = to_columns(pack(w_gateup, parts, groups, 2, tp, own_ffn, wide))
    qkv_cols = to_columns(pack(w_qkv, parts, groups, 3, tp, PAIR, PAIR))
    if outer > 1:
        w_out = lax.all_gather(w_out, "outer", axis=0, tiled=True)
        w_down = lax.all_gather(w_down, "outer", axis=0, tiled=True)
    w_rows = jnp.concatenate([w_out, w_down, jnp.zeros((wide - own_ffn, width), bf16)], axis=0)

    vectors = gathered[:, length:, :].reshape(tp, -1)[:, : small.shape[0]]
    seg_all = vectors[:, of_params:].astype(jnp.int32)
    vectors = vectors[:, :of_params]
    if outer > 1:
        vectors = lax.all_gather(vectors, "outer", axis=1, tiled=False)
    vectors = vectors.reshape(shards, -1)
    gain_all = vectors[:, :rows].reshape(1, width).astype(f32)
    bias_all = vectors[:, rows : 2 * rows].reshape(1, width).astype(f32)
    qkv_bias = vectors[:, 2 * rows :].reshape(3, tp, PAIR).astype(f32)
    my_bias = lax.dynamic_index_in_dim(qkv_bias, me, 1, keepdims=False).reshape(1, own_qkv)
    tables = rotary_tables(seg_all)

    stats, normed, gate, up, hidden, joined = gate_forward(gathered, gain_all, bias_all, gu_cols, qkv_cols)
    fused, context, probs = attend(joined, my_bias, tables, tp)
    branch_far = branches(plain_order[1], context, hidden, w_rows)[0]
    branch_sent, branch_keep = branches(plain_order[0], context, hidden, w_rows, shifted(branch_far, "c", cs, 1))
    branch_got = shifted(branch_sent, "y", ys, 1)

    dgateup, dcontext = gate_backward(cotangent_all, gate, up, w_rows, branch_sent)

    def grads_of(d, *others):
        if outer == 1:
            return split_grads(parts, normed, d, half, *others)
        mine, theirs = of_replicas(mm(normed, d, ((0,), (0,))))
        return mine, theirs.astype(bf16)

    def of_replicas(grads):
        if outer > 1:
            grads = lax.psum_scatter(grads.reshape(tp, outer, rows, -1), "outer", scatter_dimension=1, tiled=True)
        grads = grads.reshape(tp, groups, half, -1)
        mine = lax.dynamic_index_in_dim(grads, part, 1, keepdims=False)
        return mine, lax.dynamic_index_in_dim(grads, 1 - part, 1, keepdims=False)

    gu_mine, gu_theirs = grads_of(dgateup)
    gu_got = other(gu_theirs)
    dfused, bias_sums = attend_back(fused, probs, dcontext, tables, tp, gu_theirs)
    share = functools.partial(dnormed_share, gathered=gathered, stats=stats, dgateup=dgateup, dfused=dfused, gu=gu_cols, qkv=qkv_cols)
    *far_shares, branch, far_sums = share(order[1], far=(branch_keep, branch_got))
    branch_own = lax.psum_scatter(branch, "z", scatter_dimension=0, tiled=True)
    tokens32 = tokens.astype(f32)
    block_output = (tokens32 + branch_own.astype(f32)).astype(bf16)
    got = [shifted(far_share, "c", cs, 1) for far_share in far_shares]
    near_share, near_sums = share(order[0], *far_shares)
    gain_sum, bias_sum = near_sums[0] + far_sums[0], near_sums[1] + far_sums[1]

    per_row = own_qkv // half
    tiled_sums = jnp.broadcast_to(bias_sums.reshape(1, half, per_row), (width // half, half, per_row)).reshape(width, per_row)
    extra = jnp.concatenate(
        [gain_sum[:, None], bias_sum[:, None], tiled_sums, jnp.zeros((width, LANES - 2 - per_row), f32)], axis=1
    )
    mine, theirs = of_replicas(extra)
    extra = jnp.concatenate([mine[..., :2], theirs[..., :2], mine[..., 2 : 2 + per_row]], axis=2)
    extra = jnp.pad(extra, ((0, 0), (0, 0), (own_ffn, 2 * wide - own_ffn - 4 - per_row)))
    *sent, keep = combine(near_share, got)
    gu_total = (gu_mine + after(gu_got, *sent).astype(f32) + extra).astype(bf16)
    gu_own = lax.all_to_all(gu_total, TP, 0, 0, tiled=True)
    qkv_mine, qkv_theirs = grads_of(dfused, gu_total)
    qkv_got = other(qkv_theirs)
    rows_part = rows_grads(context, hidden, cotangent_all, PAIR + own_ffn, bf16 if outer == 1 else f32, qkv_theirs)
    if outer > 1:
        rows_out = lax.psum_scatter(rows_part[:PAIR], "outer", scatter_dimension=0, tiled=True)
        rows_down = lax.psum_scatter(rows_part[PAIR:], "outer", scatter_dimension=0, tiled=True)
        rows_part = jnp.concatenate([rows_out, rows_down], axis=0).astype(bf16)
    rows_got = other(rows_part)
    dnormed_own = 0.0
    leaving = []
    for i, pair in enumerate(sent):
        pair = shifted(after(pair, *leaving, rows_part) if leaving else pair, "y", ys, 1)
        at = 2 * i * length
        for j, k in enumerate(steps[2 * i : 2 * i + 2]):
            rows_at = slice(j * length, (j + 1) * length)
            term = keep[at : at + 2 * length][rows_at] + pair[rows_at].astype(f32)
            if k:
                leaving.append(term.astype(bf16))
                term = shifted(leaving[-1], "z", zs, zs - k).astype(f32)
            dnormed_own = dnormed_own + term
    centered = tokens32 - jnp.mean(tokens32, axis=1, keepdims=True)
    inv = lax.rsqrt(jnp.mean(centered * centered, axis=1, keepdims=True) + epsilon)
    xhat = centered * inv
    e = dnormed_own * gain_all
    tokens_back = inv * (e - jnp.mean(e, axis=1, keepdims=True) - xhat * jnp.mean(e * xhat, axis=1, keepdims=True))
    tokens_grad = (cotangent.astype(f32) + tokens_back).astype(bf16)
    qkv_total = (qkv_mine + qkv_got.astype(f32)).astype(bf16)
    qkv_total = after(qkv_total, gu_own, branch_own)
    qkv_own = lax.all_to_all(qkv_total, TP, 0, 0, tiled=True)
    gu_other = other(gu_own)
    gateup_grad = unpack(gu_own, gu_other, parts, 2, own_ffn, wide)
    qkv_grad = unpack(qkv_own, other(qkv_own), parts, 3, PAIR, PAIR)
    rows_grad = rows_part.astype(f32) + rows_got.astype(f32)
    sums_of = lambda x: jnp.sum(x[:, :, own_ffn : own_ffn + 4].astype(f32), axis=0)
    mine, theirs = sums_of(gu_own), sums_of(gu_other)
    here, there = mine[:, :2] + theirs[:, 2:], theirs[:, :2] + mine[:, 2:]
    first = part == 0
    own_sums = jnp.concatenate([jnp.where(first, here, there), jnp.where(first, there, here)], axis=0)
    bias_of = lambda x: x[:, :, own_ffn + 4 : own_ffn + 4 + per_row].reshape(tp, 3, PAIR).astype(f32)
    bias_grads = bias_of(gu_own) + bias_of(gu_other)
    bias_grads = bias_grads.transpose(1, 0, 2).reshape(-1)
    place = me * outer + lax.axis_index("outer")
    qkv_bias_grad = lax.dynamic_slice_in_dim(bias_grads, place * (3 * rows), 3 * rows, 0)
    return (
        block_output,
        tokens_grad,
        own_sums[:, 0],
        own_sums[:, 1],
        qkv_grad,
        qkv_bias_grad,
        rows_grad[: PAIR // outer],
        gateup_grad,
        rows_grad[PAIR // outer :],
    )


def solution(mesh):
    groups, shards = mesh.shape["replica"], mesh.shape["shard"]
    tp = math.gcd(shards, HEADS // 2)
    outer = shards // tp
    ys = cs = 2
    zs = tp // (ys * cs)
    inner_mesh = Mesh(mesh.devices.reshape(groups, zs, ys, cs, outer), ("replica", *TP, "outer"))
    everywhere = P(("replica", *TP, "outer"), None)
    vector = P((*TP, "outer"))
    matrix = P((*TP, "outer"), None)
    return jax.shard_map(
        functools.partial(per_device, groups, outer, zs, ys, cs),
        mesh=inner_mesh,
        in_specs=(everywhere, everywhere, vector, vector, matrix, vector, matrix, matrix, matrix, everywhere),
        out_specs=(everywhere, everywhere, vector, vector, matrix, vector, matrix, matrix, matrix),
        check_vma=False,
    )
```

```python
import functools
import math

import jax
import jax.numpy as jnp
from jax import lax
from jax.experimental import pallas as pl
from jax.experimental.pallas import tpu as pltpu
from jax.sharding import Mesh, PartitionSpec as P

HEADS = 32
HEAD_DIM = 64
ROT = 16
PAIR = 2 * HEAD_DIM
TP = ("z", "y", "c")
LANES = 128
SEQUENCES = 8
CHUNK = 512

epsilon = 1e-05
rope_base = 10000.0
score_scale = 1.0 / math.sqrt(HEAD_DIM)

bf16 = jnp.bfloat16
f32 = jnp.float32


def up_to(size, step):
    return -(-size // step) * step


def mm(a, b, dims):
    return lax.dot_general(a, b, (dims, ((), ())), preferred_element_type=f32)


def rotary_tables(segments):
    count, length = segments.shape
    indices = jnp.arange(length, dtype=jnp.int32)
    same_doc = segments[:, :, None] == segments[:, None, :]
    doc_start = jnp.min(jnp.where(same_doc, indices[None, None, :], length), axis=2)
    in_doc = (indices[None, :] - doc_start).astype(f32).reshape(count * length, 1)
    allowed = same_doc & (indices[:, None] >= indices[None, :])[None]
    half_rot = ROT // 2
    lane = jnp.arange(PAIR, dtype=jnp.int32) % HEAD_DIM
    inverse = rope_base ** (-((lane % half_rot).astype(f32) * (2.0 / ROT)))
    angles = in_doc * inverse[None, :]
    cos, sin = jnp.cos(angles), jnp.sin(angles)
    turned = (lane < ROT)[None, :]
    low = (lane < half_rot)[None, :]
    own = jnp.where(turned, cos, 1.0)
    after = jnp.where(low, -sin, 0.0)
    before = jnp.where(turned & ~low, sin, 0.0)
    return own, after, before, jnp.where(allowed, 0.0, -1e30).astype(f32)


def turn(x, own, after, before):
    half = ROT // 2
    width = x.shape[-1]
    return x * own + pltpu.roll(x, width - half, 1) * after + pltpu.roll(x, half, 1) * before


def head_mask(rows):
    return lax.broadcasted_iota(jnp.int32, (rows, PAIR), 1) < HEAD_DIM


def both_heads(x, first):
    zero = jnp.zeros_like(x)
    return jnp.concatenate([jnp.where(first, x, zero), jnp.where(first, zero, x)], axis=0)


def attend_kernel(joined_ref, bias_ref, own_ref, after_ref, before_ref, mask_ref, fused_ref, context_ref, probs_ref):
    length = mask_ref.shape[1]
    first = head_mask(length)
    for n in range(mask_ref.shape[0]):
        rows = pl.ds(n * length, length)
        own, after, before = own_ref[rows, :], after_ref[rows, :], before_ref[rows, :]
        joined = joined_ref[rows, :] + bias_ref[...]
        q = turn(joined[:, :PAIR], own, after, before).astype(bf16)
        k = turn(joined[:, PAIR : 2 * PAIR], own, after, before).astype(bf16)
        v = joined[:, 2 * PAIR :].astype(bf16)
        mask = mask_ref[n]
        scores = mm(both_heads(q, first), k, ((1,), (1,))) * score_scale
        scores = scores + jnp.concatenate([mask, mask], axis=0)
        top = jnp.max(scores, axis=1, keepdims=True)
        exps = jnp.exp(scores - top)
        probs = exps / jnp.sum(exps, axis=1, keepdims=True)
        low = probs.astype(bf16)
        side = jnp.concatenate([low[:length], low[length:]], axis=1)
        context = mm(side, both_heads(v, first), ((1,), (0,)))
        fused_ref[rows, :PAIR] = q
        fused_ref[rows, PAIR : 2 * PAIR] = k
        fused_ref[rows, 2 * PAIR :] = v
        context_ref[rows, :] = context.astype(bf16)
        probs_ref[n] = probs


def attend_back_kernel(fused_ref, probs_ref, dcontext_ref, own_ref, after_ref, before_ref, dfused_ref, sums_ref):
    length = probs_ref.shape[2]
    first = head_mask(length)
    total = jnp.zeros(sums_ref.shape, f32)
    for n in range(probs_ref.shape[0]):
        rows = pl.ds(n * length, length)
        own, after, before = own_ref[rows, :], after_ref[rows, :], before_ref[rows, :]
        q = fused_ref[rows, :PAIR]
        k = fused_ref[rows, PAIR : 2 * PAIR]
        v = fused_ref[rows, 2 * PAIR :]
        probs = probs_ref[n]
        dc = both_heads(dcontext_ref[rows, :], first)
        dprobs = mm(dc, v, ((1,), (1,)))
        dscores = (probs * (dprobs - jnp.sum(dprobs * probs, axis=1, keepdims=True))).astype(bf16)
        dv = mm(probs.astype(bf16), dc, ((0,), (0,)))
        side = jnp.concatenate([dscores[:length], dscores[length:]], axis=1)
        dq = mm(side, both_heads(k, first), ((1,), (0,))) * score_scale
        dk = mm(dscores, both_heads(q, first), ((0,), (0,))) * score_scale
        out = jnp.concatenate(
            [turn(dq, own, -after, -before).astype(bf16), turn(dk, own, -after, -before).astype(bf16), dv.astype(bf16)],
            axis=1,
        )
        dfused_ref[rows, :] = out
        total = total + jnp.sum(out.astype(f32), axis=0, keepdims=True)

    @pl.when(pl.program_id(0) == 0)
    def _():
        sums_ref[...] = jnp.zeros_like(sums_ref)

    sums_ref[...] += total


def attend(joined, bias, tables, count):
    own, after, before, mask = tables
    tokens, width = joined.shape
    length = tokens // count
    many = math.gcd(count, SEQUENCES)
    row = lambda w: pl.BlockSpec((many * length, w), lambda i: (i, 0))
    return pl.pallas_call(
        attend_kernel,
        name="attend",
        grid=(count // many,),
        in_specs=[
            row(width),
            pl.BlockSpec((1, width), lambda i: (0, 0)),
            row(PAIR),
            row(PAIR),
            row(PAIR),
            pl.BlockSpec((many, length, length), lambda i: (i, 0, 0)),
        ],
        out_specs=[row(width), row(PAIR), pl.BlockSpec((many, 2 * length, length), lambda i: (i, 0, 0))],
        out_shape=[
            jax.ShapeDtypeStruct((tokens, width), bf16),
            jax.ShapeDtypeStruct((tokens, PAIR), bf16),
            jax.ShapeDtypeStruct((count, 2 * length, length), f32),
        ],
        compiler_params=pltpu.CompilerParams(vmem_limit_bytes=32 << 20),
        cost_estimate=pl.CostEstimate(flops=tokens * length * PAIR * 8, bytes_accessed=tokens * 6000, transcendentals=tokens * length * 2),
    )(joined, bias, own, after, before, mask)


def attend_back(fused, probs, dcontext, tables, count, *others):
    own, after, before, _ = tables
    tokens, width = fused.shape
    length = tokens // count
    many = math.gcd(count, SEQUENCES)
    row = lambda w: pl.BlockSpec((many * length, w), lambda i: (i, 0))
    return pl.pallas_call(
        ignoring(attend_back_kernel, 6, len(others)),
        name="attend_back",
        grid=(count // many,),
        in_specs=[
            row(width),
            pl.BlockSpec((many, 2 * length, length), lambda i: (i, 0, 0)),
            row(PAIR),
            row(PAIR),
            row(PAIR),
            row(PAIR),
            *anywhere(others),
        ],
        out_specs=[row(width), pl.BlockSpec((1, width), lambda i: (0, 0))],
        out_shape=[jax.ShapeDtypeStruct((tokens, width), bf16), jax.ShapeDtypeStruct((1, width), f32)],
        compiler_params=pltpu.CompilerParams(vmem_limit_bytes=32 << 20),
        cost_estimate=pl.CostEstimate(flops=tokens * length * PAIR * 16, bytes_accessed=tokens * 6000, transcendentals=0),
    )(fused, probs, dcontext, own, after, before, *others)


def shifted(x, axis, size, step):
    return lax.ppermute(x, axis, [(i, (i + step) % size) for i in range(size)])


def limits(mib):
    return pltpu.CompilerParams(vmem_limit_bytes=mib << 20)


def cost(flops, moved):
    return pl.CostEstimate(flops=1, bytes_accessed=1, transcendentals=0)


def whole_block(array):
    return pl.BlockSpec(array.shape, lambda *_: (0,) * array.ndim)


def pack_kernel(part_ref, own_ref, out_ref, *, sections, tp, size, wide):
    own = own_ref[...]
    rows = own.shape[0]
    for t in range(tp):
        pieces = []
        for section in range(sections):
            at = (section * tp + t) * size
            pieces.append(own[:, at : at + size])
            if wide > size:
                pieces.append(jnp.zeros((rows, wide - size), own.dtype))
        out_ref[t] = jnp.concatenate(pieces, axis=1) if len(pieces) > 1 else pieces[0]


def pack(weight, part, groups, sections, tp, size, wide):
    rows, width = weight.shape
    half = rows // groups
    step = min(half, 16)
    return pl.pallas_call(
        functools.partial(pack_kernel, sections=sections, tp=tp, size=size, wide=wide),
        name="pack",
        grid_spec=pltpu.PrefetchScalarGridSpec(
            num_scalar_prefetch=1,
            grid=(half // step,),
            in_specs=[pl.BlockSpec((step, width), lambda i, part: (part[0] * (half // step) + i, 0))],
            out_specs=pl.BlockSpec((tp, step, sections * wide), lambda i, part: (0, i, 0)),
        ),
        out_shape=jax.ShapeDtypeStruct((tp, half, sections * wide), weight.dtype),
        compiler_params=limits(32),
        cost_estimate=cost(0, 4 * half * width),
    )(part, weight)


def nothing(*refs):
    del refs


def anywhere(arrays):
    return [pl.BlockSpec(memory_space=pl.ANY) for _ in arrays]


def after(x, *others):
    return pl.pallas_call(
        nothing,
        name="after",
        in_specs=anywhere((x, *others)),
        out_specs=pl.BlockSpec(memory_space=pl.ANY),
        out_shape=jax.ShapeDtypeStruct(x.shape, x.dtype),
        input_output_aliases={0: 0},
    )(x, *others)


def ignoring(kernel, at, count):
    return lambda *refs: kernel(*refs[:at], *refs[at + count :])


def unpack_kernel(part_ref, own_ref, other_ref, out_ref, *, sections, tp, size, wide):
    got = jnp.where(pl.program_id(0) == 0, own_ref[...], other_ref[...])
    for section in range(sections):
        pieces = [got[t, :, section * wide : section * wide + size] for t in range(tp)]
        out_ref[:, section * tp * size : (section + 1) * tp * size] = jnp.concatenate(pieces, axis=1).astype(f32)


def unpack(own, other, part, sections, size, wide):
    tp, half, width = own.shape
    step = min(half, 16)
    count = half // step
    return pl.pallas_call(
        functools.partial(unpack_kernel, sections=sections, tp=tp, size=size, wide=wide),
        name="unpack",
        grid_spec=pltpu.PrefetchScalarGridSpec(
            num_scalar_prefetch=1,
            grid=(2, count),
            in_specs=[
                pl.BlockSpec((tp, step, width), lambda i, j, part: (0, jnp.where(i == 0, j, count - 1), 0)),
                pl.BlockSpec((tp, step, width), lambda i, j, part: (0, jnp.where(i == 0, 0, j), 0)),
            ],
            out_specs=pl.BlockSpec(
                (step, sections * tp * size), lambda i, j, part: (lax.rem(part[0] + i, 2) * count + j, 0)
            ),
        ),
        out_shape=jax.ShapeDtypeStruct((2 * half, sections * tp * size), f32),
        compiler_params=limits(48),
        cost_estimate=cost(0, 12 * half * width * tp),
    )(part, own, other)


def gate_kernel(
    a_ref, b_ref, gain_ref, bias_ref, gu_ref, qkv_ref, stats_ref, normed_ref, gate_ref, up_ref, hidden_ref, joined_ref
):
    x = jnp.concatenate([a_ref[0], b_ref[0]], axis=0).astype(f32)
    mean = jnp.mean(x, axis=1, keepdims=True)
    centered = x - mean
    inv_std = lax.rsqrt(jnp.mean(centered * centered, axis=1, keepdims=True) + epsilon)
    lane = lax.broadcasted_iota(jnp.int32, stats_ref.shape, 1)
    stats_ref[...] = jnp.where(lane == 0, mean, inv_std)
    normed = (centered * inv_std * gain_ref[...] + bias_ref[...]).astype(bf16)
    normed_ref[...] = normed
    wide = gate_ref.shape[1]
    gateup = mm(normed, gu_ref[...], ((1,), (0,)))
    gate, up = gateup[:, :wide], gateup[:, wide:]
    gate_ref[...] = gate
    up_ref[...] = up
    hidden_ref[...] = (gate * jax.nn.sigmoid(gate) * up).astype(bf16)
    joined_ref[...] = mm(normed, qkv_ref[...], ((1,), (0,)))


def gate_forward(gathered, gain, bias, gu, qkv):
    count, padded, width = gathered.shape
    length, wide = LANES, gu.shape[1] // 2
    tokens = count * length
    block = lambda k: pl.BlockSpec((1, length, width), lambda i: (2 * i + k, 0, 0))
    row = lambda w: pl.BlockSpec((2 * length, w), lambda i: (i, 0))
    return pl.pallas_call(
        gate_kernel,
        name="gate_fwd",
        grid=(count // 2,),
        in_specs=[
            block(0),
            block(1),
            whole_block(gain),
            whole_block(bias),
            whole_block(gu),
            whole_block(qkv),
        ],
        out_specs=[row(LANES), row(width), row(wide), row(wide), row(wide), row(3 * PAIR)],
        out_shape=[
            jax.ShapeDtypeStruct((tokens, LANES), f32),
            jax.ShapeDtypeStruct((tokens, width), bf16),
            jax.ShapeDtypeStruct((tokens, wide), f32),
            jax.ShapeDtypeStruct((tokens, wide), f32),
            jax.ShapeDtypeStruct((tokens, wide), bf16),
            jax.ShapeDtypeStruct((tokens, 3 * PAIR), f32),
        ],
        compiler_params=limits(56),
        cost_estimate=cost(2 * tokens * width * (2 * wide + 3 * PAIR), tokens * (4 * width + 10 * wide + 12 * PAIR)),
    )(gathered, gathered, gain, bias, gu, qkv)


def branch_kernel(far, order_ref, ac_ref, bc_ref, ah_ref, bh_ref, w_ref, *refs):
    context = jnp.concatenate([ac_ref[...], bc_ref[...]], axis=0)
    hidden = jnp.concatenate([ah_ref[...], bh_ref[...]], axis=0)
    total = mm(context, w_ref[:PAIR, :], ((1,), (0,))) + mm(hidden, w_ref[PAIR:, :], ((1,), (0,)))
    if far:
        refs[0][...] = total.astype(bf16)
        return
    got_ref, sent_ref, keep_ref = refs
    keep_ref[...] = total + got_ref[...].astype(f32)

    @pl.when(pl.program_id(0) < pl.num_programs(0) // 2)
    def _():
        sent_ref[...] = keep_ref[...].astype(bf16)


def branches(order, context, hidden, w, got=None):
    tokens, wide = hidden.shape
    width = w.shape[1]
    count = order.shape[0]
    step = 2 * LANES
    row = lambda x, k: pl.BlockSpec((LANES, x.shape[1]), lambda i, order: (order[2 * i + k], 0))
    plain = pl.BlockSpec((step, width), lambda i, order: (i, 0))
    if got is None:
        out_specs = [plain]
        out_shape = [jax.ShapeDtypeStruct((count * LANES, width), bf16)]
        more = []
    else:
        sent = count // 4
        out_specs = [
            pl.BlockSpec((step, width), lambda i, order: (jnp.minimum(i, sent - 1), 0)),
            pl.BlockSpec((step, width), lambda i, order: (jnp.maximum(i - sent, 0), 0)),
        ]
        out_shape = [jax.ShapeDtypeStruct((count * LANES // 2, width), kind) for kind in (bf16, f32)]
        more = [got]
    return pl.pallas_call(
        functools.partial(branch_kernel, got is None),
        name="branch_far" if got is None else "branch_near",
        grid_spec=pltpu.PrefetchScalarGridSpec(
            num_scalar_prefetch=1,
            grid=(count // 2,),
            in_specs=[
                row(context, 0),
                row(context, 1),
                row(hidden, 0),
                row(hidden, 1),
                whole_block(w),
                *[plain for _ in more],
            ],
            out_specs=out_specs,
        ),
        out_shape=out_shape,
        compiler_params=limits(48),
        cost_estimate=cost(2 * tokens * width * (PAIR + wide), 2 * tokens * (width + PAIR + wide)),
    )(order, context, context, hidden, hidden, w, *more)


def gate_back_kernel(cotangent_ref, gate_ref, up_ref, w_ref, dgateup_ref, dcontext_ref):
    dinner = mm(cotangent_ref[...], w_ref[...], ((1,), (1,)))
    dcontext_ref[...] = dinner[:, :PAIR].astype(bf16)
    dhidden = dinner[:, PAIR:]
    gate, up = gate_ref[...], up_ref[...]
    s = jax.nn.sigmoid(gate)
    wide = gate.shape[1]
    dgateup_ref[:, :wide] = (dhidden * up * s * (1.0 + gate * (1.0 - s))).astype(bf16)
    dgateup_ref[:, wide:] = (dhidden * gate * s).astype(bf16)


def gate_backward(cotangent, gate, up, w, *others):
    tokens, wide = gate.shape
    width = w.shape[1]
    row = lambda w: pl.BlockSpec((2 * LANES, w), lambda i: (i, 0))
    return pl.pallas_call(
        ignoring(gate_back_kernel, 4, len(others)),
        name="gate_back",
        grid=(tokens // (2 * LANES),),
        in_specs=[row(width), row(wide), row(wide), whole_block(w), *anywhere(others)],
        out_specs=[row(2 * wide), row(PAIR)],
        out_shape=[jax.ShapeDtypeStruct((tokens, 2 * wide), bf16), jax.ShapeDtypeStruct((tokens, PAIR), bf16)],
        compiler_params=limits(48),
        cost_estimate=cost(2 * tokens * width * (PAIR + wide), tokens * (2 * width + 12 * wide)),
    )(cotangent, gate, up, w, *others)


def grads_kernel(part_ref, normed_ref, d_ref, mine_ref, theirs_ref):
    grads = mm(normed_ref[...], d_ref[...], ((0,), (0,)))
    count, half, _ = mine_ref.shape
    first = part_ref[0] == 0
    for t in range(count):
        low = grads[2 * t * half : (2 * t + 1) * half]
        high = grads[(2 * t + 1) * half : (2 * t + 2) * half]
        mine_ref[t] = jnp.where(first, low, high)
        theirs_ref[t] = jnp.where(first, high, low).astype(bf16)


def split_grads(part, normed, d, half, *others):
    tokens, width = normed.shape
    step = 4 * LANES
    out = d.shape[1]
    blocks = step // (2 * half)
    piece = lambda: pl.BlockSpec((blocks, half, out), lambda i, part: (i, 0, 0))
    return pl.pallas_call(
        ignoring(grads_kernel, 3, len(others)),
        name="grads",
        grid_spec=pltpu.PrefetchScalarGridSpec(
            num_scalar_prefetch=1,
            grid=(width // step,),
            in_specs=[pl.BlockSpec((tokens, step), lambda i, part: (0, i)), whole_block(d)]
            + anywhere(others),
            out_specs=[piece(), piece()],
        ),
        out_shape=[
            jax.ShapeDtypeStruct((width // (2 * half), half, out), f32),
            jax.ShapeDtypeStruct((width // (2 * half), half, out), bf16),
        ],
        compiler_params=limits(56),
        cost_estimate=cost(2 * tokens * width * d.shape[1], 2 * tokens * (width + d.shape[1]) + 3 * width * out),
    )(part, normed, d, *others)


def rows_kernel(context_ref, hidden_ref, cotangent_ref, out_ref):
    cotangent = cotangent_ref[...]
    out_ref[:PAIR, :] = mm(context_ref[...], cotangent, ((0,), (0,))).astype(out_ref.dtype)
    hidden = mm(hidden_ref[...], cotangent, ((0,), (0,)))
    out_ref[PAIR:, :] = hidden[: out_ref.shape[0] - PAIR].astype(out_ref.dtype)


def rows_grads(context, hidden, cotangent, own, kind, *others):
    tokens, width = cotangent.shape
    step = 4 * LANES
    return pl.pallas_call(
        ignoring(rows_kernel, 3, len(others)),
        name="rows",
        grid=(width // step,),
        in_specs=[
            whole_block(context),
            whole_block(hidden),
            pl.BlockSpec((tokens, step), lambda i: (0, i)),
            *anywhere(others),
        ],
        out_specs=pl.BlockSpec((own, step), lambda i: (0, i)),
        out_shape=jax.ShapeDtypeStruct((own, width), kind),
        compiler_params=limits(56),
        cost_estimate=cost(2 * tokens * width * own, tokens * width * 2),
    )(context, hidden, cotangent, *others)


def dnormed_kernel(order_ref, a_ref, b_ref, as_ref, bs_ref, ag_ref, bg_ref, aq_ref, bq_ref, gu_ref, qkv_ref, *refs):
    if len(refs) == 2:
        far_refs, (out_ref, sums_ref) = (), refs
    else:
        keep_ref, got_ref, *far_refs, branch_ref, sums_ref, out_ref = refs
        branch_ref[...] = (keep_ref[...] + got_ref[...].astype(f32)).astype(bf16)
    step = pl.program_id(0)
    gateup = jnp.concatenate([ag_ref[...], bg_ref[...]], axis=0)
    fused = jnp.concatenate([aq_ref[...], bq_ref[...]], axis=0)

    @pl.when(step == 0)
    def _():
        sums_ref[...] = jnp.zeros_like(sums_ref)

    means = [ref[:, 0:1] for ref in (as_ref, bs_ref)]
    stds = [ref[:, 1:2] for ref in (as_ref, bs_ref)]
    width = gu_ref.shape[0]
    for at in range(0, width, CHUNK):
        cols = pl.ds(at, CHUNK)
        dnormed = mm(gateup, gu_ref[cols, :], ((1,), (1,))) + mm(fused, qkv_ref[cols, :], ((1,), (1,)))
        out_ref[:, cols] = dnormed.astype(out_ref.dtype)
        normal = jnp.concatenate(
            [(ref[0, :, cols].astype(f32) - mean) * std for ref, mean, std in zip((a_ref, b_ref), means, stds)], axis=0
        )
        sums_ref[0:1, cols] += jnp.sum(dnormed * normal, axis=0, keepdims=True)
        sums_ref[1:2, cols] += jnp.sum(dnormed, axis=0, keepdims=True)
    for i, far_ref in enumerate(far_refs):

        @pl.when(step == i)
        def _():
            far_ref[...] = out_ref[...]


def dnormed_share(order, *others, gathered, stats, dgateup, dfused, gu, qkv, far=()):
    width = gathered.shape[2]
    count = order.shape[0]
    step = 2 * LANES
    block = lambda k: pl.BlockSpec((1, LANES, width), lambda i, order: (order[2 * i + k], 0, 0))
    row = lambda x, k: pl.BlockSpec((LANES, x.shape[1]), lambda i, order: (order[2 * i + k], 0))
    if far:
        outs = [pl.BlockSpec((step, width), lambda i, order: (0, 0)) for _ in range(count // 2)]
        shapes = [jax.ShapeDtypeStruct((step, width), bf16) for _ in range(count // 2)]
        part = pl.BlockSpec((far[0].shape[0] // (count // 2), width), lambda i, order: (i, 0))
        outs.append(part)
        shapes.append(jax.ShapeDtypeStruct(far[0].shape, bf16))
    else:
        outs = [pl.BlockSpec((step, width), lambda i, order: (i, 0))]
        shapes = [jax.ShapeDtypeStruct((count * LANES, width), f32)]
    return pl.pallas_call(
        ignoring(dnormed_kernel, 11 + len(far), len(others)),
        name="dn_far" if far else "dn_near",
        grid_spec=pltpu.PrefetchScalarGridSpec(
            num_scalar_prefetch=1,
            grid=(count // 2,),
            in_specs=[
                block(0),
                block(1),
                row(stats, 0),
                row(stats, 1),
                row(dgateup, 0),
                row(dgateup, 1),
                row(dfused, 0),
                row(dfused, 1),
                whole_block(gu),
                whole_block(qkv),
                *[part for _ in far],
                *anywhere(others),
            ],
            out_specs=[*outs, pl.BlockSpec((8, width), lambda i, order: (0, 0))],
            scratch_shapes=[pltpu.VMEM((step, width), bf16)] if far else [],
        ),
        out_shape=[*shapes, jax.ShapeDtypeStruct((8, width), f32)],
        compiler_params=limits(60),
        cost_estimate=cost(
            2 * count * LANES * width * (dgateup.shape[1] + dfused.shape[1]), count * LANES * width * 8
        ),
    )(order, gathered, gathered, stats, stats, dgateup, dgateup, dfused, dfused, gu, qkv, *far, *others)


def combine_kernel(near_ref, *refs):
    got_refs, sent_refs, keep_ref = refs[: len(refs) - 1 - (len(refs) - 1) // 3], refs[-1 - (len(refs) - 1) // 3 : -1], refs[-1]
    for i, got_ref in enumerate(got_refs):

        @pl.when(pl.program_id(0) == i)
        def _():
            total = near_ref[...] + got_ref[...].astype(f32)
            if i < len(sent_refs):
                sent_refs[i][...] = total.astype(bf16)
            else:
                keep_ref[...] = total


def combine(near, got, *others):
    rows, width = near.shape
    step = rows // len(got)
    sent = len(got) // 2
    fixed = pl.BlockSpec((step, width), lambda i: (0, 0))
    return pl.pallas_call(
        ignoring(combine_kernel, 1 + len(got), len(others)),
        name="combine",
        grid=(len(got),),
        in_specs=[pl.BlockSpec((step, width), lambda i: (i, 0)), *[fixed for _ in got], *anywhere(others)],
        out_specs=[fixed for _ in range(sent)] + [pl.BlockSpec((step, width), lambda i: (jnp.maximum(i - sent, 0), 0))],
        out_shape=[jax.ShapeDtypeStruct((step, width), bf16) for _ in range(sent)]
        + [jax.ShapeDtypeStruct((rows // 2, width), f32)],
        compiler_params=limits(48),
        cost_estimate=cost(0, rows * width * 9),
    )(near, *got, *others)


def per_device(
    groups, outer, zs, ys, cs, tokens, segments, ln_gain, ln_bias, w_qkv, b_qkv, w_out, w_gateup, w_down, cotangent
):
    length, width = tokens.shape
    tp = zs * ys * cs
    shards = tp * outer
    z, y, c = (lax.axis_index(axis) for axis in TP)
    me = (z * ys + y) * cs + c

    own_ffn = w_gateup.shape[1] // 2 // tp
    wide = up_to(own_ffn, LANES)
    own_qkv = 3 * PAIR
    rows = w_qkv.shape[0]
    half = rows // groups
    part = lax.axis_index("replica")
    parts = part.astype(jnp.int32).reshape(1)
    steps = sorted(range(zs), key=lambda k: -min(k, zs - k))
    order = [
        jnp.stack(
            [
                (lax.rem(z + zs - k, zs) * ys + lax.rem(y + ys - j, ys)) * cs + lax.rem(c + cs - i, cs)
                for j in reversed(range(ys))
                for k in steps
            ]
        ).astype(jnp.int32)
        for i in range(cs)
    ]

    plain_order = [
        jnp.stack(
            [(k * ys + lax.rem(y + ys - j, ys)) * cs + lax.rem(c + cs - i, cs) for j in reversed(range(ys)) for k in range(zs)]
        ).astype(jnp.int32)
        for i in range(cs)
    ]

    small = jnp.concatenate([ln_gain, ln_bias, b_qkv, segments[0].astype(bf16)])
    of_params = 2 * rows + b_qkv.shape[0]
    small_rows = up_to(-(-small.shape[0] // width), 8)
    small_rows_of = jnp.pad(small, (0, small_rows * width - small.shape[0])).reshape(small_rows, width)
    packed = jnp.concatenate([tokens, small_rows_of], axis=0)
    gathered = lax.all_gather(packed, TP, axis=0, tiled=False)

    cotangent_all = lax.all_gather(cotangent, TP, axis=0, tiled=True)

    vectors = gathered[:, length:, :].reshape(tp, -1)[:, : small.shape[0]]
    seg_all = vectors[:, of_params:].astype(jnp.int32)
    vectors = vectors[:, :of_params]
    if outer > 1:
        vectors = lax.all_gather(vectors, "outer", axis=1, tiled=False)
    vectors = vectors.reshape(shards, -1)
    gain_all = vectors[:, :rows].reshape(1, width).astype(f32)
    bias_all = vectors[:, rows : 2 * rows].reshape(1, width).astype(f32)
    qkv_bias = vectors[:, 2 * rows :].reshape(3, tp, PAIR).astype(f32)
    my_bias = lax.dynamic_index_in_dim(qkv_bias, me, 1, keepdims=False).reshape(1, own_qkv)
    tables = rotary_tables(seg_all)

    def other(own):
        return shifted(own, "replica", groups, 1)

    def to_columns(own, *others):
        own = lax.all_to_all(own, TP, 0, 0, tiled=True)
        whole = jnp.zeros((tp, groups, half, own.shape[-1]), bf16)
        whole = lax.dynamic_update_slice(whole, own[:, None], (0, part, 0, 0))
        moved = other(own)
        if others:
            moved = after(moved, *others)
        whole = lax.dynamic_update_slice(whole, moved[:, None], (0, 1 - part, 0, 0))
        whole = whole.reshape(tp, rows, own.shape[-1])
        if outer > 1:
            whole = lax.all_gather(whole, "outer", axis=1, tiled=False)
        return whole.reshape(width, own.shape[-1])

    gu_cols = to_columns(pack(w_gateup, parts, groups, 2, tp, own_ffn, wide))
    qkv_cols = to_columns(pack(w_qkv, parts, groups, 3, tp, PAIR, PAIR), *tables)
    if outer > 1:
        w_out = lax.all_gather(w_out, "outer", axis=0, tiled=True)
        w_down = lax.all_gather(w_down, "outer", axis=0, tiled=True)
    w_rows = jnp.concatenate([w_out, w_down, jnp.zeros((wide - own_ffn, width), bf16)], axis=0)

    stats, normed, gate, up, hidden, joined = gate_forward(gathered, gain_all, bias_all, gu_cols, qkv_cols)
    fused, context, probs = attend(joined, my_bias, tables, tp)
    branch_far = branches(plain_order[1], context, hidden, w_rows)[0]
    branch_sent, branch_keep = branches(plain_order[0], context, hidden, w_rows, shifted(branch_far, "c", cs, 1))
    branch_got = shifted(branch_sent, "y", ys, 1)

    dgateup, dcontext = gate_backward(cotangent_all, gate, up, w_rows, branch_sent)

    def grads_of(d, *others):
        if outer == 1:
            return split_grads(parts, normed, d, half, *others)
        mine, theirs = of_replicas(mm(normed, d, ((0,), (0,))))
        return mine, theirs.astype(bf16)

    def of_replicas(grads):
        if outer > 1:
            grads = lax.psum_scatter(grads.reshape(tp, outer, rows, -1), "outer", scatter_dimension=1, tiled=True)
        grads = grads.reshape(tp, groups, half, -1)
        mine = lax.dynamic_index_in_dim(grads, part, 1, keepdims=False)
        return mine, lax.dynamic_index_in_dim(grads, 1 - part, 1, keepdims=False)

    gu_mine, gu_theirs = grads_of(dgateup)
    gu_got = other(gu_theirs)
    dfused, bias_sums = attend_back(fused, probs, dcontext, tables, tp, gu_theirs)
    share = functools.partial(dnormed_share, gathered=gathered, stats=stats, dgateup=dgateup, dfused=dfused, gu=gu_cols, qkv=qkv_cols)
    *far_shares, branch, far_sums = share(order[1], far=(branch_keep, branch_got))
    branch_own = lax.psum_scatter(branch, "z", scatter_dimension=0, tiled=True)
    tokens32 = tokens.astype(f32)
    block_output = (tokens32 + branch_own.astype(f32)).astype(bf16)
    got = [shifted(far_share, "c", cs, 1) for far_share in far_shares]
    near_share, near_sums = share(order[0], *far_shares)
    gain_sum, bias_sum = near_sums[0] + far_sums[0], near_sums[1] + far_sums[1]

    per_row = own_qkv // half
    tiled_sums = jnp.broadcast_to(bias_sums.reshape(1, half, per_row), (width // half, half, per_row)).reshape(width, per_row)
    extra = jnp.concatenate(
        [gain_sum[:, None], bias_sum[:, None], tiled_sums, jnp.zeros((width, LANES - 2 - per_row), f32)], axis=1
    )
    mine, theirs = of_replicas(extra)
    extra = jnp.concatenate([mine[..., :2], theirs[..., :2], mine[..., 2 : 2 + per_row]], axis=2)
    extra = jnp.pad(extra, ((0, 0), (0, 0), (own_ffn, 2 * wide - own_ffn - 4 - per_row)))
    *sent, keep = combine(near_share, got)
    gu_total = (gu_mine + after(gu_got, *sent).astype(f32) + extra).astype(bf16)
    gu_own = lax.all_to_all(gu_total, TP, 0, 0, tiled=True)
    qkv_mine, qkv_theirs = grads_of(dfused, gu_total)
    qkv_got = other(qkv_theirs)
    rows_part = rows_grads(context, hidden, cotangent_all, PAIR + own_ffn, bf16 if outer == 1 else f32, qkv_theirs)
    if outer > 1:
        rows_out = lax.psum_scatter(rows_part[:PAIR], "outer", scatter_dimension=0, tiled=True)
        rows_down = lax.psum_scatter(rows_part[PAIR:], "outer", scatter_dimension=0, tiled=True)
        rows_part = jnp.concatenate([rows_out, rows_down], axis=0).astype(bf16)
    rows_got = other(rows_part)
    dnormed_own = 0.0
    leaving = []
    for i, pair in enumerate(sent):
        pair = shifted(after(pair, *leaving, rows_part) if leaving else pair, "y", ys, 1)
        at = 2 * i * length
        for j, k in enumerate(steps[2 * i : 2 * i + 2]):
            rows_at = slice(j * length, (j + 1) * length)
            term = keep[at : at + 2 * length][rows_at] + pair[rows_at].astype(f32)
            if k:
                leaving.append(term.astype(bf16))
                term = shifted(leaving[-1], "z", zs, zs - k).astype(f32)
            dnormed_own = dnormed_own + term
    centered = tokens32 - jnp.mean(tokens32, axis=1, keepdims=True)
    inv = lax.rsqrt(jnp.mean(centered * centered, axis=1, keepdims=True) + epsilon)
    xhat = centered * inv
    e = dnormed_own * gain_all
    tokens_back = inv * (e - jnp.mean(e, axis=1, keepdims=True) - xhat * jnp.mean(e * xhat, axis=1, keepdims=True))
    tokens_grad = (cotangent.astype(f32) + tokens_back).astype(bf16)
    qkv_total = (qkv_mine + qkv_got.astype(f32)).astype(bf16)
    qkv_total = after(qkv_total, gu_own, branch_own)
    qkv_own = lax.all_to_all(qkv_total, TP, 0, 0, tiled=True)
    gu_other = other(gu_own)
    gateup_grad = unpack(gu_own, gu_other, parts, 2, own_ffn, wide)
    qkv_grad = unpack(qkv_own, other(qkv_own), parts, 3, PAIR, PAIR)
    rows_grad = rows_part.astype(f32) + rows_got.astype(f32)
    sums_of = lambda x: jnp.sum(x[:, :, own_ffn : own_ffn + 4].astype(f32), axis=0)
    mine, theirs = sums_of(gu_own), sums_of(gu_other)
    here, there = mine[:, :2] + theirs[:, 2:], theirs[:, :2] + mine[:, 2:]
    first = part == 0
    own_sums = jnp.concatenate([jnp.where(first, here, there), jnp.where(first, there, here)], axis=0)
    bias_of = lambda x: x[:, :, own_ffn + 4 : own_ffn + 4 + per_row].reshape(tp, 3, PAIR).astype(f32)
    bias_grads = bias_of(gu_own) + bias_of(gu_other)
    bias_grads = bias_grads.transpose(1, 0, 2).reshape(-1)
    place = me * outer + lax.axis_index("outer")
    qkv_bias_grad = lax.dynamic_slice_in_dim(bias_grads, place * (3 * rows), 3 * rows, 0)
    return (
        block_output,
        tokens_grad,
        own_sums[:, 0],
        own_sums[:, 1],
        qkv_grad,
        qkv_bias_grad,
        rows_grad[: PAIR // outer],
        gateup_grad,
        rows_grad[PAIR // outer :],
    )


def solution(mesh):
    groups, shards = mesh.shape["replica"], mesh.shape["shard"]
    tp = math.gcd(shards, HEADS // 2)
    outer = shards // tp
    ys = cs = 2
    zs = tp // (ys * cs)
    inner_mesh = Mesh(mesh.devices.reshape(groups, zs, ys, cs, outer), ("replica", *TP, "outer"))
    everywhere = P(("replica", *TP, "outer"), None)
    vector = P((*TP, "outer"))
    matrix = P((*TP, "outer"), None)
    return jax.shard_map(
        functools.partial(per_device, groups, outer, zs, ys, cs),
        mesh=inner_mesh,
        in_specs=(everywhere, everywhere, vector, vector, matrix, vector, matrix, matrix, matrix, everywhere),
        out_specs=(everywhere, everywhere, vector, vector, matrix, vector, matrix, matrix, matrix),
        check_vma=False,
    )
```

```python
import functools
import math

import jax
import jax.numpy as jnp
from jax import lax
from jax.experimental import pallas as pl
from jax.experimental.pallas import tpu as pltpu
from jax.sharding import Mesh, PartitionSpec as P

HEADS = 32
HEAD_DIM = 64
ROT = 16
PAIR = 2 * HEAD_DIM
TP = ("z", "y", "c")
LANES = 128
SEQUENCES = 8
CHUNK = 512

epsilon = 1e-05
rope_base = 10000.0
score_scale = 1.0 / math.sqrt(HEAD_DIM)

bf16 = jnp.bfloat16
f32 = jnp.float32


def up_to(size, step):
    return -(-size // step) * step


def mm(a, b, dims):
    return lax.dot_general(a, b, (dims, ((), ())), preferred_element_type=f32)


def rotary_tables(segments):
    count, length = segments.shape
    indices = jnp.arange(length, dtype=jnp.int32)
    same_doc = segments[:, :, None] == segments[:, None, :]
    doc_start = jnp.min(jnp.where(same_doc, indices[None, None, :], length), axis=2)
    in_doc = (indices[None, :] - doc_start).astype(f32).reshape(count * length, 1)
    allowed = same_doc & (indices[:, None] >= indices[None, :])[None]
    half_rot = ROT // 2
    lane = jnp.arange(PAIR, dtype=jnp.int32) % HEAD_DIM
    inverse = rope_base ** (-((lane % half_rot).astype(f32) * (2.0 / ROT)))
    angles = in_doc * inverse[None, :]
    cos, sin = jnp.cos(angles), jnp.sin(angles)
    turned = (lane < ROT)[None, :]
    low = (lane < half_rot)[None, :]
    own = jnp.where(turned, cos, 1.0)
    after = jnp.where(low, -sin, 0.0)
    before = jnp.where(turned & ~low, sin, 0.0)
    return own, after, before, jnp.where(allowed, 0.0, -1e30).astype(f32)


def turn(x, own, after, before):
    half = ROT // 2
    width = x.shape[-1]
    return x * own + pltpu.roll(x, width - half, 1) * after + pltpu.roll(x, half, 1) * before


def head_mask(rows):
    return lax.broadcasted_iota(jnp.int32, (rows, PAIR), 1) < HEAD_DIM


def both_heads(x, first):
    zero = jnp.zeros_like(x)
    return jnp.concatenate([jnp.where(first, x, zero), jnp.where(first, zero, x)], axis=0)


def attend_kernel(joined_ref, bias_ref, own_ref, after_ref, before_ref, mask_ref, fused_ref, context_ref, probs_ref):
    length = mask_ref.shape[1]
    first = head_mask(length)
    for n in range(mask_ref.shape[0]):
        rows = pl.ds(n * length, length)
        own, after, before = own_ref[rows, :], after_ref[rows, :], before_ref[rows, :]
        joined = joined_ref[rows, :] + bias_ref[...]
        q = turn(joined[:, :PAIR], own, after, before).astype(bf16)
        k = turn(joined[:, PAIR : 2 * PAIR], own, after, before).astype(bf16)
        v = joined[:, 2 * PAIR :].astype(bf16)
        mask = mask_ref[n]
        scores = mm(both_heads(q, first), k, ((1,), (1,))) * score_scale
        scores = scores + jnp.concatenate([mask, mask], axis=0)
        top = jnp.max(scores, axis=1, keepdims=True)
        exps = jnp.exp(scores - top)
        probs = exps / jnp.sum(exps, axis=1, keepdims=True)
        low = probs.astype(bf16)
        side = jnp.concatenate([low[:length], low[length:]], axis=1)
        context = mm(side, both_heads(v, first), ((1,), (0,)))
        fused_ref[rows, :PAIR] = q
        fused_ref[rows, PAIR : 2 * PAIR] = k
        fused_ref[rows, 2 * PAIR :] = v
        context_ref[rows, :] = context.astype(bf16)
        probs_ref[n] = probs


def attend_back_kernel(fused_ref, probs_ref, dcontext_ref, own_ref, after_ref, before_ref, dfused_ref, sums_ref):
    length = probs_ref.shape[2]
    first = head_mask(length)
    total = jnp.zeros(sums_ref.shape, f32)
    for n in range(probs_ref.shape[0]):
        rows = pl.ds(n * length, length)
        own, after, before = own_ref[rows, :], after_ref[rows, :], before_ref[rows, :]
        q = fused_ref[rows, :PAIR]
        k = fused_ref[rows, PAIR : 2 * PAIR]
        v = fused_ref[rows, 2 * PAIR :]
        probs = probs_ref[n]
        dc = both_heads(dcontext_ref[rows, :], first)
        dprobs = mm(dc, v, ((1,), (1,)))
        dscores = (probs * (dprobs - jnp.sum(dprobs * probs, axis=1, keepdims=True))).astype(bf16)
        dv = mm(probs.astype(bf16), dc, ((0,), (0,)))
        side = jnp.concatenate([dscores[:length], dscores[length:]], axis=1)
        dq = mm(side, both_heads(k, first), ((1,), (0,))) * score_scale
        dk = mm(dscores, both_heads(q, first), ((0,), (0,))) * score_scale
        out = jnp.concatenate(
            [turn(dq, own, -after, -before).astype(bf16), turn(dk, own, -after, -before).astype(bf16), dv.astype(bf16)],
            axis=1,
        )
        dfused_ref[rows, :] = out
        total = total + jnp.sum(out.astype(f32), axis=0, keepdims=True)

    @pl.when(pl.program_id(0) == 0)
    def _():
        sums_ref[...] = jnp.zeros_like(sums_ref)

    sums_ref[...] += total


def attend(joined, bias, tables, count):
    own, after, before, mask = tables
    tokens, width = joined.shape
    length = tokens // count
    many = math.gcd(count, SEQUENCES)
    row = lambda w: pl.BlockSpec((many * length, w), lambda i: (i, 0))
    return pl.pallas_call(
        attend_kernel,
        name="attend",
        grid=(count // many,),
        in_specs=[
            row(width),
            pl.BlockSpec((1, width), lambda i: (0, 0)),
            row(PAIR),
            row(PAIR),
            row(PAIR),
            pl.BlockSpec((many, length, length), lambda i: (i, 0, 0)),
        ],
        out_specs=[row(width), row(PAIR), pl.BlockSpec((many, 2 * length, length), lambda i: (i, 0, 0))],
        out_shape=[
            jax.ShapeDtypeStruct((tokens, width), bf16),
            jax.ShapeDtypeStruct((tokens, PAIR), bf16),
            jax.ShapeDtypeStruct((count, 2 * length, length), f32),
        ],
        compiler_params=pltpu.CompilerParams(vmem_limit_bytes=32 << 20),
        cost_estimate=pl.CostEstimate(flops=tokens * length * PAIR * 8, bytes_accessed=tokens * 6000, transcendentals=tokens * length * 2),
    )(joined, bias, own, after, before, mask)


def attend_back(fused, probs, dcontext, tables, count, *others):
    own, after, before, _ = tables
    tokens, width = fused.shape
    length = tokens // count
    many = math.gcd(count, SEQUENCES)
    row = lambda w: pl.BlockSpec((many * length, w), lambda i: (i, 0))
    return pl.pallas_call(
        ignoring(attend_back_kernel, 6, len(others)),
        name="attend_back",
        grid=(count // many,),
        in_specs=[
            row(width),
            pl.BlockSpec((many, 2 * length, length), lambda i: (i, 0, 0)),
            row(PAIR),
            row(PAIR),
            row(PAIR),
            row(PAIR),
            *anywhere(others),
        ],
        out_specs=[row(width), pl.BlockSpec((1, width), lambda i: (0, 0))],
        out_shape=[jax.ShapeDtypeStruct((tokens, width), bf16), jax.ShapeDtypeStruct((1, width), f32)],
        compiler_params=pltpu.CompilerParams(vmem_limit_bytes=60 << 20),
        cost_estimate=pl.CostEstimate(flops=tokens * length * PAIR * 16, bytes_accessed=tokens * 6000, transcendentals=0),
    )(fused, probs, dcontext, own, after, before, *others)


def shifted(x, axis, size, step):
    return lax.ppermute(x, axis, [(i, (i + step) % size) for i in range(size)])


def limits(mib):
    return pltpu.CompilerParams(vmem_limit_bytes=mib << 20)


def cost(flops, moved):
    return pl.CostEstimate(flops=1, bytes_accessed=1, transcendentals=0)


def whole_block(array):
    return pl.BlockSpec(array.shape, lambda *_: (0,) * array.ndim)


def pack_kernel(part_ref, own_ref, out_ref, *, sections, tp, size, wide):
    own = own_ref[...]
    rows = own.shape[0]
    for t in range(tp):
        pieces = []
        for section in range(sections):
            at = (section * tp + t) * size
            pieces.append(own[:, at : at + size])
            if wide > size:
                pieces.append(jnp.zeros((rows, wide - size), own.dtype))
        out_ref[t] = jnp.concatenate(pieces, axis=1) if len(pieces) > 1 else pieces[0]


def pack(weight, part, groups, sections, tp, size, wide):
    rows, width = weight.shape
    half = rows // groups
    step = min(half, 16)
    return pl.pallas_call(
        functools.partial(pack_kernel, sections=sections, tp=tp, size=size, wide=wide),
        name="pack",
        grid_spec=pltpu.PrefetchScalarGridSpec(
            num_scalar_prefetch=1,
            grid=(half // step,),
            in_specs=[pl.BlockSpec((step, width), lambda i, part: (part[0] * (half // step) + i, 0))],
            out_specs=pl.BlockSpec((tp, step, sections * wide), lambda i, part: (0, i, 0)),
        ),
        out_shape=jax.ShapeDtypeStruct((tp, half, sections * wide), weight.dtype),
        compiler_params=limits(32),
        cost_estimate=cost(0, 4 * half * width),
    )(part, weight)


def nothing(*refs):
    del refs


def anywhere(arrays):
    return [pl.BlockSpec(memory_space=pl.ANY) for _ in arrays]


def after(x, *others):
    return pl.pallas_call(
        nothing,
        name="after",
        in_specs=anywhere((x, *others)),
        out_specs=pl.BlockSpec(memory_space=pl.ANY),
        out_shape=jax.ShapeDtypeStruct(x.shape, x.dtype),
        input_output_aliases={0: 0},
    )(x, *others)


def ignoring(kernel, at, count):
    return lambda *refs: kernel(*refs[:at], *refs[at + count :])


def unpack_kernel(part_ref, own_ref, other_ref, out_ref, *, sections, tp, size, wide):
    got = jnp.where(pl.program_id(0) == 0, own_ref[...], other_ref[...])
    for section in range(sections):
        pieces = [got[t, :, section * wide : section * wide + size] for t in range(tp)]
        out_ref[:, section * tp * size : (section + 1) * tp * size] = jnp.concatenate(pieces, axis=1).astype(f32)


def unpack(own, other, part, sections, size, wide):
    tp, half, width = own.shape
    step = min(half, 16)
    count = half // step
    return pl.pallas_call(
        functools.partial(unpack_kernel, sections=sections, tp=tp, size=size, wide=wide),
        name="unpack",
        grid_spec=pltpu.PrefetchScalarGridSpec(
            num_scalar_prefetch=1,
            grid=(2, count),
            in_specs=[
                pl.BlockSpec((tp, step, width), lambda i, j, part: (0, jnp.where(i == 0, j, count - 1), 0)),
                pl.BlockSpec((tp, step, width), lambda i, j, part: (0, jnp.where(i == 0, 0, j), 0)),
            ],
            out_specs=pl.BlockSpec(
                (step, sections * tp * size), lambda i, j, part: (lax.rem(part[0] + i, 2) * count + j, 0)
            ),
        ),
        out_shape=jax.ShapeDtypeStruct((2 * half, sections * tp * size), f32),
        compiler_params=limits(48),
        cost_estimate=cost(0, 12 * half * width * tp),
    )(part, own, other)


def gate_kernel(
    a_ref, b_ref, gain_ref, bias_ref, gu_ref, qkv_ref, stats_ref, normed_ref, gate_ref, up_ref, hidden_ref, joined_ref
):
    x = jnp.concatenate([a_ref[0], b_ref[0]], axis=0).astype(f32)
    mean = jnp.mean(x, axis=1, keepdims=True)
    centered = x - mean
    inv_std = lax.rsqrt(jnp.mean(centered * centered, axis=1, keepdims=True) + epsilon)
    lane = lax.broadcasted_iota(jnp.int32, stats_ref.shape, 1)
    stats_ref[...] = jnp.where(lane == 0, mean, inv_std)
    normed = (centered * inv_std * gain_ref[...] + bias_ref[...]).astype(bf16)
    normed_ref[...] = normed
    wide = gate_ref.shape[1]
    gateup = mm(normed, gu_ref[...], ((1,), (0,)))
    gate, up = gateup[:, :wide], gateup[:, wide:]
    gate_ref[...] = gate
    up_ref[...] = up
    hidden_ref[...] = (gate * jax.nn.sigmoid(gate) * up).astype(bf16)
    joined_ref[...] = mm(normed, qkv_ref[...], ((1,), (0,)))


def gate_forward(gathered, gain, bias, gu, qkv):
    count, padded, width = gathered.shape
    length, wide = LANES, gu.shape[1] // 2
    tokens = count * length
    block = lambda k: pl.BlockSpec((1, length, width), lambda i: (2 * i + k, 0, 0))
    row = lambda w: pl.BlockSpec((2 * length, w), lambda i: (i, 0))
    return pl.pallas_call(
        gate_kernel,
        name="gate_fwd",
        grid=(count // 2,),
        in_specs=[
            block(0),
            block(1),
            whole_block(gain),
            whole_block(bias),
            whole_block(gu),
            whole_block(qkv),
        ],
        out_specs=[row(LANES), row(width), row(wide), row(wide), row(wide), row(3 * PAIR)],
        out_shape=[
            jax.ShapeDtypeStruct((tokens, LANES), f32),
            jax.ShapeDtypeStruct((tokens, width), bf16),
            jax.ShapeDtypeStruct((tokens, wide), f32),
            jax.ShapeDtypeStruct((tokens, wide), f32),
            jax.ShapeDtypeStruct((tokens, wide), bf16),
            jax.ShapeDtypeStruct((tokens, 3 * PAIR), f32),
        ],
        compiler_params=limits(56),
        cost_estimate=cost(2 * tokens * width * (2 * wide + 3 * PAIR), tokens * (4 * width + 10 * wide + 12 * PAIR)),
    )(gathered, gathered, gain, bias, gu, qkv)


def branch_kernel(far, order_ref, ac_ref, bc_ref, ah_ref, bh_ref, w_ref, *refs):
    context = jnp.concatenate([ac_ref[...], bc_ref[...]], axis=0)
    hidden = jnp.concatenate([ah_ref[...], bh_ref[...]], axis=0)
    total = mm(context, w_ref[:PAIR, :], ((1,), (0,))) + mm(hidden, w_ref[PAIR:, :], ((1,), (0,)))
    if far:
        refs[0][...] = total.astype(bf16)
        return
    got_ref, sent_ref, keep_ref = refs
    keep_ref[...] = total + got_ref[...].astype(f32)

    @pl.when(pl.program_id(0) < pl.num_programs(0) // 2)
    def _():
        sent_ref[...] = keep_ref[...].astype(bf16)


def branches(order, context, hidden, w, got=None):
    tokens, wide = hidden.shape
    width = w.shape[1]
    count = order.shape[0]
    step = 2 * LANES
    row = lambda x, k: pl.BlockSpec((LANES, x.shape[1]), lambda i, order: (order[2 * i + k], 0))
    plain = pl.BlockSpec((step, width), lambda i, order: (i, 0))
    if got is None:
        out_specs = [plain]
        out_shape = [jax.ShapeDtypeStruct((count * LANES, width), bf16)]
        more = []
    else:
        sent = count // 4
        out_specs = [
            pl.BlockSpec((step, width), lambda i, order: (jnp.minimum(i, sent - 1), 0)),
            pl.BlockSpec((step, width), lambda i, order: (jnp.maximum(i - sent, 0), 0)),
        ]
        out_shape = [jax.ShapeDtypeStruct((count * LANES // 2, width), kind) for kind in (bf16, f32)]
        more = [got]
    return pl.pallas_call(
        functools.partial(branch_kernel, got is None),
        name="branch_far" if got is None else "branch_near",
        grid_spec=pltpu.PrefetchScalarGridSpec(
            num_scalar_prefetch=1,
            grid=(count // 2,),
            in_specs=[
                row(context, 0),
                row(context, 1),
                row(hidden, 0),
                row(hidden, 1),
                whole_block(w),
                *[plain for _ in more],
            ],
            out_specs=out_specs,
        ),
        out_shape=out_shape,
        compiler_params=limits(48),
        cost_estimate=cost(2 * tokens * width * (PAIR + wide), 2 * tokens * (width + PAIR + wide)),
    )(order, context, context, hidden, hidden, w, *more)


def gate_back_kernel(cotangent_ref, gate_ref, up_ref, w_ref, dgateup_ref, dcontext_ref):
    dinner = mm(cotangent_ref[...], w_ref[...], ((1,), (1,)))
    dcontext_ref[...] = dinner[:, :PAIR].astype(bf16)
    dhidden = dinner[:, PAIR:]
    gate, up = gate_ref[...], up_ref[...]
    s = jax.nn.sigmoid(gate)
    wide = gate.shape[1]
    dgateup_ref[:, :wide] = (dhidden * up * s * (1.0 + gate * (1.0 - s))).astype(bf16)
    dgateup_ref[:, wide:] = (dhidden * gate * s).astype(bf16)


def gate_backward(cotangent, gate, up, w, *others):
    tokens, wide = gate.shape
    width = w.shape[1]
    row = lambda w: pl.BlockSpec((2 * LANES, w), lambda i: (i, 0))
    return pl.pallas_call(
        ignoring(gate_back_kernel, 4, len(others)),
        name="gate_back",
        grid=(tokens // (2 * LANES),),
        in_specs=[row(width), row(wide), row(wide), whole_block(w), *anywhere(others)],
        out_specs=[row(2 * wide), row(PAIR)],
        out_shape=[jax.ShapeDtypeStruct((tokens, 2 * wide), bf16), jax.ShapeDtypeStruct((tokens, PAIR), bf16)],
        compiler_params=limits(48),
        cost_estimate=cost(2 * tokens * width * (PAIR + wide), tokens * (2 * width + 12 * wide)),
    )(cotangent, gate, up, w, *others)


def grads_kernel(part_ref, normed_ref, d_ref, mine_ref, theirs_ref):
    grads = mm(normed_ref[...], d_ref[...], ((0,), (0,)))
    count, half, _ = mine_ref.shape
    first = part_ref[0] == 0
    for t in range(count):
        low = grads[2 * t * half : (2 * t + 1) * half]
        high = grads[(2 * t + 1) * half : (2 * t + 2) * half]
        mine_ref[t] = jnp.where(first, low, high)
        theirs_ref[t] = jnp.where(first, high, low).astype(bf16)


def split_grads(part, normed, d, half, *others):
    tokens, width = normed.shape
    step = 4 * LANES
    out = d.shape[1]
    blocks = step // (2 * half)
    piece = lambda: pl.BlockSpec((blocks, half, out), lambda i, part: (i, 0, 0))
    return pl.pallas_call(
        ignoring(grads_kernel, 3, len(others)),
        name="grads",
        grid_spec=pltpu.PrefetchScalarGridSpec(
            num_scalar_prefetch=1,
            grid=(width // step,),
            in_specs=[pl.BlockSpec((tokens, step), lambda i, part: (0, i)), whole_block(d)]
            + anywhere(others),
            out_specs=[piece(), piece()],
        ),
        out_shape=[
            jax.ShapeDtypeStruct((width // (2 * half), half, out), f32),
            jax.ShapeDtypeStruct((width // (2 * half), half, out), bf16),
        ],
        compiler_params=limits(56),
        cost_estimate=cost(2 * tokens * width * d.shape[1], 2 * tokens * (width + d.shape[1]) + 3 * width * out),
    )(part, normed, d, *others)


def rows_kernel(context_ref, hidden_ref, cotangent_ref, out_ref):
    cotangent = cotangent_ref[...]
    out_ref[:PAIR, :] = mm(context_ref[...], cotangent, ((0,), (0,))).astype(out_ref.dtype)
    hidden = mm(hidden_ref[...], cotangent, ((0,), (0,)))
    out_ref[PAIR:, :] = hidden[: out_ref.shape[0] - PAIR].astype(out_ref.dtype)


def rows_grads(context, hidden, cotangent, own, kind, *others):
    tokens, width = cotangent.shape
    step = 4 * LANES
    return pl.pallas_call(
        ignoring(rows_kernel, 3, len(others)),
        name="rows",
        grid=(width // step,),
        in_specs=[
            whole_block(context),
            whole_block(hidden),
            pl.BlockSpec((tokens, step), lambda i: (0, i)),
            *anywhere(others),
        ],
        out_specs=pl.BlockSpec((own, step), lambda i: (0, i)),
        out_shape=jax.ShapeDtypeStruct((own, width), kind),
        compiler_params=limits(56),
        cost_estimate=cost(2 * tokens * width * own, tokens * width * 2),
    )(context, hidden, cotangent, *others)


def dnormed_kernel(order_ref, a_ref, b_ref, as_ref, bs_ref, ag_ref, bg_ref, aq_ref, bq_ref, gu_ref, qkv_ref, *refs):
    if len(refs) == 2:
        far_refs, (out_ref, sums_ref) = (), refs
    else:
        keep_ref, got_ref, *far_refs, branch_ref, sums_ref, out_ref = refs
        branch_ref[...] = (keep_ref[...] + got_ref[...].astype(f32)).astype(bf16)
    step = pl.program_id(0)
    gateup = jnp.concatenate([ag_ref[...], bg_ref[...]], axis=0)
    fused = jnp.concatenate([aq_ref[...], bq_ref[...]], axis=0)

    @pl.when(step == 0)
    def _():
        sums_ref[...] = jnp.zeros_like(sums_ref)

    means = [ref[:, 0:1] for ref in (as_ref, bs_ref)]
    stds = [ref[:, 1:2] for ref in (as_ref, bs_ref)]
    width = gu_ref.shape[0]
    for at in range(0, width, CHUNK):
        cols = pl.ds(at, CHUNK)
        dnormed = mm(gateup, gu_ref[cols, :], ((1,), (1,))) + mm(fused, qkv_ref[cols, :], ((1,), (1,)))
        out_ref[:, cols] = dnormed.astype(out_ref.dtype)
        normal = jnp.concatenate(
            [(ref[0, :, cols].astype(f32) - mean) * std for ref, mean, std in zip((a_ref, b_ref), means, stds)], axis=0
        )
        sums_ref[0:1, cols] += jnp.sum(dnormed * normal, axis=0, keepdims=True)
        sums_ref[1:2, cols] += jnp.sum(dnormed, axis=0, keepdims=True)
    for i, far_ref in enumerate(far_refs):

        @pl.when(step == i)
        def _():
            far_ref[...] = out_ref[...]


def dnormed_share(order, *others, gathered, stats, dgateup, dfused, gu, qkv, far=()):
    width = gathered.shape[2]
    count = order.shape[0]
    step = 2 * LANES
    block = lambda k: pl.BlockSpec((1, LANES, width), lambda i, order: (order[2 * i + k], 0, 0))
    row = lambda x, k: pl.BlockSpec((LANES, x.shape[1]), lambda i, order: (order[2 * i + k], 0))
    if far:
        outs = [pl.BlockSpec((step, width), lambda i, order: (0, 0)) for _ in range(count // 2)]
        shapes = [jax.ShapeDtypeStruct((step, width), bf16) for _ in range(count // 2)]
        part = pl.BlockSpec((far[0].shape[0] // (count // 2), width), lambda i, order: (i, 0))
        outs.append(part)
        shapes.append(jax.ShapeDtypeStruct(far[0].shape, bf16))
    else:
        outs = [pl.BlockSpec((step, width), lambda i, order: (i, 0))]
        shapes = [jax.ShapeDtypeStruct((count * LANES, width), f32)]
    return pl.pallas_call(
        ignoring(dnormed_kernel, 11 + len(far), len(others)),
        name="dn_far" if far else "dn_near",
        grid_spec=pltpu.PrefetchScalarGridSpec(
            num_scalar_prefetch=1,
            grid=(count // 2,),
            in_specs=[
                block(0),
                block(1),
                row(stats, 0),
                row(stats, 1),
                row(dgateup, 0),
                row(dgateup, 1),
                row(dfused, 0),
                row(dfused, 1),
                whole_block(gu),
                whole_block(qkv),
                *[part for _ in far],
                *anywhere(others),
            ],
            out_specs=[*outs, pl.BlockSpec((8, width), lambda i, order: (0, 0))],
            scratch_shapes=[pltpu.VMEM((step, width), bf16)] if far else [],
        ),
        out_shape=[*shapes, jax.ShapeDtypeStruct((8, width), f32)],
        compiler_params=limits(60),
        cost_estimate=cost(
            2 * count * LANES * width * (dgateup.shape[1] + dfused.shape[1]), count * LANES * width * 8
        ),
    )(order, gathered, gathered, stats, stats, dgateup, dgateup, dfused, dfused, gu, qkv, *far, *others)


def combine_kernel(near_ref, *refs):
    got_refs, sent_refs, keep_ref = refs[: len(refs) - 1 - (len(refs) - 1) // 3], refs[-1 - (len(refs) - 1) // 3 : -1], refs[-1]
    for i, got_ref in enumerate(got_refs):

        @pl.when(pl.program_id(0) == i)
        def _():
            total = near_ref[...] + got_ref[...].astype(f32)
            if i < len(sent_refs):
                sent_refs[i][...] = total.astype(bf16)
            else:
                keep_ref[...] = total


def combine(near, got, *others):
    rows, width = near.shape
    step = rows // len(got)
    sent = len(got) // 2
    fixed = pl.BlockSpec((step, width), lambda i: (0, 0))
    return pl.pallas_call(
        ignoring(combine_kernel, 1 + len(got), len(others)),
        name="combine",
        grid=(len(got),),
        in_specs=[pl.BlockSpec((step, width), lambda i: (i, 0)), *[fixed for _ in got], *anywhere(others)],
        out_specs=[fixed for _ in range(sent)] + [pl.BlockSpec((step, width), lambda i: (jnp.maximum(i - sent, 0), 0))],
        out_shape=[jax.ShapeDtypeStruct((step, width), bf16) for _ in range(sent)]
        + [jax.ShapeDtypeStruct((rows // 2, width), f32)],
        compiler_params=limits(48),
        cost_estimate=cost(0, rows * width * 9),
    )(near, *got, *others)


def per_device(
    groups, outer, zs, ys, cs, tokens, segments, ln_gain, ln_bias, w_qkv, b_qkv, w_out, w_gateup, w_down, cotangent
):
    length, width = tokens.shape
    tp = zs * ys * cs
    shards = tp * outer
    z, y, c = (lax.axis_index(axis) for axis in TP)
    me = (z * ys + y) * cs + c

    own_ffn = w_gateup.shape[1] // 2 // tp
    wide = up_to(own_ffn, LANES)
    own_qkv = 3 * PAIR
    rows = w_qkv.shape[0]
    half = rows // groups
    part = lax.axis_index("replica")
    parts = part.astype(jnp.int32).reshape(1)
    steps = sorted(range(zs), key=lambda k: -min(k, zs - k))
    order = [
        jnp.stack(
            [
                (lax.rem(z + zs - k, zs) * ys + lax.rem(y + ys - j, ys)) * cs + lax.rem(c + cs - i, cs)
                for j in reversed(range(ys))
                for k in steps
            ]
        ).astype(jnp.int32)
        for i in range(cs)
    ]

    plain_order = [
        jnp.stack(
            [(k * ys + lax.rem(y + ys - j, ys)) * cs + lax.rem(c + cs - i, cs) for j in reversed(range(ys)) for k in range(zs)]
        ).astype(jnp.int32)
        for i in range(cs)
    ]

    small = jnp.concatenate([ln_gain, ln_bias, b_qkv, segments[0].astype(bf16)])
    of_params = 2 * rows + b_qkv.shape[0]
    small_rows = up_to(-(-small.shape[0] // width), 8)
    small_rows_of = jnp.pad(small, (0, small_rows * width - small.shape[0])).reshape(small_rows, width)
    packed = jnp.concatenate([tokens, small_rows_of], axis=0)
    gathered = lax.all_gather(packed, TP, axis=0, tiled=False)

    cotangent_all = lax.all_gather(cotangent, TP, axis=0, tiled=True)

    vectors = gathered[:, length:, :].reshape(tp, -1)[:, : small.shape[0]]
    seg_all = vectors[:, of_params:].astype(jnp.int32)
    vectors = vectors[:, :of_params]
    if outer > 1:
        vectors = lax.all_gather(vectors, "outer", axis=1, tiled=False)
    vectors = vectors.reshape(shards, -1)
    gain_all = vectors[:, :rows].reshape(1, width).astype(f32)
    bias_all = vectors[:, rows : 2 * rows].reshape(1, width).astype(f32)
    qkv_bias = vectors[:, 2 * rows :].reshape(3, tp, PAIR).astype(f32)
    my_bias = lax.dynamic_index_in_dim(qkv_bias, me, 1, keepdims=False).reshape(1, own_qkv)
    tables = rotary_tables(seg_all)

    def other(own):
        return shifted(own, "replica", groups, 1)

    def to_columns(own, *others):
        own = lax.all_to_all(own, TP, 0, 0, tiled=True)
        whole = jnp.zeros((tp, groups, half, own.shape[-1]), bf16)
        whole = lax.dynamic_update_slice(whole, own[:, None], (0, part, 0, 0))
        moved = other(own)
        if others:
            moved = after(moved, *others)
        whole = lax.dynamic_update_slice(whole, moved[:, None], (0, 1 - part, 0, 0))
        whole = whole.reshape(tp, rows, own.shape[-1])
        if outer > 1:
            whole = lax.all_gather(whole, "outer", axis=1, tiled=False)
        return whole.reshape(width, own.shape[-1])

    gu_cols = to_columns(pack(w_gateup, parts, groups, 2, tp, own_ffn, wide))
    qkv_cols = to_columns(pack(w_qkv, parts, groups, 3, tp, PAIR, PAIR), *tables)
    if outer > 1:
        w_out = lax.all_gather(w_out, "outer", axis=0, tiled=True)
        w_down = lax.all_gather(w_down, "outer", axis=0, tiled=True)
    w_rows = jnp.concatenate([w_out, w_down, jnp.zeros((wide - own_ffn, width), bf16)], axis=0)

    stats, normed, gate, up, hidden, joined = gate_forward(gathered, gain_all, bias_all, gu_cols, qkv_cols)
    fused, context, probs = attend(joined, my_bias, tables, tp)
    branch_far = branches(plain_order[1], context, hidden, w_rows)[0]
    branch_sent, branch_keep = branches(plain_order[0], context, hidden, w_rows, shifted(branch_far, "c", cs, 1))
    branch_got = shifted(branch_sent, "y", ys, 1)

    dgateup, dcontext = gate_backward(cotangent_all, gate, up, w_rows, branch_sent)

    def grads_of(d, *others):
        if outer == 1:
            return split_grads(parts, normed, d, half, *others)
        mine, theirs = of_replicas(mm(normed, d, ((0,), (0,))))
        return mine, theirs.astype(bf16)

    def of_replicas(grads):
        if outer > 1:
            grads = lax.psum_scatter(grads.reshape(tp, outer, rows, -1), "outer", scatter_dimension=1, tiled=True)
        grads = grads.reshape(tp, groups, half, -1)
        mine = lax.dynamic_index_in_dim(grads, part, 1, keepdims=False)
        return mine, lax.dynamic_index_in_dim(grads, 1 - part, 1, keepdims=False)

    gu_mine, gu_theirs = grads_of(dgateup)
    gu_got = other(gu_theirs)
    dfused, bias_sums = attend_back(fused, probs, dcontext, tables, tp, gu_theirs)
    share = functools.partial(dnormed_share, gathered=gathered, stats=stats, dgateup=dgateup, dfused=dfused, gu=gu_cols, qkv=qkv_cols)
    *far_shares, branch, far_sums = share(order[1], far=(branch_keep, branch_got))
    branch_own = lax.psum_scatter(branch, "z", scatter_dimension=0, tiled=True)
    tokens32 = tokens.astype(f32)
    block_output = (tokens32 + branch_own.astype(f32)).astype(bf16)
    got = [shifted(far_share, "c", cs, 1) for far_share in far_shares]
    near_share, near_sums = share(order[0], *far_shares)
    gain_sum, bias_sum = near_sums[0] + far_sums[0], near_sums[1] + far_sums[1]

    per_row = own_qkv // half
    tiled_sums = jnp.broadcast_to(bias_sums.reshape(1, half, per_row), (width // half, half, per_row)).reshape(width, per_row)
    extra = jnp.concatenate(
        [gain_sum[:, None], bias_sum[:, None], tiled_sums, jnp.zeros((width, LANES - 2 - per_row), f32)], axis=1
    )
    mine, theirs = of_replicas(extra)
    extra = jnp.concatenate([mine[..., :2], theirs[..., :2], mine[..., 2 : 2 + per_row]], axis=2)
    extra = jnp.pad(extra, ((0, 0), (0, 0), (own_ffn, 2 * wide - own_ffn - 4 - per_row)))
    *sent, keep = combine(near_share, got)
    gu_total = (gu_mine + after(gu_got, *sent).astype(f32) + extra).astype(bf16)
    gu_own = lax.all_to_all(gu_total, TP, 0, 0, tiled=True)
    qkv_mine, qkv_theirs = grads_of(dfused, gu_total)
    qkv_got = other(qkv_theirs)
    rows_part = rows_grads(context, hidden, cotangent_all, PAIR + own_ffn, bf16 if outer == 1 else f32, qkv_theirs)
    if outer > 1:
        rows_out = lax.psum_scatter(rows_part[:PAIR], "outer", scatter_dimension=0, tiled=True)
        rows_down = lax.psum_scatter(rows_part[PAIR:], "outer", scatter_dimension=0, tiled=True)
        rows_part = jnp.concatenate([rows_out, rows_down], axis=0).astype(bf16)
    rows_got = other(rows_part)
    dnormed_own = 0.0
    leaving = []
    for i, pair in enumerate(sent):
        pair = shifted(after(pair, *leaving, rows_part) if leaving else pair, "y", ys, 1)
        at = 2 * i * length
        for j, k in enumerate(steps[2 * i : 2 * i + 2]):
            rows_at = slice(j * length, (j + 1) * length)
            term = keep[at : at + 2 * length][rows_at] + pair[rows_at].astype(f32)
            if k:
                leaving.append(term.astype(bf16))
                term = shifted(leaving[-1], "z", zs, zs - k).astype(f32)
            dnormed_own = dnormed_own + term
    centered = tokens32 - jnp.mean(tokens32, axis=1, keepdims=True)
    inv = lax.rsqrt(jnp.mean(centered * centered, axis=1, keepdims=True) + epsilon)
    xhat = centered * inv
    e = dnormed_own * gain_all
    tokens_back = inv * (e - jnp.mean(e, axis=1, keepdims=True) - xhat * jnp.mean(e * xhat, axis=1, keepdims=True))
    tokens_grad = (cotangent.astype(f32) + tokens_back).astype(bf16)
    qkv_total = (qkv_mine + qkv_got.astype(f32)).astype(bf16)
    qkv_total = after(qkv_total, gu_own, branch_own)
    qkv_own = lax.all_to_all(qkv_total, TP, 0, 0, tiled=True)
    gu_other = other(gu_own)
    gateup_grad = unpack(gu_own, gu_other, parts, 2, own_ffn, wide)
    qkv_grad = unpack(qkv_own, other(qkv_own), parts, 3, PAIR, PAIR)
    rows_grad = rows_part.astype(f32) + rows_got.astype(f32)
    sums_of = lambda x: jnp.sum(x[:, :, own_ffn : own_ffn + 4].astype(f32), axis=0)
    mine, theirs = sums_of(gu_own), sums_of(gu_other)
    here, there = mine[:, :2] + theirs[:, 2:], theirs[:, :2] + mine[:, 2:]
    first = part == 0
    own_sums = jnp.concatenate([jnp.where(first, here, there), jnp.where(first, there, here)], axis=0)
    bias_of = lambda x: x[:, :, own_ffn + 4 : own_ffn + 4 + per_row].reshape(tp, 3, PAIR).astype(f32)
    bias_grads = bias_of(gu_own) + bias_of(gu_other)
    bias_grads = bias_grads.transpose(1, 0, 2).reshape(-1)
    place = me * outer + lax.axis_index("outer")
    qkv_bias_grad = lax.dynamic_slice_in_dim(bias_grads, place * (3 * rows), 3 * rows, 0)
    return (
        block_output,
        tokens_grad,
        own_sums[:, 0],
        own_sums[:, 1],
        qkv_grad,
        qkv_bias_grad,
        rows_grad[: PAIR // outer],
        gateup_grad,
        rows_grad[PAIR // outer :],
    )


def solution(mesh):
    groups, shards = mesh.shape["replica"], mesh.shape["shard"]
    tp = math.gcd(shards, HEADS // 2)
    outer = shards // tp
    ys = cs = 2
    zs = tp // (ys * cs)
    inner_mesh = Mesh(mesh.devices.reshape(groups, zs, ys, cs, outer), ("replica", *TP, "outer"))
    everywhere = P(("replica", *TP, "outer"), None)
    vector = P((*TP, "outer"))
    matrix = P((*TP, "outer"), None)
    return jax.shard_map(
        functools.partial(per_device, groups, outer, zs, ys, cs),
        mesh=inner_mesh,
        in_specs=(everywhere, everywhere, vector, vector, matrix, vector, matrix, matrix, matrix, everywhere),
        out_specs=(everywhere, everywhere, vector, vector, matrix, vector, matrix, matrix, matrix),
        check_vma=False,
    )
```

```python
import functools
import math

import jax
import jax.numpy as jnp
from jax import lax
from jax.experimental import pallas as pl
from jax.experimental.pallas import tpu as pltpu
from jax.sharding import Mesh, PartitionSpec as P

HEADS = 32
HEAD_DIM = 64
ROT = 16
PAIR = 2 * HEAD_DIM
TP = ("z", "y", "c")
LANES = 128
SEQUENCES = 8
CHUNK = 512

epsilon = 1e-05
rope_base = 10000.0
score_scale = 1.0 / math.sqrt(HEAD_DIM)

bf16 = jnp.bfloat16
f32 = jnp.float32


def up_to(size, step):
    return -(-size // step) * step


def mm(a, b, dims):
    return lax.dot_general(a, b, (dims, ((), ())), preferred_element_type=f32)


def rotary_tables(segments):
    count, length = segments.shape
    indices = jnp.arange(length, dtype=jnp.int32)
    same_doc = segments[:, :, None] == segments[:, None, :]
    doc_start = jnp.min(jnp.where(same_doc, indices[None, None, :], length), axis=2)
    in_doc = (indices[None, :] - doc_start).astype(f32).reshape(count * length, 1)
    allowed = same_doc & (indices[:, None] >= indices[None, :])[None]
    half_rot = ROT // 2
    lane = jnp.arange(PAIR, dtype=jnp.int32) % HEAD_DIM
    inverse = rope_base ** (-((lane % half_rot).astype(f32) * (2.0 / ROT)))
    angles = in_doc * inverse[None, :]
    cos, sin = jnp.cos(angles), jnp.sin(angles)
    turned = (lane < ROT)[None, :]
    low = (lane < half_rot)[None, :]
    own = jnp.where(turned, cos, 1.0)
    after = jnp.where(low, -sin, 0.0)
    before = jnp.where(turned & ~low, sin, 0.0)
    return own, after, before, jnp.where(allowed, 0.0, -1e30).astype(f32)


def turn(x, own, after, before):
    half = ROT // 2
    width = x.shape[-1]
    return x * own + pltpu.roll(x, width - half, 1) * after + pltpu.roll(x, half, 1) * before


def head_mask(rows):
    return lax.broadcasted_iota(jnp.int32, (rows, PAIR), 1) < HEAD_DIM


def both_heads(x, first):
    zero = jnp.zeros_like(x)
    return jnp.concatenate([jnp.where(first, x, zero), jnp.where(first, zero, x)], axis=0)


def attend_kernel(joined_ref, bias_ref, own_ref, after_ref, before_ref, mask_ref, fused_ref, context_ref, probs_ref):
    length = mask_ref.shape[1]
    first = head_mask(length)
    for n in range(mask_ref.shape[0]):
        rows = pl.ds(n * length, length)
        own, after, before = own_ref[rows, :], after_ref[rows, :], before_ref[rows, :]
        joined = joined_ref[rows, :] + bias_ref[...]
        q = turn(joined[:, :PAIR], own, after, before).astype(bf16)
        k = turn(joined[:, PAIR : 2 * PAIR], own, after, before).astype(bf16)
        v = joined[:, 2 * PAIR :].astype(bf16)
        mask = mask_ref[n]
        scores = mm(both_heads(q, first), k, ((1,), (1,))) * score_scale
        scores = scores + jnp.concatenate([mask, mask], axis=0)
        top = jnp.max(scores, axis=1, keepdims=True)
        exps = jnp.exp(scores - top)
        probs = exps / jnp.sum(exps, axis=1, keepdims=True)
        low = probs.astype(bf16)
        side = jnp.concatenate([low[:length], low[length:]], axis=1)
        context = mm(side, both_heads(v, first), ((1,), (0,)))
        fused_ref[rows, :PAIR] = q
        fused_ref[rows, PAIR : 2 * PAIR] = k
        fused_ref[rows, 2 * PAIR :] = v
        context_ref[rows, :] = context.astype(bf16)
        probs_ref[n] = probs


def attend_back_kernel(fused_ref, probs_ref, dcontext_ref, own_ref, after_ref, before_ref, dfused_ref, sums_ref):
    length = probs_ref.shape[2]
    first = head_mask(length)
    total = jnp.zeros(sums_ref.shape, f32)
    for n in range(probs_ref.shape[0]):
        rows = pl.ds(n * length, length)
        own, after, before = own_ref[rows, :], after_ref[rows, :], before_ref[rows, :]
        q = fused_ref[rows, :PAIR]
        k = fused_ref[rows, PAIR : 2 * PAIR]
        v = fused_ref[rows, 2 * PAIR :]
        probs = probs_ref[n]
        dc = both_heads(dcontext_ref[rows, :], first)
        dprobs = mm(dc, v, ((1,), (1,)))
        dscores = (probs * (dprobs - jnp.sum(dprobs * probs, axis=1, keepdims=True))).astype(bf16)
        dv = mm(probs.astype(bf16), dc, ((0,), (0,)))
        side = jnp.concatenate([dscores[:length], dscores[length:]], axis=1)
        dq = mm(side, both_heads(k, first), ((1,), (0,))) * score_scale
        dk = mm(dscores, both_heads(q, first), ((0,), (0,))) * score_scale
        out = jnp.concatenate(
            [turn(dq, own, -after, -before).astype(bf16), turn(dk, own, -after, -before).astype(bf16), dv.astype(bf16)],
            axis=1,
        )
        dfused_ref[rows, :] = out
        total = total + jnp.sum(out.astype(f32), axis=0, keepdims=True)

    @pl.when(pl.program_id(0) == 0)
    def _():
        sums_ref[...] = jnp.zeros_like(sums_ref)

    sums_ref[...] += total


def attend(joined, bias, tables, count):
    own, after, before, mask = tables
    tokens, width = joined.shape
    length = tokens // count
    many = math.gcd(count, SEQUENCES)
    row = lambda w: pl.BlockSpec((many * length, w), lambda i: (i, 0))
    return pl.pallas_call(
        attend_kernel,
        name="attend",
        grid=(count // many,),
        in_specs=[
            row(width),
            pl.BlockSpec((1, width), lambda i: (0, 0)),
            row(PAIR),
            row(PAIR),
            row(PAIR),
            pl.BlockSpec((many, length, length), lambda i: (i, 0, 0)),
        ],
        out_specs=[row(width), row(PAIR), pl.BlockSpec((many, 2 * length, length), lambda i: (i, 0, 0))],
        out_shape=[
            jax.ShapeDtypeStruct((tokens, width), bf16),
            jax.ShapeDtypeStruct((tokens, PAIR), bf16),
            jax.ShapeDtypeStruct((count, 2 * length, length), f32),
        ],
        compiler_params=pltpu.CompilerParams(vmem_limit_bytes=32 << 20),
        cost_estimate=pl.CostEstimate(flops=tokens * length * PAIR * 8, bytes_accessed=tokens * 6000, transcendentals=tokens * length * 2),
    )(joined, bias, own, after, before, mask)


def attend_back(fused, probs, dcontext, tables, count, *others):
    own, after, before, _ = tables
    tokens, width = fused.shape
    length = tokens // count
    many = math.gcd(count, SEQUENCES)
    row = lambda w: pl.BlockSpec((many * length, w), lambda i: (i, 0))
    return pl.pallas_call(
        ignoring(attend_back_kernel, 6, len(others)),
        name="attend_back",
        grid=(count // many,),
        in_specs=[
            row(width),
            pl.BlockSpec((many, 2 * length, length), lambda i: (i, 0, 0)),
            row(PAIR),
            row(PAIR),
            row(PAIR),
            row(PAIR),
            *anywhere(others),
        ],
        out_specs=[row(width), pl.BlockSpec((1, width), lambda i: (0, 0))],
        out_shape=[jax.ShapeDtypeStruct((tokens, width), bf16), jax.ShapeDtypeStruct((1, width), f32)],
        compiler_params=pltpu.CompilerParams(vmem_limit_bytes=60 << 20),
        cost_estimate=pl.CostEstimate(flops=tokens * length * PAIR * 16, bytes_accessed=tokens * 6000, transcendentals=0),
    )(fused, probs, dcontext, own, after, before, *others)


def shifted(x, axis, size, step):
    return lax.ppermute(x, axis, [(i, (i + step) % size) for i in range(size)])


def limits(mib):
    return pltpu.CompilerParams(vmem_limit_bytes=mib << 20)


def cost(flops, moved):
    return pl.CostEstimate(flops=1, bytes_accessed=1, transcendentals=0)


def whole_block(array):
    return pl.BlockSpec(array.shape, lambda *_: (0,) * array.ndim)


def pack_kernel(part_ref, own_ref, out_ref, *, sections, tp, size, wide):
    own = own_ref[...]
    rows = own.shape[0]
    for t in range(tp):
        pieces = []
        for section in range(sections):
            at = (section * tp + t) * size
            pieces.append(own[:, at : at + size])
            if wide > size:
                pieces.append(jnp.zeros((rows, wide - size), own.dtype))
        out_ref[t] = jnp.concatenate(pieces, axis=1) if len(pieces) > 1 else pieces[0]


def pack(weight, part, groups, sections, tp, size, wide):
    rows, width = weight.shape
    half = rows // groups
    step = min(half, 16)
    return pl.pallas_call(
        functools.partial(pack_kernel, sections=sections, tp=tp, size=size, wide=wide),
        name="pack",
        grid_spec=pltpu.PrefetchScalarGridSpec(
            num_scalar_prefetch=1,
            grid=(half // step,),
            in_specs=[pl.BlockSpec((step, width), lambda i, part: (part[0] * (half // step) + i, 0))],
            out_specs=pl.BlockSpec((tp, step, sections * wide), lambda i, part: (0, i, 0)),
        ),
        out_shape=jax.ShapeDtypeStruct((tp, half, sections * wide), weight.dtype),
        compiler_params=limits(32),
        cost_estimate=cost(0, 4 * half * width),
    )(part, weight)


def nothing(*refs):
    del refs


def anywhere(arrays):
    return [pl.BlockSpec(memory_space=pl.ANY) for _ in arrays]


def after(x, *others):
    return pl.pallas_call(
        nothing,
        name="after",
        in_specs=anywhere((x, *others)),
        out_specs=pl.BlockSpec(memory_space=pl.ANY),
        out_shape=jax.ShapeDtypeStruct(x.shape, x.dtype),
        input_output_aliases={0: 0},
    )(x, *others)


def ignoring(kernel, at, count):
    return lambda *refs: kernel(*refs[:at], *refs[at + count :])


def unpack_kernel(part_ref, own_ref, other_ref, out_ref, *, sections, tp, size, wide):
    got = jnp.where(pl.program_id(0) == 0, own_ref[...], other_ref[...])
    for section in range(sections):
        pieces = [got[t, :, section * wide : section * wide + size] for t in range(tp)]
        out_ref[:, section * tp * size : (section + 1) * tp * size] = jnp.concatenate(pieces, axis=1).astype(f32)


def unpack(own, other, part, sections, size, wide):
    tp, half, width = own.shape
    step = min(half, 16)
    count = half // step
    return pl.pallas_call(
        functools.partial(unpack_kernel, sections=sections, tp=tp, size=size, wide=wide),
        name="unpack",
        grid_spec=pltpu.PrefetchScalarGridSpec(
            num_scalar_prefetch=1,
            grid=(2, count),
            in_specs=[
                pl.BlockSpec((tp, step, width), lambda i, j, part: (0, jnp.where(i == 0, j, count - 1), 0)),
                pl.BlockSpec((tp, step, width), lambda i, j, part: (0, jnp.where(i == 0, 0, j), 0)),
            ],
            out_specs=pl.BlockSpec(
                (step, sections * tp * size), lambda i, j, part: (lax.rem(part[0] + i, 2) * count + j, 0)
            ),
        ),
        out_shape=jax.ShapeDtypeStruct((2 * half, sections * tp * size), f32),
        compiler_params=limits(48),
        cost_estimate=cost(0, 12 * half * width * tp),
    )(part, own, other)


def gate_kernel(
    a_ref, b_ref, gain_ref, bias_ref, gu_ref, qkv_ref, stats_ref, normed_ref, gate_ref, up_ref, hidden_ref, joined_ref
):
    x = jnp.concatenate([a_ref[0], b_ref[0]], axis=0).astype(f32)
    mean = jnp.mean(x, axis=1, keepdims=True)
    centered = x - mean
    inv_std = lax.rsqrt(jnp.mean(centered * centered, axis=1, keepdims=True) + epsilon)
    lane = lax.broadcasted_iota(jnp.int32, stats_ref.shape, 1)
    stats_ref[...] = jnp.where(lane == 0, mean, inv_std)
    normed = (centered * inv_std * gain_ref[...] + bias_ref[...]).astype(bf16)
    normed_ref[...] = normed
    wide = gate_ref.shape[1]
    gateup = mm(normed, gu_ref[...], ((1,), (0,)))
    gate, up = gateup[:, :wide], gateup[:, wide:]
    gate_ref[...] = gate
    up_ref[...] = up
    hidden_ref[...] = (gate * jax.nn.sigmoid(gate) * up).astype(bf16)
    joined_ref[...] = mm(normed, qkv_ref[...], ((1,), (0,)))


def gate_forward(gathered, gain, bias, gu, qkv):
    count, padded, width = gathered.shape
    length, wide = LANES, gu.shape[1] // 2
    tokens = count * length
    block = lambda k: pl.BlockSpec((1, length, width), lambda i: (2 * i + k, 0, 0))
    row = lambda w: pl.BlockSpec((2 * length, w), lambda i: (i, 0))
    return pl.pallas_call(
        gate_kernel,
        name="gate_fwd",
        grid=(count // 2,),
        in_specs=[
            block(0),
            block(1),
            whole_block(gain),
            whole_block(bias),
            whole_block(gu),
            whole_block(qkv),
        ],
        out_specs=[row(LANES), row(width), row(wide), row(wide), row(wide), row(3 * PAIR)],
        out_shape=[
            jax.ShapeDtypeStruct((tokens, LANES), f32),
            jax.ShapeDtypeStruct((tokens, width), bf16),
            jax.ShapeDtypeStruct((tokens, wide), f32),
            jax.ShapeDtypeStruct((tokens, wide), f32),
            jax.ShapeDtypeStruct((tokens, wide), bf16),
            jax.ShapeDtypeStruct((tokens, 3 * PAIR), f32),
        ],
        compiler_params=limits(56),
        cost_estimate=cost(2 * tokens * width * (2 * wide + 3 * PAIR), tokens * (4 * width + 10 * wide + 12 * PAIR)),
    )(gathered, gathered, gain, bias, gu, qkv)


def branch_kernel(far, order_ref, ac_ref, bc_ref, ah_ref, bh_ref, w_ref, *refs):
    context = jnp.concatenate([ac_ref[...], bc_ref[...]], axis=0)
    hidden = jnp.concatenate([ah_ref[...], bh_ref[...]], axis=0)
    total = mm(context, w_ref[:PAIR, :], ((1,), (0,))) + mm(hidden, w_ref[PAIR:, :], ((1,), (0,)))
    if far:
        refs[0][...] = total.astype(bf16)
        return
    got_ref, sent_ref, keep_ref = refs
    keep_ref[...] = total + got_ref[...].astype(f32)

    @pl.when(pl.program_id(0) < pl.num_programs(0) // 2)
    def _():
        sent_ref[...] = keep_ref[...].astype(bf16)


def branches(order, context, hidden, w, got=None):
    tokens, wide = hidden.shape
    width = w.shape[1]
    count = order.shape[0]
    step = 2 * LANES
    row = lambda x, k: pl.BlockSpec((LANES, x.shape[1]), lambda i, order: (order[2 * i + k], 0))
    plain = pl.BlockSpec((step, width), lambda i, order: (i, 0))
    if got is None:
        out_specs = [plain]
        out_shape = [jax.ShapeDtypeStruct((count * LANES, width), bf16)]
        more = []
    else:
        sent = count // 4
        out_specs = [
            pl.BlockSpec((step, width), lambda i, order: (jnp.minimum(i, sent - 1), 0)),
            pl.BlockSpec((step, width), lambda i, order: (jnp.maximum(i - sent, 0), 0)),
        ]
        out_shape = [jax.ShapeDtypeStruct((count * LANES // 2, width), kind) for kind in (bf16, f32)]
        more = [got]
    return pl.pallas_call(
        functools.partial(branch_kernel, got is None),
        name="branch_far" if got is None else "branch_near",
        grid_spec=pltpu.PrefetchScalarGridSpec(
            num_scalar_prefetch=1,
            grid=(count // 2,),
            in_specs=[
                row(context, 0),
                row(context, 1),
                row(hidden, 0),
                row(hidden, 1),
                whole_block(w),
                *[plain for _ in more],
            ],
            out_specs=out_specs,
        ),
        out_shape=out_shape,
        compiler_params=limits(48),
        cost_estimate=cost(2 * tokens * width * (PAIR + wide), 2 * tokens * (width + PAIR + wide)),
    )(order, context, context, hidden, hidden, w, *more)


def gate_back_kernel(cotangent_ref, gate_ref, up_ref, w_ref, dgateup_ref, dcontext_ref):
    dinner = mm(cotangent_ref[...], w_ref[...], ((1,), (1,)))
    dcontext_ref[...] = dinner[:, :PAIR].astype(bf16)
    dhidden = dinner[:, PAIR:]
    gate, up = gate_ref[...], up_ref[...]
    s = jax.nn.sigmoid(gate)
    wide = gate.shape[1]
    dgateup_ref[:, :wide] = (dhidden * up * s * (1.0 + gate * (1.0 - s))).astype(bf16)
    dgateup_ref[:, wide:] = (dhidden * gate * s).astype(bf16)


def gate_backward(cotangent, gate, up, w, *others):
    tokens, wide = gate.shape
    width = w.shape[1]
    row = lambda w: pl.BlockSpec((2 * LANES, w), lambda i: (i, 0))
    return pl.pallas_call(
        ignoring(gate_back_kernel, 4, len(others)),
        name="gate_back",
        grid=(tokens // (2 * LANES),),
        in_specs=[row(width), row(wide), row(wide), whole_block(w), *anywhere(others)],
        out_specs=[row(2 * wide), row(PAIR)],
        out_shape=[jax.ShapeDtypeStruct((tokens, 2 * wide), bf16), jax.ShapeDtypeStruct((tokens, PAIR), bf16)],
        compiler_params=limits(60),
        cost_estimate=cost(2 * tokens * width * (PAIR + wide), tokens * (2 * width + 12 * wide)),
    )(cotangent, gate, up, w, *others)


def grads_kernel(part_ref, normed_ref, d_ref, mine_ref, theirs_ref):
    grads = mm(normed_ref[...], d_ref[...], ((0,), (0,)))
    count, half, _ = mine_ref.shape
    first = part_ref[0] == 0
    for t in range(count):
        low = grads[2 * t * half : (2 * t + 1) * half]
        high = grads[(2 * t + 1) * half : (2 * t + 2) * half]
        mine_ref[t] = jnp.where(first, low, high)
        theirs_ref[t] = jnp.where(first, high, low).astype(bf16)


def split_grads(part, normed, d, half, *others):
    tokens, width = normed.shape
    step = 4 * LANES
    out = d.shape[1]
    blocks = step // (2 * half)
    piece = lambda: pl.BlockSpec((blocks, half, out), lambda i, part: (i, 0, 0))
    return pl.pallas_call(
        ignoring(grads_kernel, 3, len(others)),
        name="grads",
        grid_spec=pltpu.PrefetchScalarGridSpec(
            num_scalar_prefetch=1,
            grid=(width // step,),
            in_specs=[pl.BlockSpec((tokens, step), lambda i, part: (0, i)), whole_block(d)]
            + anywhere(others),
            out_specs=[piece(), piece()],
        ),
        out_shape=[
            jax.ShapeDtypeStruct((width // (2 * half), half, out), f32),
            jax.ShapeDtypeStruct((width // (2 * half), half, out), bf16),
        ],
        compiler_params=limits(56),
        cost_estimate=cost(2 * tokens * width * d.shape[1], 2 * tokens * (width + d.shape[1]) + 3 * width * out),
    )(part, normed, d, *others)


def rows_kernel(context_ref, hidden_ref, cotangent_ref, out_ref):
    cotangent = cotangent_ref[...]
    out_ref[:PAIR, :] = mm(context_ref[...], cotangent, ((0,), (0,))).astype(out_ref.dtype)
    hidden = mm(hidden_ref[...], cotangent, ((0,), (0,)))
    out_ref[PAIR:, :] = hidden[: out_ref.shape[0] - PAIR].astype(out_ref.dtype)


def rows_grads(context, hidden, cotangent, own, kind, *others):
    tokens, width = cotangent.shape
    step = 4 * LANES
    return pl.pallas_call(
        ignoring(rows_kernel, 3, len(others)),
        name="rows",
        grid=(width // step,),
        in_specs=[
            whole_block(context),
            whole_block(hidden),
            pl.BlockSpec((tokens, step), lambda i: (0, i)),
            *anywhere(others),
        ],
        out_specs=pl.BlockSpec((own, step), lambda i: (0, i)),
        out_shape=jax.ShapeDtypeStruct((own, width), kind),
        compiler_params=limits(56),
        cost_estimate=cost(2 * tokens * width * own, tokens * width * 2),
    )(context, hidden, cotangent, *others)


def dnormed_kernel(order_ref, a_ref, b_ref, as_ref, bs_ref, ag_ref, bg_ref, aq_ref, bq_ref, gu_ref, qkv_ref, *refs):
    if len(refs) == 2:
        far_refs, (out_ref, sums_ref) = (), refs
    else:
        keep_ref, got_ref, *far_refs, branch_ref, sums_ref, out_ref = refs
        branch_ref[...] = (keep_ref[...] + got_ref[...].astype(f32)).astype(bf16)
    step = pl.program_id(0)
    gateup = jnp.concatenate([ag_ref[...], bg_ref[...]], axis=0)
    fused = jnp.concatenate([aq_ref[...], bq_ref[...]], axis=0)

    @pl.when(step == 0)
    def _():
        sums_ref[...] = jnp.zeros_like(sums_ref)

    means = [ref[:, 0:1] for ref in (as_ref, bs_ref)]
    stds = [ref[:, 1:2] for ref in (as_ref, bs_ref)]
    width = gu_ref.shape[0]
    for at in range(0, width, CHUNK):
        cols = pl.ds(at, CHUNK)
        dnormed = mm(gateup, gu_ref[cols, :], ((1,), (1,))) + mm(fused, qkv_ref[cols, :], ((1,), (1,)))
        out_ref[:, cols] = dnormed.astype(out_ref.dtype)
        normal = jnp.concatenate(
            [(ref[0, :, cols].astype(f32) - mean) * std for ref, mean, std in zip((a_ref, b_ref), means, stds)], axis=0
        )
        sums_ref[0:1, cols] += jnp.sum(dnormed * normal, axis=0, keepdims=True)
        sums_ref[1:2, cols] += jnp.sum(dnormed, axis=0, keepdims=True)
    for i, far_ref in enumerate(far_refs):

        @pl.when(step == i)
        def _():
            far_ref[...] = out_ref[...]


def dnormed_share(order, *others, gathered, stats, dgateup, dfused, gu, qkv, far=()):
    width = gathered.shape[2]
    count = order.shape[0]
    step = 2 * LANES
    block = lambda k: pl.BlockSpec((1, LANES, width), lambda i, order: (order[2 * i + k], 0, 0))
    row = lambda x, k: pl.BlockSpec((LANES, x.shape[1]), lambda i, order: (order[2 * i + k], 0))
    if far:
        outs = [pl.BlockSpec((step, width), lambda i, order: (0, 0)) for _ in range(count // 2)]
        shapes = [jax.ShapeDtypeStruct((step, width), bf16) for _ in range(count // 2)]
        part = pl.BlockSpec((far[0].shape[0] // (count // 2), width), lambda i, order: (i, 0))
        outs.append(part)
        shapes.append(jax.ShapeDtypeStruct(far[0].shape, bf16))
    else:
        outs = [pl.BlockSpec((step, width), lambda i, order: (i, 0))]
        shapes = [jax.ShapeDtypeStruct((count * LANES, width), f32)]
    return pl.pallas_call(
        ignoring(dnormed_kernel, 11 + len(far), len(others)),
        name="dn_far" if far else "dn_near",
        grid_spec=pltpu.PrefetchScalarGridSpec(
            num_scalar_prefetch=1,
            grid=(count // 2,),
            in_specs=[
                block(0),
                block(1),
                row(stats, 0),
                row(stats, 1),
                row(dgateup, 0),
                row(dgateup, 1),
                row(dfused, 0),
                row(dfused, 1),
                whole_block(gu),
                whole_block(qkv),
                *[part for _ in far],
                *anywhere(others),
            ],
            out_specs=[*outs, pl.BlockSpec((8, width), lambda i, order: (0, 0))],
            scratch_shapes=[pltpu.VMEM((step, width), bf16)] if far else [],
        ),
        out_shape=[*shapes, jax.ShapeDtypeStruct((8, width), f32)],
        compiler_params=limits(60),
        cost_estimate=cost(
            2 * count * LANES * width * (dgateup.shape[1] + dfused.shape[1]), count * LANES * width * 8
        ),
    )(order, gathered, gathered, stats, stats, dgateup, dgateup, dfused, dfused, gu, qkv, *far, *others)


def combine_kernel(near_ref, *refs):
    got_refs, sent_refs, keep_ref = refs[: len(refs) - 1 - (len(refs) - 1) // 3], refs[-1 - (len(refs) - 1) // 3 : -1], refs[-1]
    for i, got_ref in enumerate(got_refs):

        @pl.when(pl.program_id(0) == i)
        def _():
            total = near_ref[...] + got_ref[...].astype(f32)
            if i < len(sent_refs):
                sent_refs[i][...] = total.astype(bf16)
            else:
                keep_ref[...] = total


def combine(near, got, *others):
    rows, width = near.shape
    step = rows // len(got)
    sent = len(got) // 2
    fixed = pl.BlockSpec((step, width), lambda i: (0, 0))
    return pl.pallas_call(
        ignoring(combine_kernel, 1 + len(got), len(others)),
        name="combine",
        grid=(len(got),),
        in_specs=[pl.BlockSpec((step, width), lambda i: (i, 0)), *[fixed for _ in got], *anywhere(others)],
        out_specs=[fixed for _ in range(sent)] + [pl.BlockSpec((step, width), lambda i: (jnp.maximum(i - sent, 0), 0))],
        out_shape=[jax.ShapeDtypeStruct((step, width), bf16) for _ in range(sent)]
        + [jax.ShapeDtypeStruct((rows // 2, width), f32)],
        compiler_params=limits(48),
        cost_estimate=cost(0, rows * width * 9),
    )(near, *got, *others)


def per_device(
    groups, outer, zs, ys, cs, tokens, segments, ln_gain, ln_bias, w_qkv, b_qkv, w_out, w_gateup, w_down, cotangent
):
    length, width = tokens.shape
    tp = zs * ys * cs
    shards = tp * outer
    z, y, c = (lax.axis_index(axis) for axis in TP)
    me = (z * ys + y) * cs + c

    own_ffn = w_gateup.shape[1] // 2 // tp
    wide = up_to(own_ffn, LANES)
    own_qkv = 3 * PAIR
    rows = w_qkv.shape[0]
    half = rows // groups
    part = lax.axis_index("replica")
    parts = part.astype(jnp.int32).reshape(1)
    steps = sorted(range(zs), key=lambda k: -min(k, zs - k))
    order = [
        jnp.stack(
            [
                (lax.rem(z + zs - k, zs) * ys + lax.rem(y + ys - j, ys)) * cs + lax.rem(c + cs - i, cs)
                for j in reversed(range(ys))
                for k in steps
            ]
        ).astype(jnp.int32)
        for i in range(cs)
    ]

    plain_order = [
        jnp.stack(
            [(k * ys + lax.rem(y + ys - j, ys)) * cs + lax.rem(c + cs - i, cs) for j in reversed(range(ys)) for k in range(zs)]
        ).astype(jnp.int32)
        for i in range(cs)
    ]

    small = jnp.concatenate([ln_gain, ln_bias, b_qkv, segments[0].astype(bf16)])
    of_params = 2 * rows + b_qkv.shape[0]
    small_rows = up_to(-(-small.shape[0] // width), 8)
    small_rows_of = jnp.pad(small, (0, small_rows * width - small.shape[0])).reshape(small_rows, width)
    packed = jnp.concatenate([tokens, small_rows_of], axis=0)
    gathered = lax.all_gather(packed, TP, axis=0, tiled=False)

    cotangent_all = lax.all_gather(cotangent, TP, axis=0, tiled=True)

    vectors = gathered[:, length:, :].reshape(tp, -1)[:, : small.shape[0]]
    seg_all = vectors[:, of_params:].astype(jnp.int32)
    vectors = vectors[:, :of_params]
    if outer > 1:
        vectors = lax.all_gather(vectors, "outer", axis=1, tiled=False)
    vectors = vectors.reshape(shards, -1)
    gain_all = vectors[:, :rows].reshape(1, width).astype(f32)
    bias_all = vectors[:, rows : 2 * rows].reshape(1, width).astype(f32)
    qkv_bias = vectors[:, 2 * rows :].reshape(3, tp, PAIR).astype(f32)
    my_bias = lax.dynamic_index_in_dim(qkv_bias, me, 1, keepdims=False).reshape(1, own_qkv)
    tables = rotary_tables(seg_all)

    def other(own):
        return shifted(own, "replica", groups, 1)

    def to_columns(own, *others):
        own = lax.all_to_all(own, TP, 0, 0, tiled=True)
        whole = jnp.zeros((tp, groups, half, own.shape[-1]), bf16)
        whole = lax.dynamic_update_slice(whole, own[:, None], (0, part, 0, 0))
        moved = other(own)
        if others:
            moved = after(moved, *others)
        whole = lax.dynamic_update_slice(whole, moved[:, None], (0, 1 - part, 0, 0))
        whole = whole.reshape(tp, rows, own.shape[-1])
        if outer > 1:
            whole = lax.all_gather(whole, "outer", axis=1, tiled=False)
        return whole.reshape(width, own.shape[-1])

    gu_cols = to_columns(pack(w_gateup, parts, groups, 2, tp, own_ffn, wide))
    qkv_cols = to_columns(pack(w_qkv, parts, groups, 3, tp, PAIR, PAIR), *tables)
    if outer > 1:
        w_out = lax.all_gather(w_out, "outer", axis=0, tiled=True)
        w_down = lax.all_gather(w_down, "outer", axis=0, tiled=True)
    w_rows = jnp.concatenate([w_out, w_down, jnp.zeros((wide - own_ffn, width), bf16)], axis=0)

    stats, normed, gate, up, hidden, joined = gate_forward(gathered, gain_all, bias_all, gu_cols, qkv_cols)
    fused, context, probs = attend(joined, my_bias, tables, tp)
    branch_far = branches(plain_order[1], context, hidden, w_rows)[0]
    branch_sent, branch_keep = branches(plain_order[0], context, hidden, w_rows, shifted(branch_far, "c", cs, 1))
    branch_got = shifted(branch_sent, "y", ys, 1)

    dgateup, dcontext = gate_backward(cotangent_all, gate, up, w_rows, branch_sent)

    def grads_of(d, *others):
        if outer == 1:
            return split_grads(parts, normed, d, half, *others)
        mine, theirs = of_replicas(mm(normed, d, ((0,), (0,))))
        return mine, theirs.astype(bf16)

    def of_replicas(grads):
        if outer > 1:
            grads = lax.psum_scatter(grads.reshape(tp, outer, rows, -1), "outer", scatter_dimension=1, tiled=True)
        grads = grads.reshape(tp, groups, half, -1)
        mine = lax.dynamic_index_in_dim(grads, part, 1, keepdims=False)
        return mine, lax.dynamic_index_in_dim(grads, 1 - part, 1, keepdims=False)

    gu_mine, gu_theirs = grads_of(dgateup)
    gu_got = other(gu_theirs)
    dfused, bias_sums = attend_back(fused, probs, dcontext, tables, tp, gu_theirs)
    share = functools.partial(dnormed_share, gathered=gathered, stats=stats, dgateup=dgateup, dfused=dfused, gu=gu_cols, qkv=qkv_cols)
    *far_shares, branch, far_sums = share(order[1], far=(branch_keep, branch_got))
    branch_own = lax.psum_scatter(branch, "z", scatter_dimension=0, tiled=True)
    tokens32 = tokens.astype(f32)
    block_output = (tokens32 + branch_own.astype(f32)).astype(bf16)
    got = [shifted(far_share, "c", cs, 1) for far_share in far_shares]
    near_share, near_sums = share(order[0], *far_shares)
    gain_sum, bias_sum = near_sums[0] + far_sums[0], near_sums[1] + far_sums[1]

    per_row = own_qkv // half
    tiled_sums = jnp.broadcast_to(bias_sums.reshape(1, half, per_row), (width // half, half, per_row)).reshape(width, per_row)
    extra = jnp.concatenate(
        [gain_sum[:, None], bias_sum[:, None], tiled_sums, jnp.zeros((width, LANES - 2 - per_row), f32)], axis=1
    )
    mine, theirs = of_replicas(extra)
    extra = jnp.concatenate([mine[..., :2], theirs[..., :2], mine[..., 2 : 2 + per_row]], axis=2)
    extra = jnp.pad(extra, ((0, 0), (0, 0), (own_ffn, 2 * wide - own_ffn - 4 - per_row)))
    *sent, keep = combine(near_share, got)
    gu_total = (gu_mine + after(gu_got, *sent).astype(f32) + extra).astype(bf16)
    gu_own = lax.all_to_all(gu_total, TP, 0, 0, tiled=True)
    qkv_mine, qkv_theirs = grads_of(dfused, gu_total)
    qkv_got = other(qkv_theirs)
    rows_part = rows_grads(context, hidden, cotangent_all, PAIR + own_ffn, bf16 if outer == 1 else f32, qkv_theirs)
    if outer > 1:
        rows_out = lax.psum_scatter(rows_part[:PAIR], "outer", scatter_dimension=0, tiled=True)
        rows_down = lax.psum_scatter(rows_part[PAIR:], "outer", scatter_dimension=0, tiled=True)
        rows_part = jnp.concatenate([rows_out, rows_down], axis=0).astype(bf16)
    rows_got = other(rows_part)
    dnormed_own = 0.0
    leaving = []
    for i, pair in enumerate(sent):
        pair = shifted(after(pair, *leaving, rows_part) if leaving else pair, "y", ys, 1)
        at = 2 * i * length
        for j, k in enumerate(steps[2 * i : 2 * i + 2]):
            rows_at = slice(j * length, (j + 1) * length)
            term = keep[at : at + 2 * length][rows_at] + pair[rows_at].astype(f32)
            if k:
                leaving.append(term.astype(bf16))
                term = shifted(leaving[-1], "z", zs, zs - k).astype(f32)
            dnormed_own = dnormed_own + term
    centered = tokens32 - jnp.mean(tokens32, axis=1, keepdims=True)
    inv = lax.rsqrt(jnp.mean(centered * centered, axis=1, keepdims=True) + epsilon)
    xhat = centered * inv
    e = dnormed_own * gain_all
    tokens_back = inv * (e - jnp.mean(e, axis=1, keepdims=True) - xhat * jnp.mean(e * xhat, axis=1, keepdims=True))
    tokens_grad = (cotangent.astype(f32) + tokens_back).astype(bf16)
    qkv_total = (qkv_mine + qkv_got.astype(f32)).astype(bf16)
    qkv_total = after(qkv_total, gu_own, branch_own)
    qkv_own = lax.all_to_all(qkv_total, TP, 0, 0, tiled=True)
    gu_other = other(gu_own)
    gateup_grad = unpack(gu_own, gu_other, parts, 2, own_ffn, wide)
    qkv_grad = unpack(qkv_own, other(qkv_own), parts, 3, PAIR, PAIR)
    rows_grad = rows_part.astype(f32) + rows_got.astype(f32)
    sums_of = lambda x: jnp.sum(x[:, :, own_ffn : own_ffn + 4].astype(f32), axis=0)
    mine, theirs = sums_of(gu_own), sums_of(gu_other)
    here, there = mine[:, :2] + theirs[:, 2:], theirs[:, :2] + mine[:, 2:]
    first = part == 0
    own_sums = jnp.concatenate([jnp.where(first, here, there), jnp.where(first, there, here)], axis=0)
    bias_of = lambda x: x[:, :, own_ffn + 4 : own_ffn + 4 + per_row].reshape(tp, 3, PAIR).astype(f32)
    bias_grads = bias_of(gu_own) + bias_of(gu_other)
    bias_grads = bias_grads.transpose(1, 0, 2).reshape(-1)
    place = me * outer + lax.axis_index("outer")
    qkv_bias_grad = lax.dynamic_slice_in_dim(bias_grads, place * (3 * rows), 3 * rows, 0)
    return (
        block_output,
        tokens_grad,
        own_sums[:, 0],
        own_sums[:, 1],
        qkv_grad,
        qkv_bias_grad,
        rows_grad[: PAIR // outer],
        gateup_grad,
        rows_grad[PAIR // outer :],
    )


def solution(mesh):
    groups, shards = mesh.shape["replica"], mesh.shape["shard"]
    tp = math.gcd(shards, HEADS // 2)
    outer = shards // tp
    ys = cs = 2
    zs = tp // (ys * cs)
    inner_mesh = Mesh(mesh.devices.reshape(groups, zs, ys, cs, outer), ("replica", *TP, "outer"))
    everywhere = P(("replica", *TP, "outer"), None)
    vector = P((*TP, "outer"))
    matrix = P((*TP, "outer"), None)
    return jax.shard_map(
        functools.partial(per_device, groups, outer, zs, ys, cs),
        mesh=inner_mesh,
        in_specs=(everywhere, everywhere, vector, vector, matrix, vector, matrix, matrix, matrix, everywhere),
        out_specs=(everywhere, everywhere, vector, vector, matrix, vector, matrix, matrix, matrix),
        check_vma=False,
    )
```

```python
import functools
import math

import jax
import jax.numpy as jnp
from jax import lax
from jax.experimental import pallas as pl
from jax.experimental.pallas import tpu as pltpu
from jax.sharding import Mesh, PartitionSpec as P

HEADS = 32
HEAD_DIM = 64
ROT = 16
PAIR = 2 * HEAD_DIM
TP = ("z", "y", "c")
LANES = 128
SEQUENCES = 8
CHUNK = 1024

epsilon = 1e-05
rope_base = 10000.0
score_scale = 1.0 / math.sqrt(HEAD_DIM)

bf16 = jnp.bfloat16
f32 = jnp.float32


def up_to(size, step):
    return -(-size // step) * step


def mm(a, b, dims):
    return lax.dot_general(a, b, (dims, ((), ())), preferred_element_type=f32)


def rotary_tables(segments):
    count, length = segments.shape
    indices = jnp.arange(length, dtype=jnp.int32)
    same_doc = segments[:, :, None] == segments[:, None, :]
    doc_start = jnp.min(jnp.where(same_doc, indices[None, None, :], length), axis=2)
    in_doc = (indices[None, :] - doc_start).astype(f32).reshape(count * length, 1)
    allowed = same_doc & (indices[:, None] >= indices[None, :])[None]
    half_rot = ROT // 2
    lane = jnp.arange(PAIR, dtype=jnp.int32) % HEAD_DIM
    inverse = rope_base ** (-((lane % half_rot).astype(f32) * (2.0 / ROT)))
    angles = in_doc * inverse[None, :]
    cos, sin = jnp.cos(angles), jnp.sin(angles)
    turned = (lane < ROT)[None, :]
    low = (lane < half_rot)[None, :]
    own = jnp.where(turned, cos, 1.0)
    after = jnp.where(low, -sin, 0.0)
    before = jnp.where(turned & ~low, sin, 0.0)
    return own, after, before, jnp.where(allowed, 0.0, -1e30).astype(f32)


def turn(x, own, after, before):
    half = ROT // 2
    width = x.shape[-1]
    return x * own + pltpu.roll(x, width - half, 1) * after + pltpu.roll(x, half, 1) * before


def head_mask(rows):
    return lax.broadcasted_iota(jnp.int32, (rows, PAIR), 1) < HEAD_DIM


def both_heads(x, first):
    zero = jnp.zeros_like(x)
    return jnp.concatenate([jnp.where(first, x, zero), jnp.where(first, zero, x)], axis=0)


def attend_kernel(joined_ref, bias_ref, own_ref, after_ref, before_ref, mask_ref, fused_ref, context_ref, probs_ref):
    length = mask_ref.shape[1]
    first = head_mask(length)
    for n in range(mask_ref.shape[0]):
        rows = pl.ds(n * length, length)
        own, after, before = own_ref[rows, :], after_ref[rows, :], before_ref[rows, :]
        joined = joined_ref[rows, :] + bias_ref[...]
        q = turn(joined[:, :PAIR], own, after, before).astype(bf16)
        k = turn(joined[:, PAIR : 2 * PAIR], own, after, before).astype(bf16)
        v = joined[:, 2 * PAIR :].astype(bf16)
        mask = mask_ref[n]
        scores = mm(both_heads(q, first), k, ((1,), (1,))) * score_scale
        scores = scores + jnp.concatenate([mask, mask], axis=0)
        top = jnp.max(scores, axis=1, keepdims=True)
        exps = jnp.exp(scores - top)
        probs = exps / jnp.sum(exps, axis=1, keepdims=True)
        low = probs.astype(bf16)
        side = jnp.concatenate([low[:length], low[length:]], axis=1)
        context = mm(side, both_heads(v, first), ((1,), (0,)))
        fused_ref[rows, :PAIR] = q
        fused_ref[rows, PAIR : 2 * PAIR] = k
        fused_ref[rows, 2 * PAIR :] = v
        context_ref[rows, :] = context.astype(bf16)
        probs_ref[n] = probs


def attend_back_kernel(fused_ref, probs_ref, dcontext_ref, own_ref, after_ref, before_ref, dfused_ref, sums_ref):
    length = probs_ref.shape[2]
    first = head_mask(length)
    total = jnp.zeros(sums_ref.shape, f32)
    for n in range(probs_ref.shape[0]):
        rows = pl.ds(n * length, length)
        own, after, before = own_ref[rows, :], after_ref[rows, :], before_ref[rows, :]
        q = fused_ref[rows, :PAIR]
        k = fused_ref[rows, PAIR : 2 * PAIR]
        v = fused_ref[rows, 2 * PAIR :]
        probs = probs_ref[n]
        dc = both_heads(dcontext_ref[rows, :], first)
        dprobs = mm(dc, v, ((1,), (1,)))
        dscores = (probs * (dprobs - jnp.sum(dprobs * probs, axis=1, keepdims=True))).astype(bf16)
        dv = mm(probs.astype(bf16), dc, ((0,), (0,)))
        side = jnp.concatenate([dscores[:length], dscores[length:]], axis=1)
        dq = mm(side, both_heads(k, first), ((1,), (0,))) * score_scale
        dk = mm(dscores, both_heads(q, first), ((0,), (0,))) * score_scale
        out = jnp.concatenate(
            [turn(dq, own, -after, -before).astype(bf16), turn(dk, own, -after, -before).astype(bf16), dv.astype(bf16)],
            axis=1,
        )
        dfused_ref[rows, :] = out
        total = total + jnp.sum(out.astype(f32), axis=0, keepdims=True)

    @pl.when(pl.program_id(0) == 0)
    def _():
        sums_ref[...] = jnp.zeros_like(sums_ref)

    sums_ref[...] += total


def attend(joined, bias, tables, count):
    own, after, before, mask = tables
    tokens, width = joined.shape
    length = tokens // count
    many = math.gcd(count, SEQUENCES)
    row = lambda w: pl.BlockSpec((many * length, w), lambda i: (i, 0))
    return pl.pallas_call(
        attend_kernel,
        name="attend",
        grid=(count // many,),
        in_specs=[
            row(width),
            pl.BlockSpec((1, width), lambda i: (0, 0)),
            row(PAIR),
            row(PAIR),
            row(PAIR),
            pl.BlockSpec((many, length, length), lambda i: (i, 0, 0)),
        ],
        out_specs=[row(width), row(PAIR), pl.BlockSpec((many, 2 * length, length), lambda i: (i, 0, 0))],
        out_shape=[
            jax.ShapeDtypeStruct((tokens, width), bf16),
            jax.ShapeDtypeStruct((tokens, PAIR), bf16),
            jax.ShapeDtypeStruct((count, 2 * length, length), f32),
        ],
        compiler_params=pltpu.CompilerParams(vmem_limit_bytes=32 << 20),
        cost_estimate=pl.CostEstimate(flops=tokens * length * PAIR * 8, bytes_accessed=tokens * 6000, transcendentals=tokens * length * 2),
    )(joined, bias, own, after, before, mask)


def attend_back(fused, probs, dcontext, tables, count, *others):
    own, after, before, _ = tables
    tokens, width = fused.shape
    length = tokens // count
    many = math.gcd(count, SEQUENCES)
    row = lambda w: pl.BlockSpec((many * length, w), lambda i: (i, 0))
    return pl.pallas_call(
        ignoring(attend_back_kernel, 6, len(others)),
        name="attend_back",
        grid=(count // many,),
        in_specs=[
            row(width),
            pl.BlockSpec((many, 2 * length, length), lambda i: (i, 0, 0)),
            row(PAIR),
            row(PAIR),
            row(PAIR),
            row(PAIR),
            *anywhere(others),
        ],
        out_specs=[row(width), pl.BlockSpec((1, width), lambda i: (0, 0))],
        out_shape=[jax.ShapeDtypeStruct((tokens, width), bf16), jax.ShapeDtypeStruct((1, width), f32)],
        compiler_params=pltpu.CompilerParams(vmem_limit_bytes=60 << 20),
        cost_estimate=pl.CostEstimate(flops=tokens * length * PAIR * 16, bytes_accessed=tokens * 6000, transcendentals=0),
    )(fused, probs, dcontext, own, after, before, *others)


def shifted(x, axis, size, step):
    return lax.ppermute(x, axis, [(i, (i + step) % size) for i in range(size)])


def limits(mib):
    return pltpu.CompilerParams(vmem_limit_bytes=mib << 20)


def cost(flops, moved):
    return pl.CostEstimate(flops=1, bytes_accessed=1, transcendentals=0)


def whole_block(array):
    return pl.BlockSpec(array.shape, lambda *_: (0,) * array.ndim)


def pack_kernel(part_ref, own_ref, out_ref, *, sections, tp, size, wide):
    own = own_ref[...]
    rows = own.shape[0]
    for t in range(tp):
        pieces = []
        for section in range(sections):
            at = (section * tp + t) * size
            pieces.append(own[:, at : at + size])
            if wide > size:
                pieces.append(jnp.zeros((rows, wide - size), own.dtype))
        out_ref[t] = jnp.concatenate(pieces, axis=1) if len(pieces) > 1 else pieces[0]


def pack(weight, part, groups, sections, tp, size, wide):
    rows, width = weight.shape
    half = rows // groups
    step = min(half, 16)
    return pl.pallas_call(
        functools.partial(pack_kernel, sections=sections, tp=tp, size=size, wide=wide),
        name="pack",
        grid_spec=pltpu.PrefetchScalarGridSpec(
            num_scalar_prefetch=1,
            grid=(half // step,),
            in_specs=[pl.BlockSpec((step, width), lambda i, part: (part[0] * (half // step) + i, 0))],
            out_specs=pl.BlockSpec((tp, step, sections * wide), lambda i, part: (0, i, 0)),
        ),
        out_shape=jax.ShapeDtypeStruct((tp, half, sections * wide), weight.dtype),
        compiler_params=limits(32),
        cost_estimate=cost(0, 4 * half * width),
    )(part, weight)


def nothing(*refs):
    del refs


def anywhere(arrays):
    return [pl.BlockSpec(memory_space=pl.ANY) for _ in arrays]


def after(x, *others):
    return pl.pallas_call(
        nothing,
        name="after",
        in_specs=anywhere((x, *others)),
        out_specs=pl.BlockSpec(memory_space=pl.ANY),
        out_shape=jax.ShapeDtypeStruct(x.shape, x.dtype),
        input_output_aliases={0: 0},
    )(x, *others)


def ignoring(kernel, at, count):
    return lambda *refs: kernel(*refs[:at], *refs[at + count :])


def unpack_kernel(part_ref, own_ref, other_ref, out_ref, *, sections, tp, size, wide):
    got = jnp.where(pl.program_id(0) == 0, own_ref[...], other_ref[...])
    for section in range(sections):
        pieces = [got[t, :, section * wide : section * wide + size] for t in range(tp)]
        out_ref[:, section * tp * size : (section + 1) * tp * size] = jnp.concatenate(pieces, axis=1).astype(f32)


def unpack(own, other, part, sections, size, wide):
    tp, half, width = own.shape
    step = min(half, 16)
    count = half // step
    return pl.pallas_call(
        functools.partial(unpack_kernel, sections=sections, tp=tp, size=size, wide=wide),
        name="unpack",
        grid_spec=pltpu.PrefetchScalarGridSpec(
            num_scalar_prefetch=1,
            grid=(2, count),
            in_specs=[
                pl.BlockSpec((tp, step, width), lambda i, j, part: (0, jnp.where(i == 0, j, count - 1), 0)),
                pl.BlockSpec((tp, step, width), lambda i, j, part: (0, jnp.where(i == 0, 0, j), 0)),
            ],
            out_specs=pl.BlockSpec(
                (step, sections * tp * size), lambda i, j, part: (lax.rem(part[0] + i, 2) * count + j, 0)
            ),
        ),
        out_shape=jax.ShapeDtypeStruct((2 * half, sections * tp * size), f32),
        compiler_params=limits(48),
        cost_estimate=cost(0, 12 * half * width * tp),
    )(part, own, other)


def gate_kernel(
    a_ref, b_ref, gain_ref, bias_ref, gu_ref, qkv_ref, stats_ref, normed_ref, gate_ref, up_ref, hidden_ref, joined_ref
):
    x = jnp.concatenate([a_ref[0], b_ref[0]], axis=0).astype(f32)
    mean = jnp.mean(x, axis=1, keepdims=True)
    centered = x - mean
    inv_std = lax.rsqrt(jnp.mean(centered * centered, axis=1, keepdims=True) + epsilon)
    lane = lax.broadcasted_iota(jnp.int32, stats_ref.shape, 1)
    stats_ref[...] = jnp.where(lane == 0, mean, inv_std)
    normed = (centered * inv_std * gain_ref[...] + bias_ref[...]).astype(bf16)
    normed_ref[...] = normed
    wide = gate_ref.shape[1]
    gateup = mm(normed, gu_ref[...], ((1,), (0,)))
    gate, up = gateup[:, :wide], gateup[:, wide:]
    gate_ref[...] = gate
    up_ref[...] = up
    hidden_ref[...] = (gate * jax.nn.sigmoid(gate) * up).astype(bf16)
    joined_ref[...] = mm(normed, qkv_ref[...], ((1,), (0,)))


def gate_forward(gathered, gain, bias, gu, qkv):
    count, padded, width = gathered.shape
    length, wide = LANES, gu.shape[1] // 2
    tokens = count * length
    block = lambda k: pl.BlockSpec((1, length, width), lambda i: (2 * i + k, 0, 0))
    row = lambda w: pl.BlockSpec((2 * length, w), lambda i: (i, 0))
    return pl.pallas_call(
        gate_kernel,
        name="gate_fwd",
        grid=(count // 2,),
        in_specs=[
            block(0),
            block(1),
            whole_block(gain),
            whole_block(bias),
            whole_block(gu),
            whole_block(qkv),
        ],
        out_specs=[row(LANES), row(width), row(wide), row(wide), row(wide), row(3 * PAIR)],
        out_shape=[
            jax.ShapeDtypeStruct((tokens, LANES), f32),
            jax.ShapeDtypeStruct((tokens, width), bf16),
            jax.ShapeDtypeStruct((tokens, wide), f32),
            jax.ShapeDtypeStruct((tokens, wide), f32),
            jax.ShapeDtypeStruct((tokens, wide), bf16),
            jax.ShapeDtypeStruct((tokens, 3 * PAIR), f32),
        ],
        compiler_params=limits(56),
        cost_estimate=cost(2 * tokens * width * (2 * wide + 3 * PAIR), tokens * (4 * width + 10 * wide + 12 * PAIR)),
    )(gathered, gathered, gain, bias, gu, qkv)


def branch_kernel(far, order_ref, ac_ref, bc_ref, ah_ref, bh_ref, w_ref, *refs):
    context = jnp.concatenate([ac_ref[...], bc_ref[...]], axis=0)
    hidden = jnp.concatenate([ah_ref[...], bh_ref[...]], axis=0)
    total = mm(context, w_ref[:PAIR, :], ((1,), (0,))) + mm(hidden, w_ref[PAIR:, :], ((1,), (0,)))
    if far:
        refs[0][...] = total.astype(bf16)
        return
    got_ref, sent_ref, keep_ref = refs
    keep_ref[...] = total + got_ref[...].astype(f32)

    @pl.when(pl.program_id(0) < pl.num_programs(0) // 2)
    def _():
        sent_ref[...] = keep_ref[...].astype(bf16)


def branches(order, context, hidden, w, got=None):
    tokens, wide = hidden.shape
    width = w.shape[1]
    count = order.shape[0]
    step = 2 * LANES
    row = lambda x, k: pl.BlockSpec((LANES, x.shape[1]), lambda i, order: (order[2 * i + k], 0))
    plain = pl.BlockSpec((step, width), lambda i, order: (i, 0))
    if got is None:
        out_specs = [plain]
        out_shape = [jax.ShapeDtypeStruct((count * LANES, width), bf16)]
        more = []
    else:
        sent = count // 4
        out_specs = [
            pl.BlockSpec((step, width), lambda i, order: (jnp.minimum(i, sent - 1), 0)),
            pl.BlockSpec((step, width), lambda i, order: (jnp.maximum(i - sent, 0), 0)),
        ]
        out_shape = [jax.ShapeDtypeStruct((count * LANES // 2, width), kind) for kind in (bf16, f32)]
        more = [got]
    return pl.pallas_call(
        functools.partial(branch_kernel, got is None),
        name="branch_far" if got is None else "branch_near",
        grid_spec=pltpu.PrefetchScalarGridSpec(
            num_scalar_prefetch=1,
            grid=(count // 2,),
            in_specs=[
                row(context, 0),
                row(context, 1),
                row(hidden, 0),
                row(hidden, 1),
                whole_block(w),
                *[plain for _ in more],
            ],
            out_specs=out_specs,
        ),
        out_shape=out_shape,
        compiler_params=limits(48),
        cost_estimate=cost(2 * tokens * width * (PAIR + wide), 2 * tokens * (width + PAIR + wide)),
    )(order, context, context, hidden, hidden, w, *more)


def gate_back_kernel(cotangent_ref, gate_ref, up_ref, w_ref, dgateup_ref, dcontext_ref):
    dinner = mm(cotangent_ref[...], w_ref[...], ((1,), (1,)))
    dcontext_ref[...] = dinner[:, :PAIR].astype(bf16)
    dhidden = dinner[:, PAIR:]
    gate, up = gate_ref[...], up_ref[...]
    s = jax.nn.sigmoid(gate)
    wide = gate.shape[1]
    dgateup_ref[:, :wide] = (dhidden * up * s * (1.0 + gate * (1.0 - s))).astype(bf16)
    dgateup_ref[:, wide:] = (dhidden * gate * s).astype(bf16)


def gate_backward(cotangent, gate, up, w, *others):
    tokens, wide = gate.shape
    width = w.shape[1]
    row = lambda w: pl.BlockSpec((2 * LANES, w), lambda i: (i, 0))
    return pl.pallas_call(
        ignoring(gate_back_kernel, 4, len(others)),
        name="gate_back",
        grid=(tokens // (2 * LANES),),
        in_specs=[row(width), row(wide), row(wide), whole_block(w), *anywhere(others)],
        out_specs=[row(2 * wide), row(PAIR)],
        out_shape=[jax.ShapeDtypeStruct((tokens, 2 * wide), bf16), jax.ShapeDtypeStruct((tokens, PAIR), bf16)],
        compiler_params=limits(48),
        cost_estimate=cost(2 * tokens * width * (PAIR + wide), tokens * (2 * width + 12 * wide)),
    )(cotangent, gate, up, w, *others)


def grads_kernel(part_ref, normed_ref, d_ref, mine_ref, theirs_ref):
    grads = mm(normed_ref[...], d_ref[...], ((0,), (0,)))
    count, half, _ = mine_ref.shape
    first = part_ref[0] == 0
    for t in range(count):
        low = grads[2 * t * half : (2 * t + 1) * half]
        high = grads[(2 * t + 1) * half : (2 * t + 2) * half]
        mine_ref[t] = jnp.where(first, low, high)
        theirs_ref[t] = jnp.where(first, high, low).astype(bf16)


def split_grads(part, normed, d, half, *others):
    tokens, width = normed.shape
    step = 4 * LANES
    out = d.shape[1]
    blocks = step // (2 * half)
    piece = lambda: pl.BlockSpec((blocks, half, out), lambda i, part: (i, 0, 0))
    return pl.pallas_call(
        ignoring(grads_kernel, 3, len(others)),
        name="grads",
        grid_spec=pltpu.PrefetchScalarGridSpec(
            num_scalar_prefetch=1,
            grid=(width // step,),
            in_specs=[pl.BlockSpec((tokens, step), lambda i, part: (0, i)), whole_block(d)]
            + anywhere(others),
            out_specs=[piece(), piece()],
        ),
        out_shape=[
            jax.ShapeDtypeStruct((width // (2 * half), half, out), f32),
            jax.ShapeDtypeStruct((width // (2 * half), half, out), bf16),
        ],
        compiler_params=limits(56),
        cost_estimate=cost(2 * tokens * width * d.shape[1], 2 * tokens * (width + d.shape[1]) + 3 * width * out),
    )(part, normed, d, *others)


def rows_kernel(context_ref, hidden_ref, cotangent_ref, out_ref):
    cotangent = cotangent_ref[...]
    out_ref[:PAIR, :] = mm(context_ref[...], cotangent, ((0,), (0,))).astype(out_ref.dtype)
    hidden = mm(hidden_ref[...], cotangent, ((0,), (0,)))
    out_ref[PAIR:, :] = hidden[: out_ref.shape[0] - PAIR].astype(out_ref.dtype)


def rows_grads(context, hidden, cotangent, own, kind, *others):
    tokens, width = cotangent.shape
    step = 4 * LANES
    return pl.pallas_call(
        ignoring(rows_kernel, 3, len(others)),
        name="rows",
        grid=(width // step,),
        in_specs=[
            whole_block(context),
            whole_block(hidden),
            pl.BlockSpec((tokens, step), lambda i: (0, i)),
            *anywhere(others),
        ],
        out_specs=pl.BlockSpec((own, step), lambda i: (0, i)),
        out_shape=jax.ShapeDtypeStruct((own, width), kind),
        compiler_params=limits(56),
        cost_estimate=cost(2 * tokens * width * own, tokens * width * 2),
    )(context, hidden, cotangent, *others)


def dnormed_kernel(order_ref, a_ref, b_ref, as_ref, bs_ref, ag_ref, bg_ref, aq_ref, bq_ref, gu_ref, qkv_ref, *refs):
    if len(refs) == 2:
        far_refs, (out_ref, sums_ref) = (), refs
    else:
        keep_ref, got_ref, *far_refs, branch_ref, sums_ref, out_ref = refs
        branch_ref[...] = (keep_ref[...] + got_ref[...].astype(f32)).astype(bf16)
    step = pl.program_id(0)
    gateup = jnp.concatenate([ag_ref[...], bg_ref[...]], axis=0)
    fused = jnp.concatenate([aq_ref[...], bq_ref[...]], axis=0)

    @pl.when(step == 0)
    def _():
        sums_ref[...] = jnp.zeros_like(sums_ref)

    means = [ref[:, 0:1] for ref in (as_ref, bs_ref)]
    stds = [ref[:, 1:2] for ref in (as_ref, bs_ref)]
    width = gu_ref.shape[0]
    for at in range(0, width, CHUNK):
        cols = pl.ds(at, CHUNK)
        dnormed = mm(gateup, gu_ref[cols, :], ((1,), (1,))) + mm(fused, qkv_ref[cols, :], ((1,), (1,)))
        out_ref[:, cols] = dnormed.astype(out_ref.dtype)
        normal = jnp.concatenate(
            [(ref[0, :, cols].astype(f32) - mean) * std for ref, mean, std in zip((a_ref, b_ref), means, stds)], axis=0
        )
        sums_ref[0:1, cols] += jnp.sum(dnormed * normal, axis=0, keepdims=True)
        sums_ref[1:2, cols] += jnp.sum(dnormed, axis=0, keepdims=True)
    for i, far_ref in enumerate(far_refs):

        @pl.when(step == i)
        def _():
            far_ref[...] = out_ref[...]


def dnormed_share(order, *others, gathered, stats, dgateup, dfused, gu, qkv, far=()):
    width = gathered.shape[2]
    count = order.shape[0]
    step = 2 * LANES
    block = lambda k: pl.BlockSpec((1, LANES, width), lambda i, order: (order[2 * i + k], 0, 0))
    row = lambda x, k: pl.BlockSpec((LANES, x.shape[1]), lambda i, order: (order[2 * i + k], 0))
    if far:
        outs = [pl.BlockSpec((step, width), lambda i, order: (0, 0)) for _ in range(count // 2)]
        shapes = [jax.ShapeDtypeStruct((step, width), bf16) for _ in range(count // 2)]
        part = pl.BlockSpec((far[0].shape[0] // (count // 2), width), lambda i, order: (i, 0))
        outs.append(part)
        shapes.append(jax.ShapeDtypeStruct(far[0].shape, bf16))
    else:
        outs = [pl.BlockSpec((step, width), lambda i, order: (i, 0))]
        shapes = [jax.ShapeDtypeStruct((count * LANES, width), f32)]
    return pl.pallas_call(
        ignoring(dnormed_kernel, 11 + len(far), len(others)),
        name="dn_far" if far else "dn_near",
        grid_spec=pltpu.PrefetchScalarGridSpec(
            num_scalar_prefetch=1,
            grid=(count // 2,),
            in_specs=[
                block(0),
                block(1),
                row(stats, 0),
                row(stats, 1),
                row(dgateup, 0),
                row(dgateup, 1),
                row(dfused, 0),
                row(dfused, 1),
                whole_block(gu),
                whole_block(qkv),
                *[part for _ in far],
                *anywhere(others),
            ],
            out_specs=[*outs, pl.BlockSpec((8, width), lambda i, order: (0, 0))],
            scratch_shapes=[pltpu.VMEM((step, width), bf16)] if far else [],
        ),
        out_shape=[*shapes, jax.ShapeDtypeStruct((8, width), f32)],
        compiler_params=limits(60),
        cost_estimate=cost(
            2 * count * LANES * width * (dgateup.shape[1] + dfused.shape[1]), count * LANES * width * 8
        ),
    )(order, gathered, gathered, stats, stats, dgateup, dgateup, dfused, dfused, gu, qkv, *far, *others)


def combine_kernel(near_ref, *refs):
    got_refs, sent_refs, keep_ref = refs[: len(refs) - 1 - (len(refs) - 1) // 3], refs[-1 - (len(refs) - 1) // 3 : -1], refs[-1]
    for i, got_ref in enumerate(got_refs):

        @pl.when(pl.program_id(0) == i)
        def _():
            total = near_ref[...] + got_ref[...].astype(f32)
            if i < len(sent_refs):
                sent_refs[i][...] = total.astype(bf16)
            else:
                keep_ref[...] = total


def combine(near, got, *others):
    rows, width = near.shape
    step = rows // len(got)
    sent = len(got) // 2
    fixed = pl.BlockSpec((step, width), lambda i: (0, 0))
    return pl.pallas_call(
        ignoring(combine_kernel, 1 + len(got), len(others)),
        name="combine",
        grid=(len(got),),
        in_specs=[pl.BlockSpec((step, width), lambda i: (i, 0)), *[fixed for _ in got], *anywhere(others)],
        out_specs=[fixed for _ in range(sent)] + [pl.BlockSpec((step, width), lambda i: (jnp.maximum(i - sent, 0), 0))],
        out_shape=[jax.ShapeDtypeStruct((step, width), bf16) for _ in range(sent)]
        + [jax.ShapeDtypeStruct((rows // 2, width), f32)],
        compiler_params=limits(48),
        cost_estimate=cost(0, rows * width * 9),
    )(near, *got, *others)


def per_device(
    groups, outer, zs, ys, cs, tokens, segments, ln_gain, ln_bias, w_qkv, b_qkv, w_out, w_gateup, w_down, cotangent
):
    length, width = tokens.shape
    tp = zs * ys * cs
    shards = tp * outer
    z, y, c = (lax.axis_index(axis) for axis in TP)
    me = (z * ys + y) * cs + c

    own_ffn = w_gateup.shape[1] // 2 // tp
    wide = up_to(own_ffn, LANES)
    own_qkv = 3 * PAIR
    rows = w_qkv.shape[0]
    half = rows // groups
    part = lax.axis_index("replica")
    parts = part.astype(jnp.int32).reshape(1)
    steps = sorted(range(zs), key=lambda k: -min(k, zs - k))
    order = [
        jnp.stack(
            [
                (lax.rem(z + zs - k, zs) * ys + lax.rem(y + ys - j, ys)) * cs + lax.rem(c + cs - i, cs)
                for j in reversed(range(ys))
                for k in steps
            ]
        ).astype(jnp.int32)
        for i in range(cs)
    ]

    plain_order = [
        jnp.stack(
            [(k * ys + lax.rem(y + ys - j, ys)) * cs + lax.rem(c + cs - i, cs) for j in reversed(range(ys)) for k in range(zs)]
        ).astype(jnp.int32)
        for i in range(cs)
    ]

    small = jnp.concatenate([ln_gain, ln_bias, b_qkv, segments[0].astype(bf16)])
    of_params = 2 * rows + b_qkv.shape[0]
    small_rows = up_to(-(-small.shape[0] // width), 8)
    small_rows_of = jnp.pad(small, (0, small_rows * width - small.shape[0])).reshape(small_rows, width)
    packed = jnp.concatenate([tokens, small_rows_of], axis=0)
    gathered = lax.all_gather(packed, TP, axis=0, tiled=False)

    cotangent_all = lax.all_gather(cotangent, TP, axis=0, tiled=True)

    vectors = gathered[:, length:, :].reshape(tp, -1)[:, : small.shape[0]]
    seg_all = vectors[:, of_params:].astype(jnp.int32)
    vectors = vectors[:, :of_params]
    if outer > 1:
        vectors = lax.all_gather(vectors, "outer", axis=1, tiled=False)
    vectors = vectors.reshape(shards, -1)
    gain_all = vectors[:, :rows].reshape(1, width).astype(f32)
    bias_all = vectors[:, rows : 2 * rows].reshape(1, width).astype(f32)
    qkv_bias = vectors[:, 2 * rows :].reshape(3, tp, PAIR).astype(f32)
    my_bias = lax.dynamic_index_in_dim(qkv_bias, me, 1, keepdims=False).reshape(1, own_qkv)
    tables = rotary_tables(seg_all)

    def other(own):
        return shifted(own, "replica", groups, 1)

    def to_columns(own, *others):
        own = lax.all_to_all(own, TP, 0, 0, tiled=True)
        whole = jnp.zeros((tp, groups, half, own.shape[-1]), bf16)
        whole = lax.dynamic_update_slice(whole, own[:, None], (0, part, 0, 0))
        moved = other(own)
        if others:
            moved = after(moved, *others)
        whole = lax.dynamic_update_slice(whole, moved[:, None], (0, 1 - part, 0, 0))
        whole = whole.reshape(tp, rows, own.shape[-1])
        if outer > 1:
            whole = lax.all_gather(whole, "outer", axis=1, tiled=False)
        return whole.reshape(width, own.shape[-1])

    gu_cols = to_columns(pack(w_gateup, parts, groups, 2, tp, own_ffn, wide))
    qkv_cols = to_columns(pack(w_qkv, parts, groups, 3, tp, PAIR, PAIR), *tables)
    if outer > 1:
        w_out = lax.all_gather(w_out, "outer", axis=0, tiled=True)
        w_down = lax.all_gather(w_down, "outer", axis=0, tiled=True)
    w_rows = jnp.concatenate([w_out, w_down, jnp.zeros((wide - own_ffn, width), bf16)], axis=0)

    stats, normed, gate, up, hidden, joined = gate_forward(gathered, gain_all, bias_all, gu_cols, qkv_cols)
    fused, context, probs = attend(joined, my_bias, tables, tp)
    branch_far = branches(plain_order[1], context, hidden, w_rows)[0]
    branch_sent, branch_keep = branches(plain_order[0], context, hidden, w_rows, shifted(branch_far, "c", cs, 1))
    branch_got = shifted(branch_sent, "y", ys, 1)

    dgateup, dcontext = gate_backward(cotangent_all, gate, up, w_rows, branch_sent)

    def grads_of(d, *others):
        if outer == 1:
            return split_grads(parts, normed, d, half, *others)
        mine, theirs = of_replicas(mm(normed, d, ((0,), (0,))))
        return mine, theirs.astype(bf16)

    def of_replicas(grads):
        if outer > 1:
            grads = lax.psum_scatter(grads.reshape(tp, outer, rows, -1), "outer", scatter_dimension=1, tiled=True)
        grads = grads.reshape(tp, groups, half, -1)
        mine = lax.dynamic_index_in_dim(grads, part, 1, keepdims=False)
        return mine, lax.dynamic_index_in_dim(grads, 1 - part, 1, keepdims=False)

    gu_mine, gu_theirs = grads_of(dgateup)
    gu_got = other(gu_theirs)
    dfused, bias_sums = attend_back(fused, probs, dcontext, tables, tp, gu_theirs)
    share = functools.partial(dnormed_share, gathered=gathered, stats=stats, dgateup=dgateup, dfused=dfused, gu=gu_cols, qkv=qkv_cols)
    *far_shares, branch, far_sums = share(order[1], far=(branch_keep, branch_got))
    branch_own = lax.psum_scatter(branch, "z", scatter_dimension=0, tiled=True)
    tokens32 = tokens.astype(f32)
    block_output = (tokens32 + branch_own.astype(f32)).astype(bf16)
    got = [shifted(far_share, "c", cs, 1) for far_share in far_shares]
    near_share, near_sums = share(order[0], *far_shares)
    gain_sum, bias_sum = near_sums[0] + far_sums[0], near_sums[1] + far_sums[1]

    per_row = own_qkv // half
    tiled_sums = jnp.broadcast_to(bias_sums.reshape(1, half, per_row), (width // half, half, per_row)).reshape(width, per_row)
    extra = jnp.concatenate(
        [gain_sum[:, None], bias_sum[:, None], tiled_sums, jnp.zeros((width, LANES - 2 - per_row), f32)], axis=1
    )
    mine, theirs = of_replicas(extra)
    extra = jnp.concatenate([mine[..., :2], theirs[..., :2], mine[..., 2 : 2 + per_row]], axis=2)
    extra = jnp.pad(extra, ((0, 0), (0, 0), (own_ffn, 2 * wide - own_ffn - 4 - per_row)))
    *sent, keep = combine(near_share, got)
    gu_total = (gu_mine + after(gu_got, *sent).astype(f32) + extra).astype(bf16)
    gu_own = lax.all_to_all(gu_total, TP, 0, 0, tiled=True)
    qkv_mine, qkv_theirs = grads_of(dfused, gu_total)
    qkv_got = other(qkv_theirs)
    rows_part = rows_grads(context, hidden, cotangent_all, PAIR + own_ffn, bf16 if outer == 1 else f32, qkv_theirs)
    if outer > 1:
        rows_out = lax.psum_scatter(rows_part[:PAIR], "outer", scatter_dimension=0, tiled=True)
        rows_down = lax.psum_scatter(rows_part[PAIR:], "outer", scatter_dimension=0, tiled=True)
        rows_part = jnp.concatenate([rows_out, rows_down], axis=0).astype(bf16)
    rows_got = other(rows_part)
    dnormed_own = 0.0
    leaving = []
    for i, pair in enumerate(sent):
        pair = shifted(after(pair, *leaving, rows_part) if leaving else pair, "y", ys, 1)
        at = 2 * i * length
        for j, k in enumerate(steps[2 * i : 2 * i + 2]):
            rows_at = slice(j * length, (j + 1) * length)
            term = keep[at : at + 2 * length][rows_at] + pair[rows_at].astype(f32)
            if k:
                leaving.append(term.astype(bf16))
                term = shifted(leaving[-1], "z", zs, zs - k).astype(f32)
            dnormed_own = dnormed_own + term
    centered = tokens32 - jnp.mean(tokens32, axis=1, keepdims=True)
    inv = lax.rsqrt(jnp.mean(centered * centered, axis=1, keepdims=True) + epsilon)
    xhat = centered * inv
    e = dnormed_own * gain_all
    tokens_back = inv * (e - jnp.mean(e, axis=1, keepdims=True) - xhat * jnp.mean(e * xhat, axis=1, keepdims=True))
    tokens_grad = (cotangent.astype(f32) + tokens_back).astype(bf16)
    qkv_total = (qkv_mine + qkv_got.astype(f32)).astype(bf16)
    qkv_total = after(qkv_total, gu_own, branch_own)
    qkv_own = lax.all_to_all(qkv_total, TP, 0, 0, tiled=True)
    gu_other = other(gu_own)
    gateup_grad = unpack(gu_own, gu_other, parts, 2, own_ffn, wide)
    qkv_grad = unpack(qkv_own, other(qkv_own), parts, 3, PAIR, PAIR)
    rows_grad = rows_part.astype(f32) + rows_got.astype(f32)
    sums_of = lambda x: jnp.sum(x[:, :, own_ffn : own_ffn + 4].astype(f32), axis=0)
    mine, theirs = sums_of(gu_own), sums_of(gu_other)
    here, there = mine[:, :2] + theirs[:, 2:], theirs[:, :2] + mine[:, 2:]
    first = part == 0
    own_sums = jnp.concatenate([jnp.where(first, here, there), jnp.where(first, there, here)], axis=0)
    bias_of = lambda x: x[:, :, own_ffn + 4 : own_ffn + 4 + per_row].reshape(tp, 3, PAIR).astype(f32)
    bias_grads = bias_of(gu_own) + bias_of(gu_other)
    bias_grads = bias_grads.transpose(1, 0, 2).reshape(-1)
    place = me * outer + lax.axis_index("outer")
    qkv_bias_grad = lax.dynamic_slice_in_dim(bias_grads, place * (3 * rows), 3 * rows, 0)
    return (
        block_output,
        tokens_grad,
        own_sums[:, 0],
        own_sums[:, 1],
        qkv_grad,
        qkv_bias_grad,
        rows_grad[: PAIR // outer],
        gateup_grad,
        rows_grad[PAIR // outer :],
    )


def solution(mesh):
    groups, shards = mesh.shape["replica"], mesh.shape["shard"]
    tp = math.gcd(shards, HEADS // 2)
    outer = shards // tp
    ys = cs = 2
    zs = tp // (ys * cs)
    inner_mesh = Mesh(mesh.devices.reshape(groups, zs, ys, cs, outer), ("replica", *TP, "outer"))
    everywhere = P(("replica", *TP, "outer"), None)
    vector = P((*TP, "outer"))
    matrix = P((*TP, "outer"), None)
    return jax.shard_map(
        functools.partial(per_device, groups, outer, zs, ys, cs),
        mesh=inner_mesh,
        in_specs=(everywhere, everywhere, vector, vector, matrix, vector, matrix, matrix, matrix, everywhere),
        out_specs=(everywhere, everywhere, vector, vector, matrix, vector, matrix, matrix, matrix),
        check_vma=False,
    )
```
